128 devices in a mesh: ctx: 16 (over x_lo, y, core), ch: 8 (over z, x_hi).
Axes of the slice: x: 4 (x_hi: 2, x_lo: 2; x = x_hi * 2 + x_lo), y: 4, z: 4, core: 2. Of those that a mesh axis runs over, the one named last changes fastest.
Arguments:
- hidden: bfloat16 [8192, 4096], P('ctx', 'ch'), may hold values from -6 to 6
- norm_gain: float32 [2, 4096], replicated, may hold values from 0.5 to 2
- in_weight: bfloat16 [2, 4096, 3, 4096], P(None, 'ctx', None, 'ch'), may hold values from -0.09375 to 0.09375
- feat_filter: float32 [2, 3, 3, 4096], P(None, None, None, 'ch'), may hold values from -3 to 3
- se_filter: float32 [7, 4096], P(None, 'ch'), may hold values from -2 to 2
- mr_filter: float32 [128, 4096], P(None, 'ch'), may hold values from -0.5 to 0.5
- skip_gain: float32 [2, 4096], P(None, 'ch'), may hold values from -1 to 1
- out_weight: bfloat16 [2, 4096, 4096], P(None, 'ch', 'ctx'), may hold values from -0.125 to 0.125
Outputs:
- result: bfloat16 [8192, 4096], P('ctx', 'ch')
The draws below stay inside these ranges and needn't reach their ends.
All inputs are finite; a program needn't handle non-finite values.
Results may differ from the reference program's by a relative error of at most 0.04.
Values may be sent and summed in bfloat16 or wider, within the bound.
No kernel may reach another device: no remote copies, remote signals or barrier semaphores. Data moves between devices by JAX's collectives and lax.ppermute only.
A program may use at most 128 MiB of HBM per device.

```python
import math
import jax
import jax.numpy as jnp
from jax import lax

D = 4096
SE_LEN = 7
MR_LEN = 128
TOKENS = 8192
N_CTX = 16
N_CH = 8


def strengthened(array, key, source, target, parts, factor):
    owner, partner = [(jnp.arange(array.shape[dim]) // (array.shape[dim] // parts)).reshape([-1 if axis == dim else 1 for axis in range(array.ndim)]) for dim in (source, target)]
    chosen = jax.random.permutation(key, parts)[partner]
    strong = (owner == chosen) | (owner == (partner + parts // 2) % parts)
    return jnp.where(strong, factor * array, array)


def level_of(key, extent, split, smallest, top_value):
    factor_of, own = 1.0, jax.random.fold_in(key, 6)
    for dim, shards_of in split:
        steps = jnp.exp(jax.random.uniform(jax.random.fold_in(own, dim), (shards_of,), jnp.float32, smallest / len(split), top_value / len(split)))
        factor_of = factor_of * jnp.repeat(steps, extent[dim] // shards_of).reshape([-1 if axis == dim else 1 for axis in range(len(extent))])
    return factor_of


def noise(key, dims, spread, limit, cuts=(), kind=jnp.bfloat16):
    array = jax.random.normal(key, dims, jnp.float32) * spread
    if len(cuts) > 0:
        array = level_of(key, dims, cuts, -0.22, 0.18) * array
    return jnp.clip(array, min=-limit, max=limit).astype(kind)


def gaussian_with(own_key, shape, deviation, bound, shards, heavy, kind=jnp.bfloat16):
    drawn = deviation * jax.random.normal(own_key, shape, jnp.float32)
    if shards:
        drawn = drawn * level_of(own_key, shape, shards, -0.22, 0.18)
    return jnp.clip(strengthened(drawn, jax.random.fold_in(own_key, 3), *heavy), -bound, bound).astype(kind)


def setup_inputs(seed: int = 0) -> dict:
    keys = jax.random.split(jax.random.key(seed), 9)
    hidden = noise(keys[0], (TOKENS, D), 1.0, 6.0, ((0, 16), (1, 8)))
    norm_gain = jnp.clip(jnp.exp(jax.random.uniform(keys[1], (2, D), jnp.float32, math.log(0.5), math.log(2.0))), 0.5, 2.0)
    in_weight = noise(keys[2], (2, D, 3, D), D ** -0.5, 0.09375, ((1, 16), (3, 8)))
    feat_filter = noise(keys[3], (2, 3, 3, D), 0.6, 3.0, ((3, 8),), jnp.float32)
    se_filter = noise(keys[4], (SE_LEN, D), 0.38, 2.0, ((1, 8),), jnp.float32)
    mr_filter = noise(keys[5], (MR_LEN, D), 0.09, 0.5, ((1, 8),), jnp.float32)
    skip_gain = jnp.clip(jax.random.uniform(keys[6], (2, D), jnp.float32, -1.0, 1.0) * level_of(keys[6], (2, D), ((1, 8),), -0.4, 0.0), -1.0, 1.0)
    out_weight = gaussian_with(keys[7], (2, D, D), D ** -0.5, 0.125, ((1, 8), (2, 16)), (1, 2, 16, 2.0))
    return {"hidden": hidden, "norm_gain": norm_gain, "in_weight": in_weight, "feat_filter": feat_filter, "se_filter": se_filter, "mr_filter": mr_filter, "skip_gain": skip_gain, "out_weight": out_weight}


def rms_normed(rows_in, gain_row):
    values = rows_in.astype(jnp.float32)
    inverse_rms = lax.rsqrt(lax.optimization_barrier(jnp.mean(values * values, axis=-1, keepdims=True)) + 1e-06)
    return (values * inverse_rms * gain_row).astype(jnp.bfloat16)

def causal_filter(signal, filter_taps):
    length = filter_taps.shape[0]
    row_count = signal.shape[0]
    padded = jnp.pad(signal, ((length - 1, 0), (0, 0)))

    def add_tap(tap_index, running):
        offset = (length - 1 - tap_index).astype(jnp.int32)
        weight_tap = lax.dynamic_slice_in_dim(filter_taps, tap_index.astype(jnp.int32), 1, 0)
        return running + weight_tap * lax.dynamic_slice_in_dim(padded, offset, row_count, 0)
    return lax.fori_loop(0, length, add_tap, jnp.zeros_like(signal))

def hyena_layer(rows_in, gain_row, in_w, shaping, filter_taps, skip_term, out_w):
    normed = rms_normed(rows_in, gain_row)
    row_count = rows_in.shape[0]
    block_width = D // N_CTX
    flattened = in_w.reshape(D, 3 * D)

    def add_block(block_index, running):
        offset = (block_index * block_width).astype(jnp.int32)
        columns = lax.dynamic_slice_in_dim(normed, offset, block_width, 1)
        weight_rows = lax.dynamic_slice_in_dim(flattened, offset, block_width, 0)
        product = jnp.dot(columns, weight_rows, preferred_element_type=jnp.float32)
        return running + lax.optimization_barrier(product.astype(jnp.bfloat16)).astype(jnp.float32)
    summed = lax.fori_loop(0, N_CTX, add_block, jnp.zeros((row_count, 3 * D), jnp.float32))
    projected = summed.astype(jnp.bfloat16).reshape(row_count, 3, D).astype(jnp.float32)
    padded = jnp.pad(projected, ((2, 0), (0, 0), (0, 0)))
    shaped = shaping[0] * padded[2:] + shaping[1] * padded[1:-1] + shaping[2] * padded[:-2]
    gated_rows = shaped[:, 1] * shaped[:, 2]
    filtered = causal_filter(gated_rows, filter_taps)
    inner_out = (shaped[:, 0] * (filtered + skip_term * gated_rows)).astype(jnp.bfloat16)
    group_width = D // N_CH

    def add_group(group_index, running):
        offset = (group_index * group_width).astype(jnp.int32)
        channel_cols = lax.dynamic_slice_in_dim(inner_out, offset, group_width, 1)
        weight_rows = lax.dynamic_slice_in_dim(out_w, offset, group_width, 0)
        product = jnp.dot(channel_cols, weight_rows, preferred_element_type=jnp.float32)
        return running + lax.optimization_barrier(product.astype(jnp.bfloat16)).astype(jnp.float32)
    output_sum = lax.fori_loop(0, N_CH, add_group, jnp.zeros((row_count, D), jnp.float32))
    return (rows_in.astype(jnp.float32) + output_sum).astype(jnp.bfloat16)

def reference(hidden, norm_gain, in_weight, feat_filter, se_filter, mr_filter, skip_gain, out_weight):
    first_out = hyena_layer(hidden, norm_gain[0], in_weight[0], feat_filter[0], se_filter, skip_gain[0], out_weight[0])
    return hyena_layer(first_out, norm_gain[1], in_weight[1], feat_filter[1], mr_filter, skip_gain[1], out_weight[1])
```

```python
import jax
import jax.numpy as jnp
import numpy as np
from jax import lax
from jax.sharding import Mesh, PartitionSpec as P

AXES = ("xl", "y", "core", "z", "xh")


def shift(value, axis, by):
    size = lax.axis_size(axis)
    return lax.ppermute(value, axis, [(i, (i + by) % size) for i in range(size)])


def swap(value):
    moved = lax.ppermute(value, ("core", "xh"), [(1, 2), (2, 1)])
    same = lax.axis_index("core") == lax.axis_index("xh")
    return jnp.where(same, value, moved)


def behind(value, axes):
    size = 16
    return lax.ppermute(value, axes, [(i, i + 1) for i in range(size - 1)])


def around(value, axis="z"):
    return [value, shift(value, axis, 1), shift(value, axis, 2), shift(value, axis, -1)]


def in_order(pieces, me):
    stacked = jnp.stack(pieces)
    return [lax.dynamic_index_in_dim(stacked, (me - i) % len(pieces), 0, keepdims=False) for i in range(len(pieces))]


def normalize(whole_rows, gain_row):
    values = whole_rows.astype(jnp.float32)
    inverse_rms = lax.rsqrt(jnp.mean(values * values, axis=-1, keepdims=True) + 1e-06)
    return (values * inverse_rms * gain_row).astype(jnp.bfloat16)


def mix_channels(projected, axes, shaping, filter_taps, skip_term):
    length = filter_taps.shape[0]
    channels = projected.shape[2]
    head_rows, pair_rows = behind((projected[-2:, 0], projected[-(length + 1) :, 1:].reshape(length + 1, 2 * channels)), axes)
    queries = jnp.concatenate([head_rows, projected[:, 0]], axis=0).astype(jnp.float32)
    key_values = jnp.concatenate(
        [pair_rows.reshape(length + 1, 2, channels), projected[:, 1:]], axis=0
    ).astype(jnp.float32)
    query_shaped = shaping[0, 0] * queries[2:] + shaping[1, 0] * queries[1:-1] + shaping[2, 0] * queries[:-2]
    pair_shaped = (
        shaping[0, 1:] * key_values[2:] + shaping[1, 1:] * key_values[1:-1] + shaping[2, 1:] * key_values[:-2]
    )
    gated_rows = pair_shaped[:, 0] * pair_shaped[:, 1]
    rows = projected.shape[0]
    if length < 16:
        filtered = sum(filter_taps[j] * gated_rows[length - 1 - j : length - 1 - j + rows] for j in range(length))
    else:
        filtered = lax.conv_general_dilated(
            gated_rows[None],
            filter_taps[::-1][:, None, :],
            (1,),
            "VALID",
            dimension_numbers=("NWC", "WIO", "NWC"),
            feature_group_count=channels,
            precision=lax.Precision.HIGHEST,
        )[0]
    own_gated = gated_rows[length - 1 :]
    return (query_shaped * (filtered + skip_term * own_gated)).astype(jnp.bfloat16)


def per_device(hidden, norm_gain, in_weight, feat_filter, se_filter, mr_filter, skip_gain, out_weight):
    z = lax.axis_index("z")
    core = lax.axis_index("core")
    xh = lax.axis_index("xh")
    rows = hidden.shape[0]

    w0 = lax.all_gather(in_weight[0].reshape(256, 1536), ("xl", "y", "core"), axis=0, tiled=True)
    mine = out_weight[0]
    both = in_order([mine, shift(mine, "xl", 1)], lax.axis_index("xl"))
    both = jnp.stack(both)
    lines = around(both, "y")
    other = [shift(v, "core", 1) for v in lines]
    lines = jnp.stack(in_order(lines, lax.axis_index("y")))
    other = jnp.stack(in_order(other, lax.axis_index("y")))
    pair = jnp.stack([lines, other])
    pair = jnp.where(core == 0, pair, pair[::-1])
    o0 = pair.transpose(3, 2, 1, 0, 4).reshape(512, 4096)

    w1_mine = swap(in_weight[1].reshape(256, 1536))
    o1_mine = swap(out_weight[1])
    small = swap(jnp.concatenate([feat_filter[1].reshape(9, 512), skip_gain[1:2], mr_filter], axis=0))

    duo = jnp.concatenate(in_order([hidden, shift(hidden, "xh", 1)], xh), axis=1)
    whole = jnp.concatenate(in_order(around(duo), z), axis=1)
    normed = normalize(whole, norm_gain[0])
    projected = jnp.dot(normed, w0, preferred_element_type=jnp.float32).astype(jnp.bfloat16).reshape(rows, 3, 512)
    inner = mix_channels(projected, ("xl", "y", "core"), feat_filter[0], se_filter, skip_gain[0])
    part = jnp.dot(inner, o0, preferred_element_type=jnp.float32).astype(jnp.bfloat16)

    def for_z(array, by):
        return lax.dynamic_slice_in_dim(array, ((z + by) % 4) * 1024, 1024, 1)

    total = for_z(part, 0).astype(jnp.float32)
    for by in (1, -1, 2):
        total = total + shift(for_z(part, by), "z", by).astype(jnp.float32)
    total = total.astype(jnp.bfloat16)
    halves = [total[:, :512], total[:, 512:]]
    pick = lambda c: jnp.where(c == 0, halves[0], halves[1])
    first = lax.ppermute(pick(core), ("core", "xh"), [(1, 0), (2, 3)])
    second = lax.ppermute(pick(1 - core), ("core", "xh"), [(1, 2), (2, 1)])
    third = lax.ppermute(pick(1 - core), ("core", "xh"), [(0, 2), (3, 1)])
    base = swap(hidden)
    kept = jnp.where(core == xh, pick(core), jnp.zeros_like(first))
    current = (
        base.astype(jnp.float32)
        + kept.astype(jnp.float32)
        + first.astype(jnp.float32)
        + second.astype(jnp.float32)
        + third.astype(jnp.float32)
    ).astype(jnp.bfloat16)

    w1 = lax.all_gather(w1_mine, ("xh", "xl", "y"), axis=0, tiled=False)
    w1 = w1.reshape(2, 8, 256, 1536).transpose(1, 0, 2, 3).reshape(4096, 1536)
    o1 = lax.all_gather(o1_mine, ("xh", "xl", "y"), axis=0, tiled=False)
    o1 = o1.reshape(2, 8, 512, 256).transpose(2, 1, 0, 3).reshape(512, 4096)
    near = around(current)
    far = [shift(v, "core", 1) for v in near]
    near, far = jnp.stack(in_order(near, z)), jnp.stack(in_order(far, z))
    by_core = jnp.stack([near, far])
    by_core = jnp.where(core == 0, by_core, by_core[::-1])
    whole = by_core.transpose(2, 1, 0, 3).reshape(rows, 4096)
    normed = normalize(whole, norm_gain[1])
    projected = jnp.dot(normed, w1, preferred_element_type=jnp.float32).astype(jnp.bfloat16).reshape(rows, 3, 512)
    inner = mix_channels(projected, ("xl", "y", "xh"), small[:9].reshape(3, 3, 512), small[10:], small[9])
    part = jnp.dot(inner, o1, preferred_element_type=jnp.float32).astype(jnp.bfloat16)
    part = part.reshape(rows, 4, 2, 512).transpose(2, 1, 0, 3)
    own = jnp.where(core == 0, part[0], part[1])
    theirs = jnp.where(core == 0, part[1], part[0])
    both = (own.astype(jnp.float32) + shift(theirs, "core", 1).astype(jnp.float32)).astype(jnp.bfloat16)
    block = lambda by: lax.dynamic_index_in_dim(both, (z + by) % 4, 0, keepdims=False)
    total = current.astype(jnp.float32) + block(0).astype(jnp.float32)
    for by in (1, -1, 2):
        total = total + shift(block(by), "z", by).astype(jnp.float32)
    return swap(total.astype(jnp.bfloat16))


def solution(mesh):
    fine = Mesh(np.asarray(mesh.devices).reshape(2, 4, 2, 4, 2), AXES)
    ctx, ch = ("xl", "y", "core"), ("z", "xh")
    return jax.shard_map(
        per_device,
        mesh=fine,
        in_specs=(
            P(ctx, ch),
            P(),
            P(None, ctx, None, ch),
            P(None, None, None, ch),
            P(None, ch),
            P(None, ch),
            P(None, ch),
            P(None, ch, ctx),
        ),
        out_specs=P(ctx, ch),
        check_vma=False,
    )
```

```python
import functools

import jax
import jax.numpy as jnp
import numpy as np
from jax import lax
from jax.experimental import pallas as pl
from jax.experimental.pallas import tpu as pltpu
from jax.sharding import Mesh, PartitionSpec as P

AXES = ("xl", "y", "core", "z", "xh")
ROWS = 512
LANES = 128


def shift(value, axis, by):
    size = lax.axis_size(axis)
    return lax.ppermute(value, axis, [(i, (i + by) % size) for i in range(size)])


def shift_x(value, by):
    place = lambda x: (x % 2) * 2 + x // 2
    return lax.ppermute(value, ("xl", "xh"), [(place(x), place((x + by) % 4)) for x in range(4)])


def shift_y(value, by):
    return shift(value, "y", by)


def swap(value):
    moved = lax.ppermute(value, ("core", "xh"), [(1, 2), (2, 1)])
    same = lax.axis_index("core") == lax.axis_index("xh")
    return jnp.where(same, value, moved)


def from_behind(value, axes):
    return lax.ppermute(value, axes, [(i, i + 1) for i in range(15)])


def after(value, *others):
    return lax.optimization_barrier((value, *others))[0]


def ring_four(value, move):
    one = move(value, 1)
    three = move(value, -1)
    low = move(one[:2], 1)
    high = move(three[2:], -1)
    return one, three, low, high


def fetch(moves, sources, target, index_ref, semaphores):
    copies = []
    for number, (source, lead, lane, width, slot, other, by_rows) in enumerate(moves):
        block = pl.multiple_of(index_ref[slot] * 256, 256)
        ref = sources[source]
        if lead is not None:
            ref = ref.at[lead]
        if by_rows:
            piece = target.at[pl.ds(block, 256), other : other + width]
        else:
            piece = target.at[other : other + ref.shape[0], pl.ds(block, 256)]
        copies.append(pltpu.make_async_copy(ref.at[:, lane : lane + width], piece, semaphores.at[number]))
    return copies


def in_kernel(moves, pieces, halo, index_ref, gain_ref, *refs):
    xs, refs = refs[:pieces], refs[pieces:]
    count = 1 + max(m[0] for m in moves)
    ws, refs = refs[:count], refs[count:]
    out_ref, tail_ref, raw, normed, weights, squares, x_sems, w_sems = refs
    loads = [pltpu.make_async_copy(x, raw.at[j], x_sems.at[j]) for j, x in enumerate(xs)]
    for load in loads:
        load.start()
    copies = fetch(moves, ws, weights, index_ref, w_sems)
    for copy in copies:
        copy.start()
    squares[...] = jnp.zeros_like(squares)
    for j, load in enumerate(loads):
        load.wait()
        block = index_ref[j]
        lanes = pl.ds(pl.multiple_of(block * 512, 512), 512)
        gain = gain_ref[pl.ds(block, 1), :]

        @pl.loop(0, ROWS // 64)
        def _(step):
            rows = pl.ds(pl.multiple_of(step * 64, 64), 64)
            x = raw[j, rows, :].astype(jnp.float32)
            normed[rows, lanes] = (x * gain).astype(jnp.bfloat16)
            q = x * x
            squares[rows, :] += (q[:, :128] + q[:, 128:256]) + (q[:, 256:384] + q[:, 384:])

    squares[:, :1] = lax.rsqrt(jnp.sum(squares[...], axis=1, keepdims=True) * (1.0 / 4096) + 1e-06)
    for copy in copies:
        copy.wait()

    @pl.loop(0, 6)
    def _(step):
        lanes = pl.ds(pl.multiple_of(step * 256, 256), 256)
        product = jnp.dot(normed[...], weights[:, lanes], preferred_element_type=jnp.float32)
        out_ref[:, lanes] = (product * squares[:, :1]).astype(jnp.bfloat16)

    tail_ref[:halo, :] = out_ref[ROWS - halo :, 512:]
    tail_ref[halo:, :512] = out_ref[ROWS - 16 :, :512]
    tail_ref[halo:, 512:] = jnp.zeros((16, 512), jnp.bfloat16)


def project_in(index, gain, pieces, weights, moves, halo):
    any_space = pl.BlockSpec(memory_space=pl.ANY)
    vmem = pl.BlockSpec(memory_space=pltpu.VMEM)
    return pl.pallas_call(
        functools.partial(in_kernel, moves, len(pieces), halo),
        out_shape=[
            jax.ShapeDtypeStruct((ROWS, 1536), jnp.bfloat16),
            jax.ShapeDtypeStruct((halo + 16, 1024), jnp.bfloat16),
        ],
        in_specs=[pl.BlockSpec(memory_space=pltpu.SMEM), vmem] + [any_space] * (len(pieces) + len(weights)),
        out_specs=[vmem, vmem],
        scratch_shapes=[
            pltpu.VMEM((len(pieces), ROWS, 512), jnp.bfloat16),
            pltpu.VMEM((ROWS, 4096), jnp.bfloat16),
            pltpu.VMEM((4096, 1536), jnp.bfloat16),
            pltpu.VMEM((ROWS, LANES), jnp.float32),
            pltpu.SemaphoreType.DMA((len(pieces),)),
            pltpu.SemaphoreType.DMA((len(moves),)),
        ],
        compiler_params=pltpu.CompilerParams(vmem_limit_bytes=44 * 1024 * 1024),
        cost_estimate=pl.CostEstimate(flops=2 * ROWS * 4096 * 1536, bytes_accessed=18 * 2**20, transcendentals=0),
    )(index, gain, *pieces, *weights)


def mix_kernel(moves, halo, taps, outs, index_ref, tail_ref, main_ref, feat_ref, filter_ref, skip_ref, *refs):
    count = 1 + max(m[0] for m in moves)
    ws, refs = refs[:count], refs[count:]
    out_refs, refs = refs[:outs], refs[outs:]
    shaped, gated, copies8, inner, weights, w_sems = refs
    copies = fetch(moves, ws, weights, index_ref, w_sems)
    for copy in copies:
        copy.start()
    total = halo + ROWS

    shaped[:16, :512] = tail_ref[halo:, :512].astype(jnp.float32)
    shaped[16 : 16 + ROWS, :512] = main_ref[:, :512].astype(jnp.float32)
    shaped[:halo, 512:] = tail_ref[:halo, :].astype(jnp.float32)
    shaped[halo:total, 512:] = main_ref[:, 512:].astype(jnp.float32)

    def feature(start, size, s, lanes):
        value = None
        for j in range(3):
            tap = feat_ref[3 * j + s : 3 * j + s + 1, lanes]
            low = s * 512 + lanes.start
            term = tap * shaped[start - j : start - j + size, low : low + LANES]
            value = term if value is None else value + term
        return value

    for lane in range(0, 512, LANES):
        lanes = slice(lane, lane + LANES)
        for start in range(8, total, 64):
            size = min(64, total - start)
            gated[start : start + size, lanes] = feature(start, size, 1, lanes) * feature(start, size, 2, lanes)
        gated[:8, lanes] = jnp.zeros((8, LANES), jnp.float32)

    if taps == 7:
        for lane in range(0, 512, LANES):
            lanes = slice(lane, lane + LANES)
            for start in range(0, ROWS, 64):
                own = gated[halo + start : halo + start + 64, lanes]
                value = (skip_ref[:1, lanes] + filter_ref[:1, lanes]) * own
                for j in range(1, taps):
                    value = value + filter_ref[j : j + 1, lanes] * gated[halo + start - j : halo + start - j + 64, lanes]
                inner[start : start + 64, lanes] = (feature(16 + start, 64, 0, lanes) * value).astype(jnp.bfloat16)
    else:
        for lane in range(0, 512, LANES):
            lanes = slice(lane, lane + LANES)
            for r in range(8):
                for start in range(0, ROWS + 128, 128):
                    copies8[r, start : start + 128, :] = gated[16 + start - r : 16 + start - r + 128, lanes]

            @pl.loop(0, ROWS // 128)
            def _(step):
                base = pl.multiple_of(step * 128, 128)
                value = jnp.zeros((128, LANES), jnp.float32)
                for r in range(8):
                    for a in range(0, 16, 4):
                        window = copies8[r, pl.ds(pl.multiple_of(base + 128 - 8 * (a + 3), 8), 128 + 24), :]
                        for b in range(4):
                            tap = filter_ref[8 * (a + b) + r : 8 * (a + b) + r + 1, lanes]
                            low = 8 * (3 - b)
                            value = value + tap * window[low : low + 128]
                copies8[8, pl.ds(base, 128), :] = value

            for start in range(0, ROWS, 64):
                own = gated[halo + start : halo + start + 64, lanes]
                value = copies8[8, start : start + 64, :] + skip_ref[:1, lanes] * own
                inner[start : start + 64, lanes] = (feature(16 + start, 64, 0, lanes) * value).astype(jnp.bfloat16)

    for copy in copies:
        copy.wait()
    z = index_ref[16]
    core = index_ref[17]
    for by in range(4):
        block = lax.rem(z + by, 4)
        if outs == 4:
            columns = pl.ds(pl.multiple_of(block * 1024, 1024), 1024)
            out_refs[by][...] = jnp.dot(
                inner[...], weights[:, columns], preferred_element_type=jnp.float32
            ).astype(jnp.bfloat16)
        else:
            for side in range(2):
                place = block * 2 + (core if side == 0 else 1 - core)
                columns = pl.ds(pl.multiple_of(place * 512, 512), 512)
                out_refs[side][by] = jnp.dot(
                    inner[...], weights[:, columns], preferred_element_type=jnp.float32
                ).astype(jnp.bfloat16)


def mix_out(index, tail, main, feat, taps, skip, weights, moves, halo, out_shapes):
    any_space = pl.BlockSpec(memory_space=pl.ANY)
    vmem = pl.BlockSpec(memory_space=pltpu.VMEM)
    length = taps.shape[0]
    small = length == 7
    return pl.pallas_call(
        functools.partial(mix_kernel, moves, halo, length, len(out_shapes)),
        out_shape=[jax.ShapeDtypeStruct(s, jnp.bfloat16) for s in out_shapes],
        in_specs=[pl.BlockSpec(memory_space=pltpu.SMEM)] + [vmem] * 5 + [any_space] * len(weights),
        out_specs=[vmem] * len(out_shapes),
        scratch_shapes=[
            pltpu.VMEM((halo + ROWS + 16, 1536), jnp.float32),
            pltpu.VMEM((halo + ROWS, 512), jnp.float32),
            pltpu.VMEM((9, 8, LANES) if small else (9, ROWS + 128, LANES), jnp.float32),
            pltpu.VMEM((ROWS, 512), jnp.bfloat16),
            pltpu.VMEM((512, 4096), jnp.bfloat16),
            pltpu.SemaphoreType.DMA((len(moves),)),
        ],
        compiler_params=pltpu.CompilerParams(vmem_limit_bytes=44 * 1024 * 1024),
        cost_estimate=pl.CostEstimate(
            flops=2 * ROWS * 512 * 4096 * (1 if small else 4), bytes_accessed=10 * 2**20, transcendentals=0
        ),
    )(index, tail, main, feat, taps, skip, *weights)


def per_device(hidden, norm_gain, in_weight, feat_filter, se_filter, mr_filter, skip_gain, out_weight):
    xl, y, core, z, xh = (lax.axis_index(a) for a in AXES)
    x = 2 * xh + xl
    behind = lambda place, by: (place - by) % 4
    gains = norm_gain.reshape(2, 8, 512)

    partner = shift(hidden, "xh", 1)
    x_pieces, x_slots = [hidden], [z * 2 + xh]
    for by in (1, -1, 2):
        x_pieces.append(shift(hidden, "z", by))
        x_slots.append(behind(z, by) * 2 + xh)
    w = in_weight[0].reshape(256, 1536)
    w_xl = shift(w, "xl", 1)
    w_y = {by: shift_y(w, by) for by in (1, -1, 2)}
    x_pieces.append(partner)
    x_slots.append(z * 2 + 1 - xh)
    for by in (1, -1, 2):
        x_pieces.append(shift(partner, "z", by))
        x_slots.append(behind(z, by) * 2 + 1 - xh)

    held = [(w, xl, y, 0, 1536), (w_xl, 1 - xl, y, 0, 1536)]
    held += [(w_y[by], xl, behind(y, by), 0, 1536) for by in (1, -1, 2)]
    held += [(shift_y(w_xl[:, :768], by), 1 - xl, behind(y, by), 0, 768) for by in (1, -1, 2)]
    held += [(shift(w_y[by][:, 768:], "xl", 1), 1 - xl, behind(y, by), 768, 768) for by in (1, -1, 2)]
    w_list, w_moves, w_slots = [], [], []
    for c, get in ((core, lambda v: v), (1 - core, lambda v: shift(v, "core", 1))):
        for value, at_xl, at_y, lane, width in held:
            w_moves.append((len(w_list), None, 0, width, 8 + len(w_slots), lane, True))
            w_list.append(get(value))
            w_slots.append(at_xl * 8 + at_y * 2 + c)
    index = jnp.stack(x_slots + w_slots).astype(jnp.int32)
    projected, tail = project_in(index, gains[0], x_pieces, w_list, w_moves, 16)

    o = after(out_weight[0], w_list[8], w_list[10])
    o_duo = jnp.stack([o, shift(o, "xl", 1)])
    o_held = [o_duo] + [shift_y(o_duo, by) for by in (1, -1, 2)]
    o_list, o_moves, o_slots = [], [], []
    for c, get in ((core, lambda v: v), (1 - core, lambda v: shift(v, "core", 1))):
        for value, by in zip(o_held, (0, 1, -1, 2)):
            for e in range(2):
                o_moves.append((len(o_list), e, 0, 256, len(o_slots), 0, False))
                o_slots.append((xl if e == 0 else 1 - xl) * 8 + behind(y, by) * 2 + c)
            o_list.append(get(value))
    o_index = jnp.stack(o_slots + [z, core]).astype(jnp.int32)

    small = swap(jnp.concatenate([feat_filter[1].reshape(9, 512), skip_gain[1:2], mr_filter], axis=0))
    m = jnp.concatenate(
        [in_weight[1].reshape(256, 1536), out_weight[1, :256], out_weight[1, 256:]], axis=1
    )
    m = after(swap(m), w_list[8], w_list[10])
    a, b = m[:, :1024], m[:, 1024:]
    a4 = jnp.stack([a] + [shift_x(a, by) for by in (1, -1, 2)])
    b4 = jnp.stack([b] + [shift_y(b, by) for by in (1, -1, 2)])
    a_lists = (a4,) + ring_four(a4, shift_y)
    b_lists = (b4,) + ring_four(b4, shift_x)
    hops = (0, 1, -1, 2)
    block_of = lambda at_x, at_y: (at_x % 2) * 8 + at_y * 2 + at_x // 2
    w_list, w_moves, w_slots = [], [], []
    q_list, q_moves, q_slots = [], [], []
    for is_b, lists in ((False, a_lists), (True, b_lists)):
        for value, by, entries in zip(lists, (0, 1, -1, 2, 2), (range(4), range(4), range(4), (0, 1), (2, 3))):
            for lead, e in enumerate(entries):
                near, far = (y, x) if is_b else (x, y)
                near, far = behind(near, hops[e]), behind(far, by)
                slot = block_of(far, near) if is_b else block_of(near, far)
                if is_b:
                    w_moves.append((len(w_list), lead, 0, 512, 8 + len(w_slots), 1024, True))
                    for half in range(2):
                        q_moves.append((len(q_list), lead, 512 + 256 * half, 256, len(q_slots), 256 * half, False))
                    q_slots.append(slot)
                else:
                    w_moves.append((len(w_list), lead, 0, 1024, 8 + len(w_slots), 0, True))
                w_slots.append(slot)
            w_list.append(value)
            if is_b:
                q_list.append(value)

    tail = from_behind(tail, ("xl", "y", "core"))
    parts = mix_out(
        o_index, tail, projected, feat_filter[0].reshape(9, 512), se_filter, skip_gain[0:1], o_list, o_moves, 16,
        [(ROWS, 1024)] * 4,
    )
    total = parts[0].astype(jnp.float32)
    for by, part in ((1, parts[1]), (-1, parts[3]), (2, parts[2])):
        total = total + shift(part, "z", by).astype(jnp.float32)
    total = total.astype(jnp.bfloat16)
    pick = lambda c: jnp.where(c == 0, total[:, :512], total[:, 512:])
    mine, others = pick(core), pick(1 - core)
    first = lax.ppermute(mine, ("core", "xh"), [(1, 0), (2, 3)])
    second = lax.ppermute(others, ("core", "xh"), [(1, 2), (2, 1)])
    third = lax.ppermute(others, ("core", "xh"), [(0, 2), (3, 1)])
    kept = jnp.where(core == xh, mine, jnp.zeros_like(mine))
    current = swap(hidden).astype(jnp.float32) + kept.astype(jnp.float32)
    for value in (first, second, third):
        current = current + value.astype(jnp.float32)
    current = current.astype(jnp.bfloat16)

    x_pieces, x_slots = [], []
    near = [current] + [shift(current, "z", by) for by in (1, -1, 2)]
    for side, values in ((core, near), (1 - core, [shift(v, "core", 1) for v in near])):
        for value, by in zip(values, hops):
            x_pieces.append(value)
            x_slots.append(behind(z, by) * 2 + side)
    index = jnp.stack(x_slots + w_slots).astype(jnp.int32)
    projected, tail = project_in(index, gains[1], x_pieces, w_list, w_moves, 144)
    tail = from_behind(tail, ("xl", "y", "xh"))
    q_slots = q_slots + [z, core]
    own, theirs = mix_out(
        jnp.stack(q_slots).astype(jnp.int32), tail, projected, small[:9], small[10:], small[9:10], q_list, q_moves, 144,
        [(4, ROWS, 512)] * 2,
    )
    both = (own.astype(jnp.float32) + shift(theirs, "core", 1).astype(jnp.float32)).astype(jnp.bfloat16)
    total = current.astype(jnp.float32) + both[0].astype(jnp.float32)
    for by, place in ((1, 1), (-1, 3), (2, 2)):
        total = total + shift(both[place], "z", by).astype(jnp.float32)
    return swap(total.astype(jnp.bfloat16))


def solution(mesh):
    fine = Mesh(np.asarray(mesh.devices).reshape(2, 4, 2, 4, 2), AXES)
    ctx, ch = ("xl", "y", "core"), ("z", "xh")
    return jax.shard_map(
        per_device,
        mesh=fine,
        in_specs=(
            P(ctx, ch),
            P(),
            P(None, ctx, None, ch),
            P(None, None, None, ch),
            P(None, ch),
            P(None, ch),
            P(None, ch),
            P(None, ch, ctx),
        ),
        out_specs=P(ctx, ch),
        check_vma=False,
    )
```

```python
import functools

import jax
import jax.numpy as jnp
import numpy as np
from jax import lax
from jax.experimental.layout import Layout, with_layout_constraint
from jax.experimental import pallas as pl
from jax.experimental.pallas import tpu as pltpu
from jax.sharding import Mesh, PartitionSpec as P

AXES = ("xl", "y", "core", "z", "xh")
ROWS = 512
LANES = 128
CUT = 1152


def shift(value, axis, by):
    size = lax.axis_size(axis)
    return lax.ppermute(value, axis, [(i, (i + by) % size) for i in range(size)])


def shift_y(value, by):
    return shift(value, "y", by)


def swap(value):
    moved = lax.ppermute(value, ("core", "xh"), [(1, 2), (2, 1)])
    same = lax.axis_index("core") == lax.axis_index("xh")
    return jnp.where(same, value, moved)


def from_behind(value, axes):
    return lax.ppermute(value, axes, [(i, i + 1) for i in range(15)])


def by_rows(value):
    return with_layout_constraint(value, Layout(major_to_minor=tuple(range(value.ndim))))


def after(value, *others):
    return lax.optimization_barrier((value, *others))[0]


def fetch(moves, sources, target, index_ref, semaphores):
    copies = []
    for number, (source, lead, lane, width, slot, other, by_rows, *fixed) in enumerate(moves):
        block = fixed[0] * 256 if slot is None else pl.multiple_of(index_ref[slot] * 256, 256)
        ref = sources[source]
        if lead is not None:
            ref = ref.at[lead]
        if by_rows:
            piece = target.at[pl.ds(block, 256), other : other + width]
        else:
            piece = target.at[other : other + ref.shape[0], pl.ds(block, 256)]
        copies.append(pltpu.make_async_copy(ref.at[:, lane : lane + width], piece, semaphores.at[number]))
    return copies


def in_kernel(x_moves, moves, pieces, halo, index_ref, gain_ref, *refs):
    xs, refs = refs[:pieces], refs[pieces:]
    count = 1 + max(m[0] for m in moves)
    ws, refs = refs[:count], refs[count:]
    out_ref, tail_ref, raw, normed, weights, squares, x_sems, w_sems = refs
    loads = []
    for j, (source, lead, _) in enumerate(x_moves):
        x = xs[source] if lead is None else xs[source].at[lead]
        loads.append(pltpu.make_async_copy(x, raw.at[j], x_sems.at[j]))
    for load in loads:
        load.start()
    copies = fetch(moves, ws, weights, index_ref, w_sems)
    for copy in copies:
        copy.start()
    squares[...] = jnp.zeros_like(squares)
    for j, load in enumerate(loads):
        load.wait()
        block = x_moves[j][2] if x_moves[j][1] is not None else index_ref[j]
        lanes = pl.ds(pl.multiple_of(block * 512, 512), 512)
        gain = gain_ref[pl.ds(block, 1), :]

        @pl.loop(0, ROWS // 64)
        def _(step):
            rows = pl.ds(pl.multiple_of(step * 64, 64), 64)
            x = raw[j, rows, :].astype(jnp.float32)
            normed[rows, lanes] = (x * gain).astype(jnp.bfloat16)
            q = x * x
            squares[rows, :] += (q[:, :128] + q[:, 128:256]) + (q[:, 256:384] + q[:, 384:])

    squares[:, :1] = lax.rsqrt(jnp.sum(squares[...], axis=1, keepdims=True) * (1.0 / 4096) + 1e-06)
    for copy in copies:
        copy.wait()

    @pl.loop(0, 6)
    def _(step):
        lanes = pl.ds(pl.multiple_of(step * 256, 256), 256)
        product = jnp.dot(normed[...], weights[:, lanes], preferred_element_type=jnp.float32)
        out_ref[:, lanes] = (product * squares[:, :1]).astype(jnp.bfloat16)

    tail_ref[:halo, :] = out_ref[ROWS - halo :, 512:]
    tail_ref[halo:, :512] = out_ref[ROWS - 16 :, :512]
    tail_ref[halo:, 512:] = jnp.zeros((16, 512), jnp.bfloat16)


def project_in(index, gain, pieces, x_moves, weights, moves, halo):
    any_space = pl.BlockSpec(memory_space=pl.ANY)
    vmem = pl.BlockSpec(memory_space=pltpu.VMEM)
    return pl.pallas_call(
        functools.partial(in_kernel, x_moves, moves, len(pieces), halo),
        out_shape=[
            jax.ShapeDtypeStruct((ROWS, 1536), jnp.bfloat16),
            jax.ShapeDtypeStruct((halo + 16, 1024), jnp.bfloat16),
        ],
        in_specs=[pl.BlockSpec(memory_space=pltpu.SMEM), vmem] + [any_space] * (len(pieces) + len(weights)),
        out_specs=[vmem, vmem],
        scratch_shapes=[
            pltpu.VMEM((8, ROWS, 512), jnp.bfloat16),
            pltpu.VMEM((ROWS, 4096), jnp.bfloat16),
            pltpu.VMEM((4096, 1536), jnp.bfloat16),
            pltpu.VMEM((ROWS, LANES), jnp.float32),
            pltpu.SemaphoreType.DMA((8,)),
            pltpu.SemaphoreType.DMA((len(moves),)),
        ],
        compiler_params=pltpu.CompilerParams(vmem_limit_bytes=44 * 1024 * 1024),
        cost_estimate=pl.CostEstimate(flops=2 * ROWS * 4096 * 1536, bytes_accessed=18 * 2**20, transcendentals=0),
    )(index, gain, *pieces, *weights)


def mix_kernel(moves, halo, taps, outs, index_ref, tail_ref, main_ref, feat_ref, filter_ref, skip_ref, *refs):
    count = 1 + max(m[0] for m in moves)
    ws, refs = refs[:count], refs[count:]
    out_refs, refs = refs[:outs], refs[outs:]
    shaped, gated, copies8, inner, weights, w_sems = refs
    copies = fetch(moves, ws, weights, index_ref, w_sems)
    for copy in copies:
        copy.start()
    total = halo + ROWS

    shaped[:16, :512] = tail_ref[halo:, :512].astype(jnp.float32)
    shaped[16 : 16 + ROWS, :512] = main_ref[:, :512].astype(jnp.float32)
    shaped[:halo, 512:] = tail_ref[:halo, :].astype(jnp.float32)
    shaped[halo:total, 512:] = main_ref[:, 512:].astype(jnp.float32)

    def feature(start, size, s, lanes):
        value = None
        for j in range(3):
            tap = feat_ref[3 * j + s : 3 * j + s + 1, lanes]
            low = s * 512 + lanes.start
            term = tap * shaped[start - j : start - j + size, low : low + LANES]
            value = term if value is None else value + term
        return value

    for lane in range(0, 512, LANES):
        lanes = slice(lane, lane + LANES)
        for start in range(8, total, 64):
            size = min(64, total - start)
            gated[start : start + size, lanes] = feature(start, size, 1, lanes) * feature(start, size, 2, lanes)
        gated[:8, lanes] = jnp.zeros((8, LANES), jnp.float32)

    if taps == 7:
        for lane in range(0, 512, LANES):
            lanes = slice(lane, lane + LANES)
            for start in range(0, ROWS, 64):
                own = gated[halo + start : halo + start + 64, lanes]
                value = (skip_ref[:1, lanes] + filter_ref[:1, lanes]) * own
                for j in range(1, taps):
                    value = value + filter_ref[j : j + 1, lanes] * gated[halo + start - j : halo + start - j + 64, lanes]
                inner[start : start + 64, lanes] = (feature(16 + start, 64, 0, lanes) * value).astype(jnp.bfloat16)
    else:
        for lane in range(0, 512, LANES):
            lanes = slice(lane, lane + LANES)
            for r in range(8):
                for start in range(0, ROWS + 128, 128):
                    copies8[r, start : start + 128, :] = gated[16 + start - r : 16 + start - r + 128, lanes]

            @pl.loop(0, ROWS // 128)
            def _(step):
                base = pl.multiple_of(step * 128, 128)
                value = jnp.zeros((128, LANES), jnp.float32)
                for r in range(8):
                    for a in range(0, 16, 4):
                        window = copies8[r, pl.ds(pl.multiple_of(base + 128 - 8 * (a + 3), 8), 128 + 24), :]
                        for b in range(4):
                            tap = filter_ref[8 * (a + b) + r : 8 * (a + b) + r + 1, lanes]
                            low = 8 * (3 - b)
                            value = value + tap * window[low : low + 128]
                copies8[8, pl.ds(base, 128), :] = value

            for start in range(0, ROWS, 64):
                own = gated[halo + start : halo + start + 64, lanes]
                value = copies8[8, start : start + 64, :] + skip_ref[:1, lanes] * own
                inner[start : start + 64, lanes] = (feature(16 + start, 64, 0, lanes) * value).astype(jnp.bfloat16)

    for copy in copies:
        copy.wait()
    z = index_ref[0]
    core = index_ref[1]
    for by in range(4):
        block = lax.rem(z + by, 4)
        if outs == 4:
            columns = pl.ds(pl.multiple_of(block * 1024, 1024), 1024)
            out_refs[by][...] = jnp.dot(
                inner[...], weights[:, columns], preferred_element_type=jnp.float32
            ).astype(jnp.bfloat16)
        else:
            for side in range(2):
                place = block * 2 + (core if side == 0 else 1 - core)
                columns = pl.ds(pl.multiple_of(place * 512, 512), 512)
                out_refs[side][by] = jnp.dot(
                    inner[...], weights[:, columns], preferred_element_type=jnp.float32
                ).astype(jnp.bfloat16)


def mix_out(index, tail, main, feat, taps, skip, weights, moves, halo, out_shapes):
    any_space = pl.BlockSpec(memory_space=pl.ANY)
    vmem = pl.BlockSpec(memory_space=pltpu.VMEM)
    length = taps.shape[0]
    small = length == 7
    return pl.pallas_call(
        functools.partial(mix_kernel, moves, halo, length, len(out_shapes)),
        out_shape=[jax.ShapeDtypeStruct(s, jnp.bfloat16) for s in out_shapes],
        in_specs=[pl.BlockSpec(memory_space=pltpu.SMEM)] + [vmem] * 5 + [any_space] * len(weights),
        out_specs=[vmem] * len(out_shapes),
        scratch_shapes=[
            pltpu.VMEM((halo + ROWS + 16, 1536), jnp.float32),
            pltpu.VMEM((halo + ROWS, 512), jnp.float32),
            pltpu.VMEM((9, 8, LANES) if small else (9, ROWS + 128, LANES), jnp.float32),
            pltpu.VMEM((ROWS, 512), jnp.bfloat16),
            pltpu.VMEM((512, 4096), jnp.bfloat16),
            pltpu.SemaphoreType.DMA((len(moves),)),
        ],
        compiler_params=pltpu.CompilerParams(vmem_limit_bytes=44 * 1024 * 1024),
        cost_estimate=pl.CostEstimate(
            flops=2 * ROWS * 512 * 4096 * (1 if small else 4), bytes_accessed=10 * 2**20, transcendentals=0
        ),
    )(index, tail, main, feat, taps, skip, *weights)


def per_device(hidden, norm_gain, in_weight, feat_filter, se_filter, mr_filter, skip_gain, out_weight):
    xl, y, core, z, xh = (lax.axis_index(a) for a in AXES)
    behind = lambda place, by: (place - by) % 4
    gains = norm_gain.reshape(2, 8, 512)
    hops = (0, 1, -1, 2)

    def side_by_side(layer):
        return jnp.concatenate(
            [in_weight[layer].reshape(256, 1536), out_weight[layer, :256], out_weight[layer, 256:]], axis=1
        )

    whole = lax.all_gather(hidden, ("z", "xh"), axis=0, tiled=False)

    m = side_by_side(0)
    m_y = {by: shift_y(m, by) for by in (1, -1, 2)}
    m_xl = shift(m, "xl", 1)
    held = [(m, xl, y, 0, 2048), (m_xl, 1 - xl, y, 0, 2048)]
    held += [(m_y[by], xl, behind(y, by), 0, 2048) for by in (1, -1, 2)]
    rest = shift(jnp.stack([m_y[by][:, CUT:] for by in (1, -1, 2)]), "xl", 1)
    held += [(shift_y(m_xl[:, :CUT], by), 1 - xl, behind(y, by), 0, CUT) for by in (1, -1, 2)]
    w_list, w_moves, w_slots = [], [], []
    q_list, q_moves, q_slots = [], [], []
    for c, get in ((core, lambda v: v), (1 - core, lambda v: shift(v, "core", 1))):
        ready = [(get(value), None, *where) for value, *where in held]
        value = get(rest)
        ready += [(value, e, 1 - xl, behind(y, by), CUT, 2048) for e, by in enumerate((1, -1, 2))]
        for value, lead, at_xl, at_y, low, high in ready:
            slot = at_xl * 8 + at_y * 2 + c
            w_moves.append((len(w_list), lead, 0, min(high, 1536) - low, len(w_slots), low, True))
            w_list.append(value)
            w_slots.append(slot)
            if high == 2048:
                for half in range(2):
                    q_moves.append((len(q_list), lead, 1536 + 256 * half - low, 256, 2 + len(q_slots), 256 * half, False))
                q_list.append(value)
                q_slots.append(slot)
    w_index = jnp.stack(w_slots).astype(jnp.int32)
    q_index = jnp.stack([z, core] + q_slots).astype(jnp.int32)

    m = swap(by_rows(after(side_by_side(1), m_xl, *m_y.values())))
    m = after(m, *w_list[5:9])
    w1 = by_rows(lax.all_gather(by_rows(m[:, :1536]), ("xh", "xl", "y"), axis=0, tiled=False))
    o1 = by_rows(lax.all_gather(by_rows(m[:, 1536:]), ("xh", "xl", "y"), axis=0, tiled=False))
    small, base = jnp.concatenate([feat_filter[1].reshape(9, 512), skip_gain[1:2], mr_filter], axis=0), hidden
    small, base = after((small, base), *w_list[5:9])
    small, base = swap(small), swap(base)

    x_moves = [(0, j, j) for j in range(8)]
    projected, tail = project_in(w_index, gains[0], [whole], x_moves, w_list, w_moves, 16)
    tail = from_behind(tail, ("xl", "y", "core"))
    parts = mix_out(
        q_index, tail, projected, feat_filter[0].reshape(9, 512), se_filter, skip_gain[0:1], q_list, q_moves, 16,
        [(ROWS, 1024)] * 4,
    )
    total = parts[0].astype(jnp.float32)
    for by, part in ((1, parts[1]), (-1, parts[3]), (2, parts[2])):
        total = total + shift(part, "z", by).astype(jnp.float32)
    total = total.astype(jnp.bfloat16)
    pick = lambda c: jnp.where(c == 0, total[:, :512], total[:, 512:])
    mine, others = pick(core), pick(1 - core)
    first = lax.ppermute(mine, ("core", "xh"), [(1, 0), (2, 3)])
    second = lax.ppermute(others, ("core", "xh"), [(1, 2), (2, 1)])
    third = lax.ppermute(others, ("core", "xh"), [(0, 2), (3, 1)])
    kept = jnp.where(core == xh, mine, jnp.zeros_like(mine))
    current = base.astype(jnp.float32) + kept.astype(jnp.float32)
    for value in (first, second, third):
        current = current + value.astype(jnp.float32)
    current = current.astype(jnp.bfloat16)

    x_pieces, x_slots = [], []
    near = [current] + [shift(current, "z", by) for by in (1, -1, 2)]
    for side, values in ((core, near), (1 - core, [shift(v, "core", 1) for v in near])):
        for value, by in zip(values, hops):
            x_pieces.append(value)
            x_slots.append(behind(z, by) * 2 + side)
    index = jnp.stack(x_slots).astype(jnp.int32)
    places = [(p, (p // 4 % 2) * 8 + (p % 4) * 2 + p // 8) for p in range(16)]
    x_moves = [(j, None, j) for j in range(8)]
    w_moves = [(0, p, 0, 1536, None, 0, True, block) for p, block in places]
    projected, tail = project_in(index, gains[1], x_pieces, x_moves, [w1], w_moves, 144)
    tail = from_behind(tail, ("xl", "y", "xh"))
    q_moves = [(0, p, 256 * half, 256, None, 256 * half, False, block) for p, block in places for half in range(2)]
    own, theirs = mix_out(
        jnp.stack([z, core]).astype(jnp.int32), tail, projected, small[:9], small[10:], small[9:10], [o1], q_moves, 144,
        [(4, ROWS, 512)] * 2,
    )
    both = (own.astype(jnp.float32) + shift(theirs, "core", 1).astype(jnp.float32)).astype(jnp.bfloat16)
    total = current.astype(jnp.float32) + both[0].astype(jnp.float32)
    for by, place in ((1, 1), (-1, 3), (2, 2)):
        total = total + shift(both[place], "z", by).astype(jnp.float32)
    return swap(total.astype(jnp.bfloat16))


def solution(mesh):
    fine = Mesh(np.asarray(mesh.devices).reshape(2, 4, 2, 4, 2), AXES)
    ctx, ch = ("xl", "y", "core"), ("z", "xh")
    return jax.shard_map(
        per_device,
        mesh=fine,
        in_specs=(
            P(ctx, ch),
            P(),
            P(None, ctx, None, ch),
            P(None, None, None, ch),
            P(None, ch),
            P(None, ch),
            P(None, ch),
            P(None, ch, ctx),
        ),
        out_specs=P(ctx, ch),
        check_vma=False,
    )
```

```python
import functools

import jax
import jax.numpy as jnp
import numpy as np
from jax import lax
from jax.experimental.layout import Layout, with_layout_constraint
from jax.experimental import pallas as pl
from jax.experimental.pallas import tpu as pltpu
from jax.sharding import Mesh, PartitionSpec as P

AXES = ("xl", "y", "core", "z", "xh")
HALF = 256
LANES = 128
CUT = 896


def shift(value, axis, by):
    size = lax.axis_size(axis)
    return lax.ppermute(value, axis, [(i, (i + by) % size) for i in range(size)])


def shift_y(value, by):
    return shift(value, "y", by)


def swap(value):
    moved = lax.ppermute(value, ("core", "xh"), [(1, 2), (2, 1)])
    same = lax.axis_index("core") == lax.axis_index("xh")
    return jnp.where(same, value, moved)


def from_behind(value, axes):
    return lax.ppermute(value, axes, [(i, i + 1) for i in range(15)])


def by_rows(value):
    return with_layout_constraint(value, Layout(major_to_minor=tuple(range(value.ndim))))


def after(value, *others):
    return lax.optimization_barrier((value, *others))[0]


def fetch(moves, sources, target, index_ref, semaphores):
    copies = []
    for number, (source, lead, lane, width, slot, other, by_rows, *fixed) in enumerate(moves):
        block = fixed[0] * 256 if slot is None else pl.multiple_of(index_ref[slot] * 256, 256)
        ref = sources[source]
        if lead is not None:
            ref = ref.at[lead]
        if by_rows:
            piece = target.at[pl.ds(block, 256), other : other + width]
        else:
            piece = target.at[other : other + ref.shape[0], pl.ds(block, 256)]
        copies.append(pltpu.make_async_copy(ref.at[:, lane : lane + width], piece, semaphores.at[number]))
    return copies


def in_kernel(x_moves, moves, sources, parts, halo, index_ref, gain_ref, *refs):
    xs, refs = refs[:sources], refs[sources:]
    count = 1 + max(m[0] for m in moves)
    ws, refs = refs[:count], refs[count:]
    out_refs, refs = refs[:parts], refs[parts:]
    tail_ref, refs = (refs[0], refs[1:]) if halo else (None, refs)
    raw, normed, weights, squares, x_sems, w_sems = refs
    loads = []
    for j, (source, lead, _) in enumerate(x_moves):
        x = xs[source] if lead is None else xs[source].at[lead]
        loads.append(pltpu.make_async_copy(x, raw.at[j], x_sems.at[j]))
    for load in loads:
        load.start()
    copies = fetch(moves, ws, weights, index_ref, w_sems)
    for copy in copies:
        copy.start()
    squares[...] = jnp.zeros_like(squares)
    for j, load in enumerate(loads):
        load.wait()
        block = x_moves[j][2] if x_moves[j][1] is not None else index_ref[j]
        lanes = pl.ds(pl.multiple_of(block * 512, 512), 512)
        gain = gain_ref[pl.ds(block, 1), :]

        @pl.loop(0, parts * HALF // 64)
        def _(step):
            rows = pl.ds(pl.multiple_of(step * 64, 64), 64)
            x = raw[j, rows, :].astype(jnp.float32)
            normed[rows, lanes] = (x * gain).astype(jnp.bfloat16)
            q = x * x
            squares[rows, :] += (q[:, :128] + q[:, 128:256]) + (q[:, 256:384] + q[:, 384:])

    squares[:, :1] = lax.rsqrt(jnp.sum(squares[...], axis=1, keepdims=True) * (1.0 / 4096) + 1e-06)
    for copy in copies:
        copy.wait()

    @pl.loop(0, 6)
    def _(step):
        lanes = pl.ds(pl.multiple_of(step * 256, 256), 256)
        product = jnp.dot(normed[...], weights[:, lanes], preferred_element_type=jnp.float32)
        product = (product * squares[:, :1]).astype(jnp.bfloat16)
        for part, out_ref in enumerate(out_refs):
            out_ref[:, lanes] = product[part * HALF : (part + 1) * HALF]

    if halo:
        last = out_refs[-1]
        tail_ref[:halo, :] = last[HALF - halo :, 512:]
        tail_ref[halo:, :512] = last[HALF - 16 :, :512]
        tail_ref[halo:, 512:] = jnp.zeros((16, 512), jnp.bfloat16)


def project_in(index, gain, pieces, x_moves, weights, moves, parts, halo):
    any_space = pl.BlockSpec(memory_space=pl.ANY)
    vmem = pl.BlockSpec(memory_space=pltpu.VMEM)
    rows = parts * HALF
    shapes = [jax.ShapeDtypeStruct((HALF, 1536), jnp.bfloat16)] * parts
    if halo:
        shapes.append(jax.ShapeDtypeStruct((halo + 16, 1024), jnp.bfloat16))
    return pl.pallas_call(
        functools.partial(in_kernel, x_moves, moves, len(pieces), parts, halo),
        out_shape=shapes,
        in_specs=[pl.BlockSpec(memory_space=pltpu.SMEM), vmem] + [any_space] * (len(pieces) + len(weights)),
        out_specs=[vmem] * len(shapes),
        scratch_shapes=[
            pltpu.VMEM((8, rows, 512), jnp.bfloat16),
            pltpu.VMEM((rows, 4096), jnp.bfloat16),
            pltpu.VMEM((4096, 1536), jnp.bfloat16),
            pltpu.VMEM((rows, LANES), jnp.float32),
            pltpu.SemaphoreType.DMA((8,)),
            pltpu.SemaphoreType.DMA((len(moves),)),
        ],
        compiler_params=pltpu.CompilerParams(vmem_limit_bytes=40 * 1024 * 1024),
        cost_estimate=pl.CostEstimate(flops=2 * rows * 4096 * 1536, bytes_accessed=18 * 2**20, transcendentals=0),
    )(index, gain, *pieces, *weights)


def mix_kernel(moves, halo, taps, outs, index_ref, before_ref, main_ref, feat_ref, filter_ref, skip_ref, *refs):
    count = 1 + max(m[0] for m in moves)
    ws, refs = refs[:count], refs[count:]
    out_refs, refs = refs[:outs], refs[outs:]
    shaped, gated, copies8, inner, weights, w_sems = refs
    copies = fetch(moves, ws, weights, index_ref, w_sems)
    for copy in copies:
        copy.start()
    total = halo + HALF

    if before_ref.shape[1] == 1024:
        shaped[:16, :512] = before_ref[halo:, :512].astype(jnp.float32)
        shaped[:halo, 512:] = before_ref[:halo, :].astype(jnp.float32)
    else:
        shaped[:16, :512] = before_ref[HALF - 16 :, :512].astype(jnp.float32)
        shaped[:halo, 512:] = before_ref[HALF - halo :, 512:].astype(jnp.float32)
    shaped[16 : 16 + HALF, :512] = main_ref[:, :512].astype(jnp.float32)
    shaped[halo:total, 512:] = main_ref[:, 512:].astype(jnp.float32)

    def feature(start, size, s, lanes):
        value = None
        for j in range(3):
            tap = feat_ref[3 * j + s : 3 * j + s + 1, lanes]
            low = s * 512 + lanes.start
            term = tap * shaped[start - j : start - j + size, low : low + LANES]
            value = term if value is None else value + term
        return value

    for lane in range(0, 512, LANES):
        lanes = slice(lane, lane + LANES)
        for start in range(8, total, 64):
            size = min(64, total - start)
            gated[start : start + size, lanes] = feature(start, size, 1, lanes) * feature(start, size, 2, lanes)
        gated[:8, lanes] = jnp.zeros((8, LANES), jnp.float32)

    if taps == 7:
        for lane in range(0, 512, LANES):
            lanes = slice(lane, lane + LANES)
            for start in range(0, HALF, 64):
                own = gated[halo + start : halo + start + 64, lanes]
                value = (skip_ref[:1, lanes] + filter_ref[:1, lanes]) * own
                for j in range(1, taps):
                    value = value + filter_ref[j : j + 1, lanes] * gated[halo + start - j : halo + start - j + 64, lanes]
                inner[start : start + 64, lanes] = (feature(16 + start, 64, 0, lanes) * value).astype(jnp.bfloat16)
    else:
        for lane in range(0, 512, LANES):
            lanes = slice(lane, lane + LANES)
            for r in range(8):
                for start in range(0, HALF + 128, 128):
                    copies8[r, start : start + 128, :] = gated[16 + start - r : 16 + start - r + 128, lanes]

            @pl.loop(0, HALF // 128)
            def _(step):
                base = pl.multiple_of(step * 128, 128)
                value = jnp.zeros((128, LANES), jnp.float32)
                for r in range(8):
                    for a in range(0, 16, 4):
                        window = copies8[r, pl.ds(pl.multiple_of(base + 128 - 8 * (a + 3), 8), 128 + 24), :]
                        for b in range(4):
                            tap = filter_ref[8 * (a + b) + r : 8 * (a + b) + r + 1, lanes]
                            low = 8 * (3 - b)
                            value = value + tap * window[low : low + 128]
                copies8[8, pl.ds(base, 128), :] = value

            for start in range(0, HALF, 64):
                own = gated[halo + start : halo + start + 64, lanes]
                value = copies8[8, start : start + 64, :] + skip_ref[:1, lanes] * own
                inner[start : start + 64, lanes] = (feature(16 + start, 64, 0, lanes) * value).astype(jnp.bfloat16)

    for copy in copies:
        copy.wait()
    z = index_ref[0]
    core = index_ref[1]
    for by in range(4):
        block = lax.rem(z + by, 4)
        if outs == 4:
            columns = pl.ds(pl.multiple_of(block * 1024, 1024), 1024)
            out_refs[by][...] = jnp.dot(
                inner[...], weights[:, columns], preferred_element_type=jnp.float32
            ).astype(jnp.bfloat16)
        else:
            for side in range(2):
                place = block * 2 + (core if side == 0 else 1 - core)
                columns = pl.ds(pl.multiple_of(place * 512, 512), 512)
                out_refs[side][by] = jnp.dot(
                    inner[...], weights[:, columns], preferred_element_type=jnp.float32
                ).astype(jnp.bfloat16)


def mix_out(index, before, main, feat, taps, skip, weights, moves, halo, out_shapes):
    any_space = pl.BlockSpec(memory_space=pl.ANY)
    vmem = pl.BlockSpec(memory_space=pltpu.VMEM)
    length = taps.shape[0]
    small = length == 7
    return pl.pallas_call(
        functools.partial(mix_kernel, moves, halo, length, len(out_shapes)),
        out_shape=[jax.ShapeDtypeStruct(s, jnp.bfloat16) for s in out_shapes],
        in_specs=[pl.BlockSpec(memory_space=pltpu.SMEM)] + [vmem] * 5 + [any_space] * len(weights),
        out_specs=[vmem] * len(out_shapes),
        scratch_shapes=[
            pltpu.VMEM((halo + HALF + 16, 1536), jnp.float32),
            pltpu.VMEM((halo + HALF, 512), jnp.float32),
            pltpu.VMEM((9, 8, LANES) if small else (9, HALF + 128, LANES), jnp.float32),
            pltpu.VMEM((HALF, 512), jnp.bfloat16),
            pltpu.VMEM((512, 4096), jnp.bfloat16),
            pltpu.SemaphoreType.DMA((len(moves),)),
        ],
        compiler_params=pltpu.CompilerParams(vmem_limit_bytes=32 * 1024 * 1024),
        cost_estimate=pl.CostEstimate(
            flops=2 * HALF * 512 * 4096 * (1 if small else 4), bytes_accessed=6 * 2**20, transcendentals=0
        ),
    )(index, before, main, feat, taps, skip, *weights)


def per_device(hidden, norm_gain, in_weight, feat_filter, se_filter, mr_filter, skip_gain, out_weight):
    xl, y, core, z, xh = (lax.axis_index(a) for a in AXES)
    behind = lambda place, by: (place - by) % 4
    gains = norm_gain.reshape(2, 8, 512)
    ways = (1, -1, 2)

    def side_by_side(layer):
        blocks = [in_weight[layer, :, s] for s in range(3)] + [out_weight[layer, :256], out_weight[layer, 256:]]
        return by_rows(jnp.concatenate(blocks, axis=1))

    whole = lax.all_gather(hidden, ("z", "xh"), axis=0, tiled=False)

    m = side_by_side(0)
    w = m[:, :1536]
    m_xl = shift(m, "xl", 1)
    w_xl = m_xl[:, :1536]
    w_y = [shift_y(w, by) for by in ways]
    first = jnp.stack([w, w_xl, *w_y])
    first_far = shift(first, "core", 1)
    rest = shift(jnp.stack([v[:, CUT:] for v in w_y]), "xl", 1)
    most = [shift_y(m_xl[:, :CUT], by) for by in ways]
    o = jnp.stack([m[:, 1536:], m_xl[:, 1536:]])
    o_list = [o] + [shift_y(after(o, rest, *most), by) for by in ways]

    w_list, w_moves, slots = [first, first_far, rest, *most], [], []

    def take(number, lead, at_xl, at_y, at_core, low, high):
        w_moves.append((number, lead, 0, high - low, len(slots), low, True))
        slots.append(at_xl * 8 + at_y * 2 + at_core)

    for number, c in ((0, core), (1, 1 - core)):
        take(number, 0, xl, y, c, 0, 1536)
        take(number, 1, 1 - xl, y, c, 0, 1536)
        for e, by in enumerate(ways):
            take(number, 2 + e, xl, behind(y, by), c, 0, 1536)
    w_list += [shift(v, "core", 1) for v in w_list[2:6]]
    for number, c in ((2, core), (6, 1 - core)):
        for e, by in enumerate(ways):
            take(number, e, 1 - xl, behind(y, by), c, CUT, 1536)
            take(number + 1 + e, None, 1 - xl, behind(y, by), c, 0, CUT)
    w_index = jnp.stack(slots).astype(jnp.int32)

    q_moves, slots = [], [z, core]
    for number, (c, by) in enumerate([(c, by) for c in (core, 1 - core) for by in (0, *ways)]):
        for e, at_xl in enumerate((xl, 1 - xl)):
            for half in range(2):
                q_moves.append((number, e, 256 * half, 256, len(slots), 256 * half, False))
            slots.append(at_xl * 8 + behind(y, by) * 2 + c)
    q_index = jnp.stack(slots).astype(jnp.int32)

    m1 = swap(side_by_side(1))
    m1 = after(m1, m_xl, *w_y)
    w1 = by_rows(lax.all_gather(by_rows(m1[:, :1536]), ("xh", "xl", "y"), axis=0, tiled=False))
    o1 = by_rows(lax.all_gather(by_rows(m1[:, 1536:]), ("xh", "xl", "y"), axis=0, tiled=False))
    small, base = jnp.concatenate([feat_filter[1].reshape(9, 512), skip_gain[1:2], mr_filter], axis=0), hidden
    small, base = after((small, base), rest, *most)
    small, base = swap(small), swap(base)

    x_moves = [(0, j, j) for j in range(8)]
    low, high, tail = project_in(w_index, gains[0], [whole], x_moves, w_list, w_moves, 2, 16)
    q_list = o_list + [shift(after(v, tail), "core", 1) for v in o_list]
    tail = from_behind(tail, ("xl", "y", "core"))

    def sum_first(before, main, rows):
        parts = mix_out(
            q_index, before, main, feat_filter[0].reshape(9, 512), se_filter, skip_gain[0:1], q_list, q_moves, 16,
            [(HALF, 1024)] * 4,
        )
        total = parts[0].astype(jnp.float32)
        for by, part in ((1, parts[1]), (-1, parts[3]), (2, parts[2])):
            total = total + shift(part, "z", by).astype(jnp.float32)
        total = total.astype(jnp.bfloat16)
        pick = lambda c: jnp.where(c == 0, total[:, :512], total[:, 512:])
        mine, others = pick(core), pick(1 - core)
        one = lax.ppermute(mine, ("core", "xh"), [(1, 0), (2, 3)])
        two = lax.ppermute(others, ("core", "xh"), [(1, 2), (2, 1)])
        three = lax.ppermute(others, ("core", "xh"), [(0, 2), (3, 1)])
        kept = jnp.where(core == xh, mine, jnp.zeros_like(mine))
        current = base[rows : rows + HALF].astype(jnp.float32) + kept.astype(jnp.float32)
        for value in (one, two, three):
            current = current + value.astype(jnp.float32)
        return current.astype(jnp.bfloat16)

    high = sum_first(low, high, HALF)
    low = sum_first(tail, low, 0)

    places = [(p, (p // 4 % 2) * 8 + (p % 4) * 2 + p // 8) for p in range(16)]
    w_moves = [(0, p, 0, 1536, None, 0, True, block) for p, block in places]
    q_moves = [(0, p, 256 * half, 256, None, 256 * half, False, block) for p, block in places for half in range(2)]
    x_moves = [(j, None, j) for j in range(8)]
    x_index = jnp.stack([behind(z, by) * 2 + c for c in (core, 1 - core) for by in (0, *ways)]).astype(jnp.int32)

    def projected(rows, halo):
        near = [rows] + [shift(rows, "z", by) for by in ways]
        far = [shift(v, "core", 1) for v in near]
        return project_in(x_index, gains[1], near + far, x_moves, [w1], w_moves, 1, halo)

    p_high, tail = projected(high, 144)
    tail = from_behind(tail, ("xl", "y", "xh"))
    (p_low,) = projected(low, 0)
    place = jnp.stack([z, core]).astype(jnp.int32)

    def sum_second(before, main, rows):
        own, theirs = mix_out(
            place, before, main, small[:9], small[10:], small[9:10], [o1], q_moves, 144, [(4, HALF, 512)] * 2
        )
        both = (own.astype(jnp.float32) + shift(theirs, "core", 1).astype(jnp.float32)).astype(jnp.bfloat16)
        total = rows.astype(jnp.float32) + both[0].astype(jnp.float32)
        for by, at in ((1, 1), (-1, 3), (2, 2)):
            total = total + shift(both[at], "z", by).astype(jnp.float32)
        return swap(total.astype(jnp.bfloat16))

    high = sum_second(p_low, p_high, high)
    low = sum_second(tail, p_low, low)
    return jnp.concatenate([low, high], axis=0)


def solution(mesh):
    fine = Mesh(np.asarray(mesh.devices).reshape(2, 4, 2, 4, 2), AXES)
    ctx, ch = ("xl", "y", "core"), ("z", "xh")
    return jax.shard_map(
        per_device,
        mesh=fine,
        in_specs=(
            P(ctx, ch),
            P(),
            P(None, ctx, None, ch),
            P(None, None, None, ch),
            P(None, ch),
            P(None, ch),
            P(None, ch),
            P(None, ch, ctx),
        ),
        out_specs=P(ctx, ch),
        check_vma=False,
    )
```

```python
import functools

import jax
import jax.numpy as jnp
import numpy as np
from jax import lax
from jax.experimental.layout import Layout, with_layout_constraint
from jax.experimental import pallas as pl
from jax.experimental.pallas import tpu as pltpu
from jax.sharding import Mesh, PartitionSpec as P

AXES = ("xl", "y", "core", "z", "xh")
HALF = 256
LANES = 128
CUT = 1024


def shift(value, axis, by):
    size = lax.axis_size(axis)
    return lax.ppermute(value, axis, [(i, (i + by) % size) for i in range(size)])


def shift_y(value, by):
    return shift(value, "y", by)


def swap(value):
    moved = lax.ppermute(value, ("core", "xh"), [(1, 2), (2, 1)])
    same = lax.axis_index("core") == lax.axis_index("xh")
    return jnp.where(same, value, moved)


def from_behind(value, axes):
    return lax.ppermute(value, axes, [(i, i + 1) for i in range(15)])


def by_rows(value):
    return with_layout_constraint(value, Layout(major_to_minor=tuple(range(value.ndim))))


def after(value, *others):
    return lax.optimization_barrier((value, *others))[0]


def together(*values):
    return lax.optimization_barrier(values)


def fetch(moves, sources, target, index_ref, semaphores):
    copies = []
    for number, (source, lead, lane, width, slot, other, by_rows, *fixed) in enumerate(moves):
        block = fixed[0] * 256 if slot is None else pl.multiple_of(index_ref[slot] * 256, 256)
        ref = sources[source]
        if lead is not None:
            ref = ref.at[lead]
        if by_rows:
            piece = target.at[pl.ds(block, 256), other : other + width]
        else:
            piece = target.at[other : other + ref.shape[0], pl.ds(block, 256)]
        copies.append(pltpu.make_async_copy(ref.at[:, lane : lane + width], piece, semaphores.at[number]))
    return copies


def in_kernel(x_moves, moves, sources, parts, halo, index_ref, gain_ref, *refs):
    xs, refs = refs[:sources], refs[sources:]
    count = 1 + max(m[0] for m in moves)
    ws, refs = refs[:count], refs[count:]
    out_refs, refs = refs[:parts], refs[parts:]
    tail_ref, refs = (refs[0], refs[1:]) if halo else (None, refs)
    raw, normed, weights, squares, x_sems, w_sems = refs
    loads = []
    for j, (source, lead, _) in enumerate(x_moves):
        x = xs[source] if lead is None else xs[source].at[lead]
        loads.append(pltpu.make_async_copy(x, raw.at[j], x_sems.at[j]))
    for load in loads:
        load.start()
    copies = fetch(moves, ws, weights, index_ref, w_sems)
    for copy in copies:
        copy.start()
    squares[...] = jnp.zeros_like(squares)
    for j, load in enumerate(loads):
        load.wait()
        block = x_moves[j][2] if x_moves[j][1] is not None else index_ref[j]
        lanes = pl.ds(pl.multiple_of(block * 512, 512), 512)
        gain = gain_ref[pl.ds(block, 1), :]

        @pl.loop(0, parts * HALF // 64)
        def _(step):
            rows = pl.ds(pl.multiple_of(step * 64, 64), 64)
            x = raw[j, rows, :].astype(jnp.float32)
            normed[rows, lanes] = (x * gain).astype(jnp.bfloat16)
            q = x * x
            squares[rows, :] += (q[:, :128] + q[:, 128:256]) + (q[:, 256:384] + q[:, 384:])

    squares[:, :1] = lax.rsqrt(jnp.sum(squares[...], axis=1, keepdims=True) * (1.0 / 4096) + 1e-06)
    for copy in copies:
        copy.wait()

    @pl.loop(0, 6)
    def _(step):
        lanes = pl.ds(pl.multiple_of(step * 256, 256), 256)
        product = jnp.dot(normed[...], weights[:, lanes], preferred_element_type=jnp.float32)
        product = (product * squares[:, :1]).astype(jnp.bfloat16)
        for part, out_ref in enumerate(out_refs):
            out_ref[:, lanes] = product[part * HALF : (part + 1) * HALF]

    if halo:
        last = out_refs[-1]
        tail_ref[:halo, :] = last[HALF - halo :, 512:]
        tail_ref[halo:, :512] = last[HALF - 16 :, :512]
        tail_ref[halo:, 512:] = jnp.zeros((16, 512), jnp.bfloat16)


def project_in(index, gain, pieces, x_moves, weights, moves, parts, halo):
    any_space = pl.BlockSpec(memory_space=pl.ANY)
    vmem = pl.BlockSpec(memory_space=pltpu.VMEM)
    rows = parts * HALF
    shapes = [jax.ShapeDtypeStruct((HALF, 1536), jnp.bfloat16)] * parts
    if halo:
        shapes.append(jax.ShapeDtypeStruct((halo + 16, 1024), jnp.bfloat16))
    return pl.pallas_call(
        functools.partial(in_kernel, x_moves, moves, len(pieces), parts, halo),
        out_shape=shapes,
        in_specs=[pl.BlockSpec(memory_space=pltpu.SMEM), vmem] + [any_space] * (len(pieces) + len(weights)),
        out_specs=[vmem] * len(shapes),
        scratch_shapes=[
            pltpu.VMEM((8, rows, 512), jnp.bfloat16),
            pltpu.VMEM((rows, 4096), jnp.bfloat16),
            pltpu.VMEM((4096, 1536), jnp.bfloat16),
            pltpu.VMEM((rows, LANES), jnp.float32),
            pltpu.SemaphoreType.DMA((8,)),
            pltpu.SemaphoreType.DMA((len(moves),)),
        ],
        compiler_params=pltpu.CompilerParams(vmem_limit_bytes=56 * 1024 * 1024),
        cost_estimate=pl.CostEstimate(flops=2 * rows * 4096 * 1536, bytes_accessed=18 * 2**20, transcendentals=0),
    )(index, gain, *pieces, *weights)


def mix_kernel(moves, halo, taps, outs, index_ref, before_ref, main_ref, feat_ref, filter_ref, skip_ref, *refs):
    count = 1 + max(m[0] for m in moves)
    ws, refs = refs[:count], refs[count:]
    out_refs, refs = refs[:outs], refs[outs:]
    shaped, gated, copies8, inner, weights, w_sems = refs
    copies = fetch(moves, ws, weights, index_ref, w_sems)
    for copy in copies:
        copy.start()
    total = halo + HALF

    if before_ref.shape[1] == 1024:
        shaped[:16, :512] = before_ref[halo:, :512].astype(jnp.float32)
        shaped[:halo, 512:] = before_ref[:halo, :].astype(jnp.float32)
    else:
        shaped[:16, :512] = before_ref[HALF - 16 :, :512].astype(jnp.float32)
        shaped[:halo, 512:] = before_ref[HALF - halo :, 512:].astype(jnp.float32)
    shaped[16 : 16 + HALF, :512] = main_ref[:, :512].astype(jnp.float32)
    shaped[halo:total, 512:] = main_ref[:, 512:].astype(jnp.float32)

    def feature(start, size, s, lanes):
        value = None
        for j in range(3):
            tap = feat_ref[3 * j + s : 3 * j + s + 1, lanes]
            low = s * 512 + lanes.start
            term = tap * shaped[start - j : start - j + size, low : low + LANES]
            value = term if value is None else value + term
        return value

    for lane in range(0, 512, LANES):
        lanes = slice(lane, lane + LANES)
        for start in range(8, total, 64):
            size = min(64, total - start)
            gated[start : start + size, lanes] = feature(start, size, 1, lanes) * feature(start, size, 2, lanes)
        gated[:8, lanes] = jnp.zeros((8, LANES), jnp.float32)

    if taps == 7:
        for lane in range(0, 512, LANES):
            lanes = slice(lane, lane + LANES)
            for start in range(0, HALF, 64):
                own = gated[halo + start : halo + start + 64, lanes]
                value = (skip_ref[:1, lanes] + filter_ref[:1, lanes]) * own
                for j in range(1, taps):
                    value = value + filter_ref[j : j + 1, lanes] * gated[halo + start - j : halo + start - j + 64, lanes]
                inner[start : start + 64, lanes] = (feature(16 + start, 64, 0, lanes) * value).astype(jnp.bfloat16)
    else:
        for lane in range(0, 512, LANES):
            lanes = slice(lane, lane + LANES)
            for r in range(8):
                for start in range(0, HALF + 128, 128):
                    copies8[r, start : start + 128, :] = gated[16 + start - r : 16 + start - r + 128, lanes]

            @pl.loop(0, HALF // 128)
            def _(step):
                base = pl.multiple_of(step * 128, 128)
                value = jnp.zeros((128, LANES), jnp.float32)
                for r in range(8):
                    for a in range(0, 16, 4):
                        window = copies8[r, pl.ds(pl.multiple_of(base + 128 - 8 * (a + 3), 8), 128 + 24), :]
                        for b in range(4):
                            tap = filter_ref[8 * (a + b) + r : 8 * (a + b) + r + 1, lanes]
                            low = 8 * (3 - b)
                            value = value + tap * window[low : low + 128]
                copies8[8, pl.ds(base, 128), :] = value

            for start in range(0, HALF, 64):
                own = gated[halo + start : halo + start + 64, lanes]
                value = copies8[8, start : start + 64, :] + skip_ref[:1, lanes] * own
                inner[start : start + 64, lanes] = (feature(16 + start, 64, 0, lanes) * value).astype(jnp.bfloat16)

    for copy in copies:
        copy.wait()
    z = index_ref[0]
    core = index_ref[1]
    for by in range(4):
        block = lax.rem(z + by, 4)
        if outs == 4:
            columns = pl.ds(pl.multiple_of(block * 1024, 1024), 1024)
            out_refs[by][...] = jnp.dot(
                inner[...], weights[:, columns], preferred_element_type=jnp.float32
            ).astype(jnp.bfloat16)
        else:
            for side in range(2):
                place = block * 2 + (core if side == 0 else 1 - core)
                columns = pl.ds(pl.multiple_of(place * 512, 512), 512)
                out_refs[side][by] = jnp.dot(
                    inner[...], weights[:, columns], preferred_element_type=jnp.float32
                ).astype(jnp.bfloat16)


def mix_out(index, before, main, feat, taps, skip, weights, moves, halo, out_shapes):
    any_space = pl.BlockSpec(memory_space=pl.ANY)
    vmem = pl.BlockSpec(memory_space=pltpu.VMEM)
    length = taps.shape[0]
    small = length == 7
    return pl.pallas_call(
        functools.partial(mix_kernel, moves, halo, length, len(out_shapes)),
        out_shape=[jax.ShapeDtypeStruct(s, jnp.bfloat16) for s in out_shapes],
        in_specs=[pl.BlockSpec(memory_space=pltpu.SMEM)] + [vmem] * 5 + [any_space] * len(weights),
        out_specs=[vmem] * len(out_shapes),
        scratch_shapes=[
            pltpu.VMEM((halo + HALF + 16, 1536), jnp.float32),
            pltpu.VMEM((halo + HALF, 512), jnp.float32),
            pltpu.VMEM((9, 8, LANES) if small else (9, HALF + 128, LANES), jnp.float32),
            pltpu.VMEM((HALF, 512), jnp.bfloat16),
            pltpu.VMEM((512, 4096), jnp.bfloat16),
            pltpu.SemaphoreType.DMA((len(moves),)),
        ],
        compiler_params=pltpu.CompilerParams(vmem_limit_bytes=56 * 1024 * 1024),
        cost_estimate=pl.CostEstimate(
            flops=2 * HALF * 512 * 4096 * (1 if small else 4), bytes_accessed=6 * 2**20, transcendentals=0
        ),
    )(index, before, main, feat, taps, skip, *weights)


def per_device(hidden, norm_gain, in_weight, feat_filter, se_filter, mr_filter, skip_gain, out_weight):
    xl, y, core, z, xh = (lax.axis_index(a) for a in AXES)
    behind = lambda place, by: (place - by) % 4
    gains = norm_gain.reshape(2, 8, 512)
    ways = (1, -1, 2)
    other_core = lambda value: shift(value, "core", 1)

    whole = lax.all_gather(hidden, ("z", "xh"), axis=0, tiled=False)

    w = in_weight[0].reshape(256, 1536)
    o = out_weight[0]
    w_xl = shift(w, "xl", 1)
    w_xl, *w_y, w1, o_xl = together(
        w_xl, *[shift_y(w, by) for by in ways], swap(in_weight[1]), shift(after(o, w_xl), "xl", 1)
    )
    rest = shift(jnp.stack([v[:, CUT:] for v in w_y]), "xl", 1)
    most = [shift_y(w_xl[:, :CUT], by) for by in ways]
    rest, *more = together(rest, *most, *[other_core(after(v, most[0])) for v in (w, w_xl, *w_y)])
    most, first_far = more[:3], more[3:]
    w_list = [w, w_xl, *w_y, *first_far, rest, *most] + [other_core(v) for v in (rest, *most)]
    w_moves, slots = [], []

    def take(number, lead, at_xl, at_y, at_core, low, high):
        w_moves.append((number, lead, 0, high - low, len(slots), low, True))
        slots.append(at_xl * 8 + at_y * 2 + at_core)

    for number, c in ((0, core), (5, 1 - core)):
        take(number, None, xl, y, c, 0, 1536)
        take(number + 1, None, 1 - xl, y, c, 0, 1536)
        for e, by in enumerate(ways):
            take(number + 2 + e, None, xl, behind(y, by), c, 0, 1536)
    for number, c in ((10, core), (14, 1 - core)):
        for e, by in enumerate(ways):
            take(number, e, 1 - xl, behind(y, by), c, CUT, 1536)
            take(number + 1 + e, None, 1 - xl, behind(y, by), c, 0, CUT)
    w_index = jnp.stack(slots).astype(jnp.int32)

    w1 = by_rows(after(w1, rest, *most).reshape(256, 1536))
    w1 = by_rows(lax.all_gather(w1, ("xh", "xl", "y"), axis=0, tiled=False))

    x_moves = [(0, j, j) for j in range(8)]
    low, high, tail = project_in(w_index, gains[0], [whole], x_moves, w_list, w_moves, 2, 16)
    small = jnp.concatenate([feat_filter[1].reshape(9, 512), skip_gain[1:2], mr_filter], axis=0)
    o, o1, base, small = after((jnp.stack([o, o_xl]), out_weight[1], hidden, small), rest, *most)
    *o_y, o1 = [shift_y(o, by) for by in ways] + [swap(o1)]
    tail, low, high, *o_y = together(tail, low, high, *o_y)
    o_list = [o, *o_y]
    q_list = o_list + [other_core(v) for v in o_list]
    q_moves, slots = [], [z, core]
    for number, (c, by) in enumerate([(c, by) for c in (core, 1 - core) for by in (0, *ways)]):
        for e, at_xl in enumerate((xl, 1 - xl)):
            q_moves.append((number, e, 0, 256, len(slots), 0, False))
            slots.append(at_xl * 8 + behind(y, by) * 2 + c)
    q_index = jnp.stack(slots).astype(jnp.int32)
    tail = from_behind(tail, ("xl", "y", "core"))
    base, small = after((base, small), low)
    base, small = swap(base), swap(small)
    o1 = by_rows(lax.all_gather(o1, ("xh", "xl", "y"), axis=0, tiled=False))

    def first_parts(before, main):
        parts = mix_out(
            q_index, before, main, feat_filter[0].reshape(9, 512), se_filter, skip_gain[0:1], q_list, q_moves, 16,
            [(HALF, 1024)] * 4,
        )
        return parts[0], [shift(part, "z", by) for by, part in ((1, parts[1]), (-1, parts[3]), (2, parts[2]))]

    def over_z(own, received):
        total = own.astype(jnp.float32)
        for value in received:
            total = total + value.astype(jnp.float32)
        total = total.astype(jnp.bfloat16)
        pick = lambda c: jnp.where(c == 0, total[:, :512], total[:, 512:])
        mine, others = pick(core), pick(1 - core)
        return mine, [
            lax.ppermute(mine, ("core", "xh"), [(1, 0), (2, 3)]),
            lax.ppermute(others, ("core", "xh"), [(1, 2), (2, 1)]),
            lax.ppermute(others, ("core", "xh"), [(0, 2), (3, 1)]),
        ]

    def over_x(mine, received, rows):
        kept = jnp.where(core == xh, mine, jnp.zeros_like(mine))
        current = base[rows : rows + HALF].astype(jnp.float32) + kept.astype(jnp.float32)
        for value in received:
            current = current + value.astype(jnp.float32)
        return current.astype(jnp.bfloat16)

    own_high, high_z = first_parts(low, high)
    own_low, low_z = first_parts(tail, low)
    mine_high, high_x = over_z(own_high, high_z)
    *low_z, one, two, three = together(*low_z, *high_x)
    high = over_x(mine_high, (one, two, three), HALF)
    mine_low, low_x = over_z(own_low, low_z)
    high_near = [shift(high, "z", by) for by in ways]
    one, two, three, *high_near = together(*low_x, *high_near)
    low = over_x(mine_low, (one, two, three), 0)

    places = [(p, (p // 4 % 2) * 8 + (p % 4) * 2 + p // 8) for p in range(16)]
    w_moves = [(0, p, 0, 1536, None, 0, True, block) for p, block in places]
    q_moves = [(0, p, 0, 256, None, 0, False, block) for p, block in places]
    x_moves = [(j, None, j) for j in range(8)]
    x_index = jnp.stack([behind(z, by) * 2 + c for c in (core, 1 - core) for by in (0, *ways)]).astype(jnp.int32)

    def projected(near, halo):
        return project_in(x_index, gains[1], near + [other_core(v) for v in near], x_moves, [w1], w_moves, 1, halo)

    p_high, tail = projected([high] + high_near, 144)
    low_near = [shift(low, "z", by) for by in ways]
    p_high, tail, *low_near = together(p_high, tail, *low_near)
    tail = from_behind(tail, ("xl", "y", "xh"))
    (p_low,) = projected([low] + low_near, 0)
    place = jnp.stack([z, core]).astype(jnp.int32)

    def second_parts(before, main):
        return mix_out(
            place, before, main, small[:9], small[10:], small[9:10], [o1], q_moves, 144, [(4, HALF, 512)] * 2
        )

    def sum_second(own, theirs, rows):
        both = (own.astype(jnp.float32) + theirs.astype(jnp.float32)).astype(jnp.bfloat16)
        total = rows.astype(jnp.float32) + both[0].astype(jnp.float32)
        for by, at in ((1, 1), (-1, 3), (2, 2)):
            total = total + shift(both[at], "z", by).astype(jnp.float32)
        return swap(total.astype(jnp.bfloat16))

    own_high, theirs_high = second_parts(p_low, p_high)
    theirs_high = other_core(theirs_high)
    theirs_high, p_low = together(theirs_high, p_low)
    own_low, theirs_low = second_parts(tail, p_low)
    high = sum_second(own_high, theirs_high, high)
    low = sum_second(own_low, other_core(theirs_low), low)
    return jnp.concatenate([low, high], axis=0)


def solution(mesh):
    fine = Mesh(np.asarray(mesh.devices).reshape(2, 4, 2, 4, 2), AXES)
    ctx, ch = ("xl", "y", "core"), ("z", "xh")
    return jax.shard_map(
        per_device,
        mesh=fine,
        in_specs=(
            P(ctx, ch),
            P(),
            P(None, ctx, None, ch),
            P(None, None, None, ch),
            P(None, ch),
            P(None, ch),
            P(None, ch),
            P(None, ch, ctx),
        ),
        out_specs=P(ctx, ch),
        check_vma=False,
    )
```

```python
import functools

import jax
import jax.numpy as jnp
import numpy as np
from jax import lax
from jax.experimental.layout import Layout, with_layout_constraint
from jax.experimental import pallas as pl
from jax.experimental.pallas import tpu as pltpu
from jax.sharding import Mesh, PartitionSpec as P

AXES = ("xl", "y", "core", "z", "xh")
HALF = 256
LANES = 128


def shift(value, axis, by):
    size = lax.axis_size(axis)
    return lax.ppermute(value, axis, [(i, (i + by) % size) for i in range(size)])


def swap(value):
    moved = lax.ppermute(value, ("core", "xh"), [(1, 2), (2, 1)])
    same = lax.axis_index("core") == lax.axis_index("xh")
    return jnp.where(same, value, moved)


def from_behind(value, axes):
    return lax.ppermute(value, axes, [(i, i + 1) for i in range(15)])


def by_rows(value):
    return with_layout_constraint(value, Layout(major_to_minor=tuple(range(value.ndim))))


def after(value, *others):
    return lax.optimization_barrier((value, *others))[0]


def together(*values):
    return lax.optimization_barrier(values)


def fetch(moves, sources, target, index_ref, semaphores):
    copies = []
    for number, (source, lead, lane, width, slot, other, by_rows, *fixed) in enumerate(moves):
        block = fixed[0] * 256 if slot is None else pl.multiple_of(index_ref[slot] * 256, 256)
        ref = sources[source]
        if lead is not None:
            ref = ref.at[lead]
        if by_rows:
            piece = target.at[pl.ds(block, 256), other : other + width]
        else:
            piece = target.at[other : other + ref.shape[0], pl.ds(block, 256)]
        copies.append(pltpu.make_async_copy(ref.at[:, lane : lane + width], piece, semaphores.at[number]))
    return copies


def norm_pieces(loads, places, raw, gain_ref, normed, squares):
    squares[...] = jnp.zeros_like(squares)
    for j, load in enumerate(loads):
        load.wait()
        lanes = pl.ds(pl.multiple_of(places[j] * 512, 512), 512)
        gain = gain_ref[pl.ds(places[j], 1), :]

        @pl.loop(0, squares.shape[0] // 64)
        def _(step):
            rows = pl.ds(pl.multiple_of(step * 64, 64), 64)
            x = raw[j, rows, :].astype(jnp.float32)
            normed[rows, lanes] = (x * gain).astype(jnp.bfloat16)
            q = x * x
            squares[rows, :] += (q[:, :128] + q[:, 128:256]) + (q[:, 256:384] + q[:, 384:])

    squares[:, :1] = lax.rsqrt(jnp.sum(squares[...], axis=1, keepdims=True) * (1.0 / 4096) + 1e-06)


def norm_kernel(index_ref, gain_ref, *refs):
    xs, (normed, squares, raw, x_sems) = refs[:8], refs[8:]
    loads = [pltpu.make_async_copy(x, raw.at[j], x_sems.at[j]) for j, x in enumerate(xs)]
    for load in loads:
        load.start()
    norm_pieces(loads, [index_ref[j] for j in range(8)], raw, gain_ref, normed, squares)


def norm_rows(index, gain, pieces):
    rows = pieces[0].shape[0]
    any_space = pl.BlockSpec(memory_space=pl.ANY)
    vmem = pl.BlockSpec(memory_space=pltpu.VMEM)
    return pl.pallas_call(
        norm_kernel,
        out_shape=[
            jax.ShapeDtypeStruct((rows, 4096), jnp.bfloat16),
            jax.ShapeDtypeStruct((rows, LANES), jnp.float32),
        ],
        in_specs=[pl.BlockSpec(memory_space=pltpu.SMEM), vmem] + [any_space] * 8,
        out_specs=[vmem, vmem],
        scratch_shapes=[pltpu.VMEM((8, rows, 512), jnp.bfloat16), pltpu.SemaphoreType.DMA((8,))],
        compiler_params=pltpu.CompilerParams(vmem_limit_bytes=24 * 1024 * 1024),
        cost_estimate=pl.CostEstimate(flops=rows * 4096 * 4, bytes_accessed=rows * 4096 * 4, transcendentals=0),
    )(index, gain, *pieces)


def multiply(normed, weights, squares, out_refs, tail_ref, halo):
    @pl.loop(0, 6)
    def _(step):
        lanes = pl.ds(pl.multiple_of(step * 256, 256), 256)
        product = jnp.dot(normed[...], weights[:, lanes], preferred_element_type=jnp.float32)
        product = (product * squares[:, :1]).astype(jnp.bfloat16)
        for part, out_ref in enumerate(out_refs):
            out_ref[:, lanes] = product[part * HALF : (part + 1) * HALF]

    if halo:
        last = out_refs[-1]
        tail_ref[:halo, :] = last[HALF - halo :, 512:]
        tail_ref[halo:, :512] = last[HALF - 16 :, :512]
        tail_ref[halo:, 512:] = jnp.zeros((16, 512), jnp.bfloat16)


def in_kernel(moves, sources, parts, halo, index_ref, *refs):
    ins, refs = refs[: sources + 1], refs[sources + 1 :]
    w_ref, refs = refs[0], refs[1:]
    out_refs, refs = refs[:parts], refs[parts:]
    tail_ref, refs = (refs[0], refs[1:]) if halo else (None, refs)
    weights, w_sems, *refs = refs
    copies = fetch(moves, [w_ref], weights, index_ref, w_sems)
    if sources == 8:
        raw, normed, squares, x_sems = refs
        loads = [pltpu.make_async_copy(x, raw.at[j], x_sems.at[j]) for j, x in enumerate(ins[1:])]
        for copy in loads + copies:
            copy.start()
        norm_pieces(loads, [index_ref[j] for j in range(8)], raw, ins[0], normed, squares)
    else:
        normed, squares = ins
        for copy in copies:
            copy.start()
    for copy in copies:
        copy.wait()
    multiply(normed, weights, squares, out_refs, tail_ref, halo)


def project_in(index, pieces, weight, moves, parts, halo):
    any_space = pl.BlockSpec(memory_space=pl.ANY)
    vmem = pl.BlockSpec(memory_space=pltpu.VMEM)
    rows = parts * HALF
    shapes = [jax.ShapeDtypeStruct((HALF, 1536), jnp.bfloat16)] * parts
    if halo:
        shapes.append(jax.ShapeDtypeStruct((halo + 16, 1024), jnp.bfloat16))
    scratch = [pltpu.VMEM((4096, 1536), jnp.bfloat16), pltpu.SemaphoreType.DMA((len(moves),))]
    specs = [vmem, vmem]
    if len(pieces) == 9:
        scratch += [
            pltpu.VMEM((8, rows, 512), jnp.bfloat16),
            pltpu.VMEM((rows, 4096), jnp.bfloat16),
            pltpu.VMEM((rows, LANES), jnp.float32),
            pltpu.SemaphoreType.DMA((8,)),
        ]
        specs = [vmem] + [any_space] * 8
    return pl.pallas_call(
        functools.partial(in_kernel, moves, len(pieces) - 1, parts, halo),
        out_shape=shapes,
        in_specs=[pl.BlockSpec(memory_space=pltpu.SMEM)] + specs + [any_space],
        out_specs=[vmem] * len(shapes),
        scratch_shapes=scratch,
        compiler_params=pltpu.CompilerParams(vmem_limit_bytes=32 * 1024 * 1024),
        cost_estimate=pl.CostEstimate(flops=2 * rows * 4096 * 1536, bytes_accessed=18 * 2**20, transcendentals=0),
    )(index, *pieces, weight)


def mix_kernel(moves, halo, taps, outs, index_ref, before_ref, main_ref, feat_ref, filter_ref, skip_ref, *refs):
    count = 1 + max(m[0] for m in moves)
    ws, refs = refs[:count], refs[count:]
    out_refs, refs = refs[:outs], refs[outs:]
    shaped, gated, copies8, inner, weights, w_sems = refs
    copies = fetch(moves, ws, weights, index_ref, w_sems)
    for copy in copies:
        copy.start()
    total = halo + HALF

    if before_ref.shape[1] == 1024:
        shaped[:16, :512] = before_ref[halo:, :512].astype(jnp.float32)
        shaped[:halo, 512:] = before_ref[:halo, :].astype(jnp.float32)
    else:
        shaped[:16, :512] = before_ref[HALF - 16 :, :512].astype(jnp.float32)
        shaped[:halo, 512:] = before_ref[HALF - halo :, 512:].astype(jnp.float32)
    shaped[16 : 16 + HALF, :512] = main_ref[:, :512].astype(jnp.float32)
    shaped[halo:total, 512:] = main_ref[:, 512:].astype(jnp.float32)

    def feature(start, size, s, lanes):
        value = None
        for j in range(3):
            tap = feat_ref[3 * j + s : 3 * j + s + 1, lanes]
            low = s * 512 + lanes.start
            term = tap * shaped[start - j : start - j + size, low : low + LANES]
            value = term if value is None else value + term
        return value

    for lane in range(0, 512, LANES):
        lanes = slice(lane, lane + LANES)
        for start in range(8, total, 64):
            size = min(64, total - start)
            gated[start : start + size, lanes] = feature(start, size, 1, lanes) * feature(start, size, 2, lanes)
        gated[:8, lanes] = jnp.zeros((8, LANES), jnp.float32)

    if taps == 7:
        for lane in range(0, 512, LANES):
            lanes = slice(lane, lane + LANES)
            for start in range(0, HALF, 64):
                own = gated[halo + start : halo + start + 64, lanes]
                value = (skip_ref[:1, lanes] + filter_ref[:1, lanes]) * own
                for j in range(1, taps):
                    value = value + filter_ref[j : j + 1, lanes] * gated[halo + start - j : halo + start - j + 64, lanes]
                inner[start : start + 64, lanes] = (feature(16 + start, 64, 0, lanes) * value).astype(jnp.bfloat16)
    else:
        for lane in range(0, 512, LANES):
            lanes = slice(lane, lane + LANES)
            for r in range(8):
                for start in range(0, HALF + 128, 128):
                    copies8[r, start : start + 128, :] = gated[16 + start - r : 16 + start - r + 128, lanes]

            @pl.loop(0, HALF // 128)
            def _(step):
                base = pl.multiple_of(step * 128, 128)
                value = jnp.zeros((128, LANES), jnp.float32)
                for r in range(8):
                    for a in range(0, 16, 4):
                        window = copies8[r, pl.ds(pl.multiple_of(base + 128 - 8 * (a + 3), 8), 128 + 24), :]
                        for b in range(4):
                            tap = filter_ref[8 * (a + b) + r : 8 * (a + b) + r + 1, lanes]
                            low = 8 * (3 - b)
                            value = value + tap * window[low : low + 128]
                copies8[8, pl.ds(base, 128), :] = value

            for start in range(0, HALF, 64):
                own = gated[halo + start : halo + start + 64, lanes]
                value = copies8[8, start : start + 64, :] + skip_ref[:1, lanes] * own
                inner[start : start + 64, lanes] = (feature(16 + start, 64, 0, lanes) * value).astype(jnp.bfloat16)

    for copy in copies:
        copy.wait()
    z = index_ref[0]
    core = index_ref[1]
    for by in range(4):
        block = lax.rem(z + by, 4)
        if outs == 4:
            columns = pl.ds(pl.multiple_of(block * 1024, 1024), 1024)
            out_refs[by][...] = jnp.dot(
                inner[...], weights[:, columns], preferred_element_type=jnp.float32
            ).astype(jnp.bfloat16)
        else:
            for side in range(2):
                place = block * 2 + (core if side == 0 else 1 - core)
                columns = pl.ds(pl.multiple_of(place * 512, 512), 512)
                out_refs[side][by] = jnp.dot(
                    inner[...], weights[:, columns], preferred_element_type=jnp.float32
                ).astype(jnp.bfloat16)


def mix_out(index, before, main, feat, taps, skip, weights, moves, halo, out_shapes):
    any_space = pl.BlockSpec(memory_space=pl.ANY)
    vmem = pl.BlockSpec(memory_space=pltpu.VMEM)
    length = taps.shape[0]
    small = length == 7
    return pl.pallas_call(
        functools.partial(mix_kernel, moves, halo, length, len(out_shapes)),
        out_shape=[jax.ShapeDtypeStruct(s, jnp.bfloat16) for s in out_shapes],
        in_specs=[pl.BlockSpec(memory_space=pltpu.SMEM)] + [vmem] * 5 + [any_space] * len(weights),
        out_specs=[vmem] * len(out_shapes),
        scratch_shapes=[
            pltpu.VMEM((halo + HALF + 16, 1536), jnp.float32),
            pltpu.VMEM((halo + HALF, 512), jnp.float32),
            pltpu.VMEM((9, 8, LANES) if small else (9, HALF + 128, LANES), jnp.float32),
            pltpu.VMEM((HALF, 512), jnp.bfloat16),
            pltpu.VMEM((512, 4096), jnp.bfloat16),
            pltpu.SemaphoreType.DMA((len(moves),)),
        ],
        compiler_params=pltpu.CompilerParams(vmem_limit_bytes=24 * 1024 * 1024),
        cost_estimate=pl.CostEstimate(
            flops=2 * HALF * 512 * 4096 * (1 if small else 4), bytes_accessed=6 * 2**20, transcendentals=0
        ),
    )(index, before, main, feat, taps, skip, *weights)


def per_device(hidden, norm_gain, in_weight, feat_filter, se_filter, mr_filter, skip_gain, out_weight):
    xl, y, core, z, xh = (lax.axis_index(a) for a in AXES)
    behind = lambda place, by: (place - by) % 4
    gains = norm_gain.reshape(2, 8, 512)
    ways = (1, -1, 2)
    other_core = lambda value: shift(value, "core", 1)
    gather = lambda value, axes: by_rows(lax.all_gather(by_rows(value), axes, axis=0, tiled=False))

    w0 = jnp.concatenate([in_weight[0].reshape(256, 1536), out_weight[0, :256], out_weight[0, 256:]], axis=1)
    w0 = gather(w0, ("xl", "y", "core"))
    w_moves = [(0, p, 0, 1536, None, 0, True, p) for p in range(16)]
    q_moves = [(0, p, 1536 + 256 * half, 256, None, 256 * half, False, p) for p in range(16) for half in range(2)]

    partner = shift(hidden, "xh", 1)
    x_pieces = [hidden] + [shift(hidden, "z", by) for by in ways]
    x_pieces += [partner] + [shift(partner, "z", by) for by in ways]
    x_index = jnp.stack([behind(z, by) * 2 + c for c in (xh, 1 - xh) for by in (0, *ways)]).astype(jnp.int32)

    w1 = swap(after(in_weight[1], partner))
    small = jnp.concatenate([feat_filter[1].reshape(9, 512), skip_gain[1:2], mr_filter], axis=0)
    o1, base, small = after((out_weight[1], hidden, small), *x_pieces)
    o1, base, small = swap(o1), swap(base), swap(small)
    w1 = gather(after(w1, *x_pieces).reshape(256, 1536), ("xh", "xl", "y"))
    o1 = gather(o1, ("xh", "xl", "y"))

    pieces = norm_rows(x_index, gains[0], x_pieces)
    low, high, tail = project_in(x_index, pieces, w0, w_moves, 2, 16)
    tail = from_behind(tail, ("xl", "y", "core"))
    q_index = jnp.stack([z, core]).astype(jnp.int32)
    q_list = [w0]

    def first_parts(before, main):
        parts = mix_out(
            q_index, before, main, feat_filter[0].reshape(9, 512), se_filter, skip_gain[0:1], q_list, q_moves, 16,
            [(HALF, 1024)] * 4,
        )
        return parts[0], [shift(part, "z", by) for by, part in ((1, parts[1]), (-1, parts[3]), (2, parts[2]))]

    def over_z(own, received):
        total = own.astype(jnp.float32)
        for value in received:
            total = total + value.astype(jnp.float32)
        total = total.astype(jnp.bfloat16)
        pick = lambda c: jnp.where(c == 0, total[:, :512], total[:, 512:])
        mine, others = pick(core), pick(1 - core)
        return mine, [
            lax.ppermute(mine, ("core", "xh"), [(1, 0), (2, 3)]),
            lax.ppermute(others, ("core", "xh"), [(1, 2), (2, 1)]),
            lax.ppermute(others, ("core", "xh"), [(0, 2), (3, 1)]),
        ]

    def over_x(mine, received, rows):
        kept = jnp.where(core == xh, mine, jnp.zeros_like(mine))
        current = base[rows : rows + HALF].astype(jnp.float32) + kept.astype(jnp.float32)
        for value in received:
            current = current + value.astype(jnp.float32)
        return current.astype(jnp.bfloat16)

    own_high, high_z = first_parts(low, high)
    own_low, low_z = first_parts(tail, low)
    mine_high, high_x = over_z(own_high, high_z)
    *low_z, one, two, three = together(*low_z, *high_x)
    high = over_x(mine_high, (one, two, three), HALF)
    mine_low, low_x = over_z(own_low, low_z)
    high_near = [shift(high, "z", by) for by in ways]
    one, two, three, *high_near = together(*low_x, *high_near)
    low = over_x(mine_low, (one, two, three), 0)

    places = [(p, (p // 4 % 2) * 8 + (p % 4) * 2 + p // 8) for p in range(16)]
    w_moves = [(0, p, 0, 1536, None, 0, True, block) for p, block in places]
    q_moves = [(0, p, 0, 256, None, 0, False, block) for p, block in places]
    x_index = jnp.stack([behind(z, by) * 2 + c for c in (core, 1 - core) for by in (0, *ways)]).astype(jnp.int32)

    def projected(near, halo):
        return project_in(x_index, [gains[1], *near, *[other_core(v) for v in near]], w1, w_moves, 1, halo)

    p_high, tail = projected([high] + high_near, 144)
    low_near = [shift(low, "z", by) for by in ways]
    p_high, tail, *low_near = together(p_high, tail, *low_near)
    tail = from_behind(tail, ("xl", "y", "xh"))
    (p_low,) = projected([low] + low_near, 0)
    tail, p_low = together(tail, p_low)

    def second_parts(before, main):
        return mix_out(
            q_index, before, main, small[:9], small[10:], small[9:10], [o1], q_moves, 144, [(4, HALF, 512)] * 2
        )

    def second_z(own, theirs):
        both = (own.astype(jnp.float32) + theirs.astype(jnp.float32)).astype(jnp.bfloat16)
        return both[0], [shift(both[at], "z", by) for by, at in ((1, 1), (-1, 3), (2, 2))]

    def second_sum(own, received, rows):
        total = rows.astype(jnp.float32) + own.astype(jnp.float32)
        for value in received:
            total = total + value.astype(jnp.float32)
        return swap(total.astype(jnp.bfloat16))

    own_high, theirs_high = second_parts(p_low, p_high)
    theirs_high = other_core(theirs_high)
    theirs_high, p_low = together(theirs_high, p_low)
    own_high, high_z = second_z(own_high, theirs_high)
    own_low, theirs_low = second_parts(tail, p_low)
    own_low, theirs_low, *high_z = together(own_low, theirs_low, *high_z)
    high = second_sum(own_high, high_z, high)
    own_low, low_z = second_z(own_low, other_core(theirs_low))
    low = second_sum(own_low, low_z, low)
    return jnp.concatenate([low, high], axis=0)


def solution(mesh):
    fine = Mesh(np.asarray(mesh.devices).reshape(2, 4, 2, 4, 2), AXES)
    ctx, ch = ("xl", "y", "core"), ("z", "xh")
    return jax.shard_map(
        per_device,
        mesh=fine,
        in_specs=(
            P(ctx, ch),
            P(),
            P(None, ctx, None, ch),
            P(None, None, None, ch),
            P(None, ch),
            P(None, ch),
            P(None, ch),
            P(None, ch, ctx),
        ),
        out_specs=P(ctx, ch),
        check_vma=False,
    )
```

```python
import functools

import jax
import jax.numpy as jnp
import numpy as np
from jax import lax
from jax.experimental.layout import Layout, with_layout_constraint
from jax.experimental import pallas as pl
from jax.experimental.pallas import tpu as pltpu
from jax.sharding import Mesh, PartitionSpec as P

AXES = ("xl", "y", "core", "z", "xh")
HALF = 256
LANES = 128


def shift(value, axis, by):
    size = lax.axis_size(axis)
    return lax.ppermute(value, axis, [(i, (i + by) % size) for i in range(size)])


def swap(value):
    moved = lax.ppermute(value, ("core", "xh"), [(1, 2), (2, 1)])
    same = lax.axis_index("core") == lax.axis_index("xh")
    return jnp.where(same, value, moved)


def from_behind(value, axes):
    return lax.ppermute(value, axes, [(i, i + 1) for i in range(15)])


def by_rows(value):
    return with_layout_constraint(value, Layout(major_to_minor=tuple(range(value.ndim))))


def after(value, *others):
    return lax.optimization_barrier((value, *others))[0]


def together(*values):
    return lax.optimization_barrier(values)


def fetch(moves, sources, target, index_ref, semaphores):
    copies = []
    for number, (source, lead, lane, width, slot, other, by_rows, *fixed) in enumerate(moves):
        block = fixed[0] * 256 if slot is None else pl.multiple_of(index_ref[slot] * 256, 256)
        ref = sources[source]
        if lead is not None:
            ref = ref.at[lead]
        if by_rows:
            piece = target.at[pl.ds(block, 256), other : other + width]
        else:
            piece = target.at[other : other + ref.shape[0], pl.ds(block, 256)]
        copies.append(pltpu.make_async_copy(ref.at[:, lane : lane + width], piece, semaphores.at[number]))
    return copies


def norm_pieces(loads, places, raw, gain_ref, normed, squares):
    squares[...] = jnp.zeros_like(squares)
    for j, load in enumerate(loads):
        load.wait()
        lanes = pl.ds(pl.multiple_of(places[j] * 512, 512), 512)
        gain = gain_ref[pl.ds(places[j], 1), :]

        @pl.loop(0, squares.shape[0] // 64)
        def _(step):
            rows = pl.ds(pl.multiple_of(step * 64, 64), 64)
            x = raw[j, rows, :].astype(jnp.float32)
            normed[rows, lanes] = (x * gain).astype(jnp.bfloat16)
            q = x * x
            squares[rows, :] += (q[:, :128] + q[:, 128:256]) + (q[:, 256:384] + q[:, 384:])

    squares[:, :1] = lax.rsqrt(jnp.sum(squares[...], axis=1, keepdims=True) * (1.0 / 4096) + 1e-06)


def norm_kernel(index_ref, gain_ref, *refs):
    xs, (normed, squares, raw, x_sems) = refs[:8], refs[8:]
    loads = [pltpu.make_async_copy(x, raw.at[j], x_sems.at[j]) for j, x in enumerate(xs)]
    for load in loads:
        load.start()
    norm_pieces(loads, [index_ref[j] for j in range(8)], raw, gain_ref, normed, squares)


def norm_rows(index, gain, pieces):
    rows = pieces[0].shape[0]
    any_space = pl.BlockSpec(memory_space=pl.ANY)
    vmem = pl.BlockSpec(memory_space=pltpu.VMEM)
    return pl.pallas_call(
        norm_kernel,
        out_shape=[
            jax.ShapeDtypeStruct((rows, 4096), jnp.bfloat16),
            jax.ShapeDtypeStruct((rows, LANES), jnp.float32),
        ],
        in_specs=[pl.BlockSpec(memory_space=pltpu.SMEM), vmem] + [any_space] * 8,
        out_specs=[vmem, vmem],
        scratch_shapes=[pltpu.VMEM((8, rows, 512), jnp.bfloat16), pltpu.SemaphoreType.DMA((8,))],
        compiler_params=pltpu.CompilerParams(vmem_limit_bytes=24 * 1024 * 1024),
        cost_estimate=pl.CostEstimate(flops=rows * 4096 * 4, bytes_accessed=rows * 4096 * 4, transcendentals=0),
    )(index, gain, *pieces)


def multiply(normed, weights, squares, out_refs, tail_ref, halo):
    @pl.loop(0, 6)
    def _(step):
        lanes = pl.ds(pl.multiple_of(step * 256, 256), 256)
        product = jnp.dot(normed[...], weights[:, lanes], preferred_element_type=jnp.float32)
        product = (product * squares[:, :1]).astype(jnp.bfloat16)
        for part, out_ref in enumerate(out_refs):
            out_ref[:, lanes] = product[part * HALF : (part + 1) * HALF]

    if halo:
        last = out_refs[-1]
        tail_ref[:halo, :] = last[HALF - halo :, 512:]
        tail_ref[halo:, :512] = last[HALF - 16 :, :512]
        tail_ref[halo:, 512:] = jnp.zeros((16, 512), jnp.bfloat16)


def in_kernel(moves, sources, parts, halo, index_ref, *refs):
    ins, refs = refs[: sources + 1], refs[sources + 1 :]
    w_ref, refs = refs[0], refs[1:]
    out_refs, refs = refs[:parts], refs[parts:]
    tail_ref, refs = (refs[0], refs[1:]) if halo else (None, refs)
    weights, w_sems, *refs = refs
    copies = fetch(moves, [w_ref], weights, index_ref, w_sems)
    if sources == 8:
        raw, normed, squares, x_sems = refs
        loads = [pltpu.make_async_copy(x, raw.at[j], x_sems.at[j]) for j, x in enumerate(ins[1:])]
        for copy in loads + copies:
            copy.start()
        norm_pieces(loads, [index_ref[j] for j in range(8)], raw, ins[0], normed, squares)
    else:
        normed, squares = ins
        for copy in copies:
            copy.start()
    for copy in copies:
        copy.wait()
    multiply(normed, weights, squares, out_refs, tail_ref, halo)


def project_in(index, pieces, weight, moves, parts, halo):
    any_space = pl.BlockSpec(memory_space=pl.ANY)
    vmem = pl.BlockSpec(memory_space=pltpu.VMEM)
    rows = parts * HALF
    shapes = [jax.ShapeDtypeStruct((HALF, 1536), jnp.bfloat16)] * parts
    if halo:
        shapes.append(jax.ShapeDtypeStruct((halo + 16, 1024), jnp.bfloat16))
    scratch = [pltpu.VMEM((4096, 1536), jnp.bfloat16), pltpu.SemaphoreType.DMA((len(moves),))]
    specs = [vmem, vmem]
    if len(pieces) == 9:
        scratch += [
            pltpu.VMEM((8, rows, 512), jnp.bfloat16),
            pltpu.VMEM((rows, 4096), jnp.bfloat16),
            pltpu.VMEM((rows, LANES), jnp.float32),
            pltpu.SemaphoreType.DMA((8,)),
        ]
        specs = [vmem] + [any_space] * 8
    return pl.pallas_call(
        functools.partial(in_kernel, moves, len(pieces) - 1, parts, halo),
        out_shape=shapes,
        in_specs=[pl.BlockSpec(memory_space=pltpu.SMEM)] + specs + [any_space],
        out_specs=[vmem] * len(shapes),
        scratch_shapes=scratch,
        compiler_params=pltpu.CompilerParams(vmem_limit_bytes=52 * 1024 * 1024),
        cost_estimate=pl.CostEstimate(flops=2 * rows * 4096 * 1536, bytes_accessed=18 * 2**20, transcendentals=0),
    )(index, *pieces, weight)


def filter_rows(halo, taps, before_ref, main_ref, feat_ref, filter_ref, skip_ref, inner, shaped, gated, copies8):
    total = halo + HALF

    if before_ref.shape[1] == 1024:
        shaped[:16, :512] = before_ref[halo:, :512].astype(jnp.float32)
        shaped[:halo, 512:] = before_ref[:halo, :].astype(jnp.float32)
    else:
        shaped[:16, :512] = before_ref[HALF - 16 :, :512].astype(jnp.float32)
        shaped[:halo, 512:] = before_ref[HALF - halo :, 512:].astype(jnp.float32)
    shaped[16 : 16 + HALF, :512] = main_ref[:, :512].astype(jnp.float32)
    shaped[halo:total, 512:] = main_ref[:, 512:].astype(jnp.float32)

    def feature(start, size, s, lanes):
        value = None
        for j in range(3):
            tap = feat_ref[3 * j + s : 3 * j + s + 1, lanes]
            low = s * 512 + lanes.start
            term = tap * shaped[start - j : start - j + size, low : low + LANES]
            value = term if value is None else value + term
        return value

    for lane in range(0, 512, LANES):
        lanes = slice(lane, lane + LANES)
        for start in range(8, total, 64):
            size = min(64, total - start)
            gated[start : start + size, lanes] = feature(start, size, 1, lanes) * feature(start, size, 2, lanes)
        gated[:8, lanes] = jnp.zeros((8, LANES), jnp.float32)

    if taps == 7:
        for lane in range(0, 512, LANES):
            lanes = slice(lane, lane + LANES)
            for start in range(0, HALF, 64):
                own = gated[halo + start : halo + start + 64, lanes]
                value = (skip_ref[:1, lanes] + filter_ref[:1, lanes]) * own
                for j in range(1, taps):
                    value = value + filter_ref[j : j + 1, lanes] * gated[halo + start - j : halo + start - j + 64, lanes]
                inner[start : start + 64, lanes] = (feature(16 + start, 64, 0, lanes) * value).astype(jnp.bfloat16)
    else:
        for lane in range(0, 512, LANES):
            lanes = slice(lane, lane + LANES)
            for r in range(8):
                for start in range(0, HALF + 128, 128):
                    copies8[r, start : start + 128, :] = gated[16 + start - r : 16 + start - r + 128, lanes]

            @pl.loop(0, HALF // 128)
            def _(step):
                base = pl.multiple_of(step * 128, 128)
                value = jnp.zeros((128, LANES), jnp.float32)
                for r in range(8):
                    for a in range(0, 16, 4):
                        window = copies8[r, pl.ds(pl.multiple_of(base + 128 - 8 * (a + 3), 8), 128 + 24), :]
                        for b in range(4):
                            tap = filter_ref[8 * (a + b) + r : 8 * (a + b) + r + 1, lanes]
                            low = 8 * (3 - b)
                            value = value + tap * window[low : low + 128]
                copies8[8, pl.ds(base, 128), :] = value

            for start in range(0, HALF, 64):
                own = gated[halo + start : halo + start + 64, lanes]
                value = copies8[8, start : start + 64, :] + skip_ref[:1, lanes] * own
                inner[start : start + 64, lanes] = (feature(16 + start, 64, 0, lanes) * value).astype(jnp.bfloat16)


def product_rows(outs, index_ref, inner, weights, out_refs):
    z = index_ref[0]
    core = index_ref[1]
    for by in range(4):
        block = lax.rem(z + by, 4)
        if outs == 4:
            columns = pl.ds(pl.multiple_of(block * 1024, 1024), 1024)
            out_refs[by][...] = jnp.dot(
                inner[...], weights[:, columns], preferred_element_type=jnp.float32
            ).astype(jnp.bfloat16)
        else:
            for side in range(2):
                place = block * 2 + (core if side == 0 else 1 - core)
                columns = pl.ds(pl.multiple_of(place * 512, 512), 512)
                out_refs[side][by] = jnp.dot(
                    inner[...], weights[:, columns], preferred_element_type=jnp.float32
                ).astype(jnp.bfloat16)


def filter_scratch(halo, taps):
    return [
        pltpu.VMEM((halo + HALF + 16, 1536), jnp.float32),
        pltpu.VMEM((halo + HALF, 512), jnp.float32),
        pltpu.VMEM((9, 8, LANES) if taps == 7 else (9, HALF + 128, LANES), jnp.float32),
    ]


def mix_kernel(moves, halo, taps, outs, index_ref, before_ref, main_ref, feat_ref, filter_ref, skip_ref, *refs):
    count = 1 + max(m[0] for m in moves)
    ws, refs = refs[:count], refs[count:]
    out_refs, refs = refs[:outs], refs[outs:]
    shaped, gated, copies8, inner, weights, w_sems = refs
    copies = fetch(moves, ws, weights, index_ref, w_sems)
    for copy in copies:
        copy.start()
    filter_rows(halo, taps, before_ref, main_ref, feat_ref, filter_ref, skip_ref, inner, shaped, gated, copies8)
    for copy in copies:
        copy.wait()
    product_rows(outs, index_ref, inner, weights, out_refs)


def mix_out(index, before, main, feat, taps, skip, weights, moves, halo, out_shapes):
    any_space = pl.BlockSpec(memory_space=pl.ANY)
    vmem = pl.BlockSpec(memory_space=pltpu.VMEM)
    length = taps.shape[0]
    return pl.pallas_call(
        functools.partial(mix_kernel, moves, halo, length, len(out_shapes)),
        out_shape=[jax.ShapeDtypeStruct(s, jnp.bfloat16) for s in out_shapes],
        in_specs=[pl.BlockSpec(memory_space=pltpu.SMEM)] + [vmem] * 5 + [any_space] * len(weights),
        out_specs=[vmem] * len(out_shapes),
        scratch_shapes=filter_scratch(halo, length)
        + [
            pltpu.VMEM((HALF, 512), jnp.bfloat16),
            pltpu.VMEM((512, 4096), jnp.bfloat16),
            pltpu.SemaphoreType.DMA((len(moves),)),
        ],
        compiler_params=pltpu.CompilerParams(vmem_limit_bytes=40 * 1024 * 1024),
        cost_estimate=pl.CostEstimate(flops=2 * HALF * 512 * 4096, bytes_accessed=6 * 2**20, transcendentals=0),
    )(index, before, main, feat, taps, skip, *weights)


def filter_kernel(halo, taps, before_ref, main_ref, feat_ref, filter_ref, skip_ref, inner, shaped, gated, copies8):
    filter_rows(halo, taps, before_ref, main_ref, feat_ref, filter_ref, skip_ref, inner, shaped, gated, copies8)


def filtered(before, main, feat, taps, skip, halo):
    vmem = pl.BlockSpec(memory_space=pltpu.VMEM)
    length = taps.shape[0]
    return pl.pallas_call(
        functools.partial(filter_kernel, halo, length),
        out_shape=jax.ShapeDtypeStruct((HALF, 512), jnp.bfloat16),
        in_specs=[vmem] * 5,
        out_specs=vmem,
        scratch_shapes=filter_scratch(halo, length),
        compiler_params=pltpu.CompilerParams(vmem_limit_bytes=24 * 1024 * 1024),
        cost_estimate=pl.CostEstimate(flops=2 * HALF * 512 * 4096 * 3, bytes_accessed=3 * 2**20, transcendentals=0),
    )(before, main, feat, taps, skip)


def product_kernel(moves, outs, index_ref, inner, weight_ref, *refs):
    out_refs, (weights, w_sems) = refs[:outs], refs[outs:]
    copies = fetch(moves, [weight_ref], weights, index_ref, w_sems)
    for copy in copies:
        copy.start()
    for copy in copies:
        copy.wait()
    product_rows(outs, index_ref, inner, weights, out_refs)


def project_out(index, inner, weight, moves, out_shapes):
    vmem = pl.BlockSpec(memory_space=pltpu.VMEM)
    return pl.pallas_call(
        functools.partial(product_kernel, moves, len(out_shapes)),
        out_shape=[jax.ShapeDtypeStruct(s, jnp.bfloat16) for s in out_shapes],
        in_specs=[pl.BlockSpec(memory_space=pltpu.SMEM), vmem, pl.BlockSpec(memory_space=pl.ANY)],
        out_specs=[vmem] * len(out_shapes),
        scratch_shapes=[pltpu.VMEM((512, 4096), jnp.bfloat16), pltpu.SemaphoreType.DMA((len(moves),))],
        compiler_params=pltpu.CompilerParams(vmem_limit_bytes=40 * 1024 * 1024),
        cost_estimate=pl.CostEstimate(flops=2 * HALF * 512 * 4096, bytes_accessed=6 * 2**20, transcendentals=0),
    )(index, inner, weight)


def per_device(hidden, norm_gain, in_weight, feat_filter, se_filter, mr_filter, skip_gain, out_weight):
    xl, y, core, z, xh = (lax.axis_index(a) for a in AXES)
    behind = lambda place, by: (place - by) % 4
    gains = norm_gain.reshape(2, 8, 512)
    ways = (1, -1, 2)
    other_core = lambda value: shift(value, "core", 1)
    gather = lambda value, axes: by_rows(lax.all_gather(by_rows(value), axes, axis=0, tiled=False))

    w0 = gather(in_weight[0].reshape(256, 1536), ("xl", "y", "core"))
    w_moves = [(0, p, 0, 1536, None, 0, True, p) for p in range(16)]

    o = out_weight[0]
    partner, o_xl, *near = together(shift(hidden, "xh", 1), shift(o, "xl", 1), *[shift(hidden, "z", by) for by in ways])
    x_pieces = [hidden, *near, partner] + [shift(partner, "z", by) for by in ways]
    x_index = jnp.stack([behind(z, by) * 2 + c for c in (xh, 1 - xh) for by in (0, *ways)]).astype(jnp.int32)
    o = jnp.stack([o, o_xl])
    o_list = [o] + [shift(o, "y", by) for by in ways]
    q_list = o_list + [other_core(v) for v in o_list]
    q_moves, slots = [], [z, core]
    for number, (c, by) in enumerate([(c, by) for c in (core, 1 - core) for by in (0, *ways)]):
        for e, at_xl in enumerate((xl, 1 - xl)):
            q_moves.append((number, e, 0, 256, len(slots), 0, False))
            slots.append(at_xl * 8 + behind(y, by) * 2 + c)
    q_index = jnp.stack(slots).astype(jnp.int32)

    w1 = swap(after(in_weight[1], partner))
    small = jnp.concatenate([feat_filter[1].reshape(9, 512), skip_gain[1:2], mr_filter], axis=0)
    o1, base, small = after((out_weight[1], hidden, small), *x_pieces, *o_list)
    o1, base, small = swap(o1), swap(base), swap(small)
    w1 = gather(after(w1, *x_pieces).reshape(256, 1536), ("xh", "xl", "y"))
    o1 = gather(o1, ("xh", "xl", "y"))

    pieces = norm_rows(x_index, gains[0], x_pieces)
    low, high, tail = project_in(x_index, pieces, w0, w_moves, 2, 16)
    tail = from_behind(tail, ("xl", "y", "core"))

    def first_parts(before, main):
        parts = mix_out(
            q_index, before, main, feat_filter[0].reshape(9, 512), se_filter, skip_gain[0:1], q_list, q_moves, 16,
            [(HALF, 1024)] * 4,
        )
        return parts[0], [shift(part, "z", by) for by, part in ((1, parts[1]), (-1, parts[3]), (2, parts[2]))]

    def over_z(own, received):
        total = own.astype(jnp.float32)
        for value in received:
            total = total + value.astype(jnp.float32)
        total = total.astype(jnp.bfloat16)
        pick = lambda c: jnp.where(c == 0, total[:, :512], total[:, 512:])
        mine, others = pick(core), pick(1 - core)
        return mine, [
            lax.ppermute(mine, ("core", "xh"), [(1, 0), (2, 3)]),
            lax.ppermute(others, ("core", "xh"), [(1, 2), (2, 1)]),
            lax.ppermute(others, ("core", "xh"), [(0, 2), (3, 1)]),
        ]

    def over_x(mine, received, rows):
        kept = jnp.where(core == xh, mine, jnp.zeros_like(mine))
        current = base[rows : rows + HALF].astype(jnp.float32) + kept.astype(jnp.float32)
        for value in received:
            current = current + value.astype(jnp.float32)
        return current.astype(jnp.bfloat16)

    own_high, high_z = first_parts(low, high)
    own_low, low_z = first_parts(tail, low)
    mine_high, high_x = over_z(own_high, high_z)
    *low_z, one, two, three = together(*low_z, *high_x)
    high = over_x(mine_high, (one, two, three), HALF)
    mine_low, low_x = over_z(own_low, low_z)
    high_near = [shift(high, "z", by) for by in ways]
    one, two, three, *high_near = together(*low_x, *high_near)
    low = over_x(mine_low, (one, two, three), 0)

    places = [(p, (p // 4 % 2) * 8 + (p % 4) * 2 + p // 8) for p in range(16)]
    w_moves = [(0, p, 0, 1536, None, 0, True, block) for p, block in places]
    q_moves = [(0, p, 0, 256, None, 0, False, block) for p, block in places]
    x_index = jnp.stack([behind(z, by) * 2 + c for c in (core, 1 - core) for by in (0, *ways)]).astype(jnp.int32)

    def projected(near, halo):
        return project_in(x_index, [gains[1], *near, *[other_core(v) for v in near]], w1, w_moves, 1, halo)

    p_high, tail = projected([high] + high_near, 144)
    low_near = [shift(low, "z", by) for by in ways]
    p_high, tail, *low_near = together(p_high, tail, *low_near)
    tail = from_behind(tail, ("xl", "y", "xh"))
    (p_low,) = projected([low] + low_near, 0)
    tail, p_low = together(tail, p_low)

    def second_filter(before, main):
        return filtered(before, main, small[:9], small[10:], small[9:10], 144)

    def second_parts(inner):
        return project_out(q_index, inner, o1, q_moves, [(4, HALF, 512)] * 2)

    def second_z(own, theirs):
        both = (own.astype(jnp.float32) + theirs.astype(jnp.float32)).astype(jnp.bfloat16)
        return both[0], [shift(both[at], "z", by) for by, at in ((1, 1), (-1, 3), (2, 2))]

    def second_sum(own, received, rows):
        total = rows.astype(jnp.float32) + own.astype(jnp.float32)
        for value in received:
            total = total + value.astype(jnp.float32)
        return swap(total.astype(jnp.bfloat16))

    inner_high = second_filter(p_low, p_high)
    inner_low = second_filter(tail, p_low)
    inner_high, inner_low, o1 = together(inner_high, inner_low, o1)
    own_high, theirs_high = second_parts(inner_high)
    theirs_high = other_core(theirs_high)
    theirs_high, inner_low = together(theirs_high, inner_low)
    own_high, high_z = second_z(own_high, theirs_high)
    own_low, theirs_low = second_parts(inner_low)
    theirs_low = other_core(theirs_low)
    own_low, theirs_low, *high_z = together(own_low, theirs_low, *high_z)
    high = second_sum(own_high, high_z, high)
    own_low, low_z = second_z(own_low, theirs_low)
    low = second_sum(own_low, low_z, low)
    return jnp.concatenate([low, high], axis=0)


def solution(mesh):
    fine = Mesh(np.asarray(mesh.devices).reshape(2, 4, 2, 4, 2), AXES)
    ctx, ch = ("xl", "y", "core"), ("z", "xh")
    return jax.shard_map(
        per_device,
        mesh=fine,
        in_specs=(
            P(ctx, ch),
            P(),
            P(None, ctx, None, ch),
            P(None, None, None, ch),
            P(None, ch),
            P(None, ch),
            P(None, ch),
            P(None, ch, ctx),
        ),
        out_specs=P(ctx, ch),
        check_vma=False,
    )
```

```python
import functools

import jax
import jax.numpy as jnp
import numpy as np
from jax import lax
from jax.experimental.layout import Layout, with_layout_constraint
from jax.experimental import pallas as pl
from jax.experimental.pallas import tpu as pltpu
from jax.sharding import Mesh, PartitionSpec as P

AXES = ("xl", "y", "core", "z", "xh")
HALF = 256
CUT = 1152
LANES = 128


def shift(value, axis, by):
    size = lax.axis_size(axis)
    return lax.ppermute(value, axis, [(i, (i + by) % size) for i in range(size)])


def swap(value):
    moved = lax.ppermute(value, ("core", "xh"), [(1, 2), (2, 1)])
    same = lax.axis_index("core") == lax.axis_index("xh")
    return jnp.where(same, value, moved)


def from_behind(value, axes):
    return lax.ppermute(value, axes, [(i, i + 1) for i in range(15)])


def by_rows(value):
    return with_layout_constraint(value, Layout(major_to_minor=tuple(range(value.ndim))))


def after(value, *others):
    return lax.optimization_barrier((value, *others))[0]


def together(*values):
    return lax.optimization_barrier(values)


def fetch(moves, sources, target, index_ref, semaphores):
    copies = []
    for number, (source, lead, lane, width, slot, other, by_rows, *fixed) in enumerate(moves):
        block = fixed[0] * 256 if slot is None else pl.multiple_of(index_ref[slot] * 256, 256)
        ref = sources[source]
        if lead is not None:
            ref = ref.at[lead]
        if by_rows:
            piece = target.at[pl.ds(block, 256), other : other + width]
        else:
            piece = target.at[other : other + ref.shape[0], pl.ds(block, 256)]
        copies.append(pltpu.make_async_copy(ref.at[:, lane : lane + width], piece, semaphores.at[number]))
    return copies


def norm_pieces(loads, places, raw, gain_ref, normed, squares):
    squares[...] = jnp.zeros_like(squares)
    for j, load in enumerate(loads):
        load.wait()
        lanes = pl.ds(pl.multiple_of(places[j] * 512, 512), 512)
        gain = gain_ref[pl.ds(places[j], 1), :]

        @pl.loop(0, squares.shape[0] // 64)
        def _(step):
            rows = pl.ds(pl.multiple_of(step * 64, 64), 64)
            x = raw[j, rows, :].astype(jnp.float32)
            normed[rows, lanes] = (x * gain).astype(jnp.bfloat16)
            q = x * x
            squares[rows, :] += (q[:, :128] + q[:, 128:256]) + (q[:, 256:384] + q[:, 384:])

    squares[:, :1] = lax.rsqrt(jnp.sum(squares[...], axis=1, keepdims=True) * (1.0 / 4096) + 1e-06)


def norm_kernel(index_ref, gain_ref, *refs):
    xs, (normed, squares, raw, x_sems) = refs[:-4], refs[-4:]
    xs = [xs[0].at[j] for j in range(8)] if len(xs) == 1 else xs
    loads = [pltpu.make_async_copy(x, raw.at[j], x_sems.at[j]) for j, x in enumerate(xs)]
    for load in loads:
        load.start()
    norm_pieces(loads, [index_ref[j] for j in range(8)], raw, gain_ref, normed, squares)


def norm_rows(index, gain, pieces):
    rows = pieces[0].shape[-2]
    any_space = pl.BlockSpec(memory_space=pl.ANY)
    vmem = pl.BlockSpec(memory_space=pltpu.VMEM)
    return pl.pallas_call(
        norm_kernel,
        out_shape=[
            jax.ShapeDtypeStruct((rows, 4096), jnp.bfloat16),
            jax.ShapeDtypeStruct((rows, LANES), jnp.float32),
        ],
        in_specs=[pl.BlockSpec(memory_space=pltpu.SMEM), vmem] + [any_space] * len(pieces),
        out_specs=[vmem, vmem],
        scratch_shapes=[pltpu.VMEM((8, rows, 512), jnp.bfloat16), pltpu.SemaphoreType.DMA((8,))],
        compiler_params=pltpu.CompilerParams(vmem_limit_bytes=24 * 1024 * 1024),
        cost_estimate=pl.CostEstimate(flops=rows * 4096 * 4, bytes_accessed=rows * 4096 * 4, transcendentals=0),
    )(index, gain, *pieces)


def in_kernel(moves, groups, halo, index_ref, *refs):
    ins, refs = refs[: 2 * groups], refs[2 * groups :]
    count = 1 + max(m[0] for m in moves)
    ws, refs = refs[:count], refs[count:]
    out_refs, (tail_ref, weights, w_sems) = refs[:2], refs[2:]
    copies = fetch(moves, ws, weights, index_ref, w_sems)
    for copy in copies:
        copy.start()
    for copy in copies:
        copy.wait()

    @pl.loop(0, 6)
    def _(step):
        lanes = pl.ds(pl.multiple_of(step * 256, 256), 256)
        for group in range(groups):
            normed, squares = ins[2 * group], ins[2 * group + 1]
            product = jnp.dot(normed[...], weights[:, lanes], preferred_element_type=jnp.float32)
            product = (product * squares[:, :1]).astype(jnp.bfloat16)
            for part in range(2 // groups):
                out_refs[group + part][:, lanes] = product[part * HALF : (part + 1) * HALF]

    last = out_refs[-1]
    tail_ref[:halo, :] = last[HALF - halo :, 512:]
    tail_ref[halo:, :512] = last[HALF - 16 :, :512]
    tail_ref[halo:, 512:] = jnp.zeros((16, 512), jnp.bfloat16)


def project_in(index, rows, weights, moves, halo):
    any_space = pl.BlockSpec(memory_space=pl.ANY)
    vmem = pl.BlockSpec(memory_space=pltpu.VMEM)
    return pl.pallas_call(
        functools.partial(in_kernel, moves, len(rows) // 2, halo),
        out_shape=[jax.ShapeDtypeStruct((HALF, 1536), jnp.bfloat16)] * 2
        + [jax.ShapeDtypeStruct((halo + 16, 1024), jnp.bfloat16)],
        in_specs=[pl.BlockSpec(memory_space=pltpu.SMEM)] + [vmem] * len(rows) + [any_space] * len(weights),
        out_specs=[vmem] * 3,
        scratch_shapes=[pltpu.VMEM((4096, 1536), jnp.bfloat16), pltpu.SemaphoreType.DMA((len(moves),))],
        compiler_params=pltpu.CompilerParams(vmem_limit_bytes=48 * 1024 * 1024),
        cost_estimate=pl.CostEstimate(flops=4 * HALF * 4096 * 1536, bytes_accessed=18 * 2**20, transcendentals=0),
    )(index, *rows, *weights)


def filter_rows(halo, taps, before_ref, main_ref, feat_ref, filter_ref, skip_ref, inner, shaped, gated, copies8):
    total = halo + HALF

    if before_ref.shape[1] == 1024:
        shaped[:16, :512] = before_ref[halo:, :512].astype(jnp.float32)
        shaped[:halo, 512:] = before_ref[:halo, :].astype(jnp.float32)
    else:
        shaped[:16, :512] = before_ref[HALF - 16 :, :512].astype(jnp.float32)
        shaped[:halo, 512:] = before_ref[HALF - halo :, 512:].astype(jnp.float32)
    shaped[16 : 16 + HALF, :512] = main_ref[:, :512].astype(jnp.float32)
    shaped[halo:total, 512:] = main_ref[:, 512:].astype(jnp.float32)

    def feature(start, size, s, lanes):
        value = None
        for j in range(3):
            tap = feat_ref[3 * j + s : 3 * j + s + 1, lanes]
            low = s * 512 + lanes.start
            term = tap * shaped[start - j : start - j + size, low : low + LANES]
            value = term if value is None else value + term
        return value

    for lane in range(0, 512, LANES):
        lanes = slice(lane, lane + LANES)
        for start in range(8, total, 64):
            size = min(64, total - start)
            gated[start : start + size, lanes] = feature(start, size, 1, lanes) * feature(start, size, 2, lanes)
        gated[:8, lanes] = jnp.zeros((8, LANES), jnp.float32)

    if taps == 7:
        for lane in range(0, 512, LANES):
            lanes = slice(lane, lane + LANES)
            for start in range(0, HALF, 64):
                own = gated[halo + start : halo + start + 64, lanes]
                value = (skip_ref[:1, lanes] + filter_ref[:1, lanes]) * own
                for j in range(1, taps):
                    value = value + filter_ref[j : j + 1, lanes] * gated[halo + start - j : halo + start - j + 64, lanes]
                inner[start : start + 64, lanes] = (feature(16 + start, 64, 0, lanes) * value).astype(jnp.bfloat16)
    else:
        for lane in range(0, 512, LANES):
            lanes = slice(lane, lane + LANES)
            for r in range(8):
                for start in range(0, HALF + 128, 128):
                    copies8[r, start : start + 128, :] = gated[16 + start - r : 16 + start - r + 128, lanes]

            @pl.loop(0, HALF // 128)
            def _(step):
                base = pl.multiple_of(step * 128, 128)
                value = jnp.zeros((128, LANES), jnp.float32)
                for r in range(8):
                    for a in range(0, 16, 4):
                        window = copies8[r, pl.ds(pl.multiple_of(base + 128 - 8 * (a + 3), 8), 128 + 24), :]
                        for b in range(4):
                            tap = filter_ref[8 * (a + b) + r : 8 * (a + b) + r + 1, lanes]
                            low = 8 * (3 - b)
                            value = value + tap * window[low : low + 128]
                copies8[8, pl.ds(base, 128), :] = value

            for start in range(0, HALF, 64):
                own = gated[halo + start : halo + start + 64, lanes]
                value = copies8[8, start : start + 64, :] + skip_ref[:1, lanes] * own
                inner[start : start + 64, lanes] = (feature(16 + start, 64, 0, lanes) * value).astype(jnp.bfloat16)


def product_rows(outs, index_ref, inner, weights, out_refs):
    z = index_ref[0]
    core = index_ref[1]
    for by in range(4):
        block = lax.rem(z + by, 4)
        if outs == 4:
            columns = pl.ds(pl.multiple_of(block * 1024, 1024), 1024)
            out_refs[by][...] = jnp.dot(
                inner[...], weights[:, columns], preferred_element_type=jnp.float32
            ).astype(jnp.bfloat16)
        else:
            for side in range(2):
                place = block * 2 + (core if side == 0 else 1 - core)
                columns = pl.ds(pl.multiple_of(place * 512, 512), 512)
                out_refs[side][by] = jnp.dot(
                    inner[...], weights[:, columns], preferred_element_type=jnp.float32
                ).astype(jnp.bfloat16)


def filter_scratch(halo, taps):
    return [
        pltpu.VMEM((halo + HALF + 16, 1536), jnp.float32),
        pltpu.VMEM((halo + HALF, 512), jnp.float32),
        pltpu.VMEM((9, 8, LANES) if taps == 7 else (9, HALF + 128, LANES), jnp.float32),
    ]


def mix_kernel(moves, halo, taps, outs, index_ref, before_ref, main_ref, feat_ref, filter_ref, skip_ref, *refs):
    count = 1 + max(m[0] for m in moves)
    ws, refs = refs[:count], refs[count:]
    out_refs, refs = refs[:outs], refs[outs:]
    shaped, gated, copies8, inner, weights, w_sems = refs
    copies = fetch(moves, ws, weights, index_ref, w_sems)
    for copy in copies:
        copy.start()
    filter_rows(halo, taps, before_ref, main_ref, feat_ref, filter_ref, skip_ref, inner, shaped, gated, copies8)
    for copy in copies:
        copy.wait()
    product_rows(outs, index_ref, inner, weights, out_refs)


def mix_out(index, before, main, feat, taps, skip, weights, moves, halo, out_shapes):
    any_space = pl.BlockSpec(memory_space=pl.ANY)
    vmem = pl.BlockSpec(memory_space=pltpu.VMEM)
    length = taps.shape[0]
    return pl.pallas_call(
        functools.partial(mix_kernel, moves, halo, length, len(out_shapes)),
        out_shape=[jax.ShapeDtypeStruct(s, jnp.bfloat16) for s in out_shapes],
        in_specs=[pl.BlockSpec(memory_space=pltpu.SMEM)] + [vmem] * 5 + [any_space] * len(weights),
        out_specs=[vmem] * len(out_shapes),
        scratch_shapes=filter_scratch(halo, length)
        + [
            pltpu.VMEM((HALF, 512), jnp.bfloat16),
            pltpu.VMEM((512, 4096), jnp.bfloat16),
            pltpu.SemaphoreType.DMA((len(moves),)),
        ],
        compiler_params=pltpu.CompilerParams(vmem_limit_bytes=48 * 1024 * 1024),
        cost_estimate=pl.CostEstimate(flops=2 * HALF * 512 * 4096, bytes_accessed=6 * 2**20, transcendentals=0),
    )(index, before, main, feat, taps, skip, *weights)


def filter_kernel(halo, taps, before_ref, main_ref, feat_ref, filter_ref, skip_ref, inner, shaped, gated, copies8):
    filter_rows(halo, taps, before_ref, main_ref, feat_ref, filter_ref, skip_ref, inner, shaped, gated, copies8)


def filtered(before, main, feat, taps, skip, halo):
    vmem = pl.BlockSpec(memory_space=pltpu.VMEM)
    length = taps.shape[0]
    return pl.pallas_call(
        functools.partial(filter_kernel, halo, length),
        out_shape=jax.ShapeDtypeStruct((HALF, 512), jnp.bfloat16),
        in_specs=[vmem] * 5,
        out_specs=vmem,
        scratch_shapes=filter_scratch(halo, length),
        compiler_params=pltpu.CompilerParams(vmem_limit_bytes=24 * 1024 * 1024),
        cost_estimate=pl.CostEstimate(flops=2 * HALF * 512 * 4096 * 3, bytes_accessed=3 * 2**20, transcendentals=0),
    )(before, main, feat, taps, skip)


def product_kernel(moves, outs, index_ref, inner, weight_ref, *refs):
    out_refs, (weights, w_sems) = refs[:outs], refs[outs:]
    copies = fetch(moves, [weight_ref], weights, index_ref, w_sems)
    for copy in copies:
        copy.start()
    for copy in copies:
        copy.wait()
    product_rows(outs, index_ref, inner, weights, out_refs)


def project_out(index, inner, weight, moves, out_shapes):
    vmem = pl.BlockSpec(memory_space=pltpu.VMEM)
    return pl.pallas_call(
        functools.partial(product_kernel, moves, len(out_shapes)),
        out_shape=[jax.ShapeDtypeStruct(s, jnp.bfloat16) for s in out_shapes],
        in_specs=[pl.BlockSpec(memory_space=pltpu.SMEM), vmem, pl.BlockSpec(memory_space=pl.ANY)],
        out_specs=[vmem] * len(out_shapes),
        scratch_shapes=[pltpu.VMEM((512, 4096), jnp.bfloat16), pltpu.SemaphoreType.DMA((len(moves),))],
        compiler_params=pltpu.CompilerParams(vmem_limit_bytes=48 * 1024 * 1024),
        cost_estimate=pl.CostEstimate(flops=2 * HALF * 512 * 4096, bytes_accessed=6 * 2**20, transcendentals=0),
    )(index, inner, weight)


def per_device(hidden, norm_gain, in_weight, feat_filter, se_filter, mr_filter, skip_gain, out_weight):
    xl, y, core, z, xh = (lax.axis_index(a) for a in AXES)
    behind = lambda place, by: (place - by) % 4
    gains = norm_gain.reshape(2, 8, 512)
    ways = (1, -1, 2)
    other_core = lambda value: shift(value, "core", 1)
    gather = lambda value, axes: by_rows(lax.all_gather(by_rows(value), axes, axis=0, tiled=False))

    side_by_side = lambda w, o: jnp.concatenate([w.reshape(256, 1536), o[:256], o[256:]], axis=1)

    whole = lax.all_gather(hidden, ("z", "xh"), axis=0, tiled=False)

    m = side_by_side(in_weight[0], out_weight[0])
    m_xl = shift(m, "xl", 1)
    m_xl, w1, *m_y = together(m_xl, swap(in_weight[1]), *[shift(m, "y", by) for by in ways])
    o1 = swap(after(out_weight[1], m_xl))
    rest = shift(jnp.stack([v[:, CUT:] for v in m_y]), "xl", 1)
    most = [shift(m_xl[:, :CUT], "y", by) for by in ways]
    rest, *more = together(rest, *most, *[other_core(after(v, most[0])) for v in (m, m_xl, *m_y)])
    most, far = more[:3], more[3:]
    w_list = [m, m_xl, *m_y, *far, rest, *most] + [other_core(v) for v in (rest, *most)]
    w_moves, q_moves, slots = [], [], [z, core]

    def take(number, lead, at_xl, at_y, at_core, low, high):
        w_moves.append((number, lead, 0, min(high, 1536) - low, len(slots), low, True))
        if high == 2048:
            for half in range(2):
                q_moves.append((number, lead, 1536 + 256 * half - low, 256, len(slots), 256 * half, False))
        slots.append(at_xl * 8 + at_y * 2 + at_core)

    for number, c in ((0, core), (5, 1 - core)):
        take(number, None, xl, y, c, 0, 2048)
        take(number + 1, None, 1 - xl, y, c, 0, 2048)
        for e, by in enumerate(ways):
            take(number + 2 + e, None, xl, behind(y, by), c, 0, 2048)
    for number, c in ((10, core), (14, 1 - core)):
        for e, by in enumerate(ways):
            take(number, e, 1 - xl, behind(y, by), c, CUT, 2048)
            take(number + 1 + e, None, 1 - xl, behind(y, by), c, 0, CUT)
    q_index = jnp.stack(slots).astype(jnp.int32)
    q_list = w_list[:15]

    w1 = gather(after(side_by_side(w1, o1), rest, *most), ("xh", "xl", "y"))
    small = jnp.concatenate([feat_filter[1].reshape(9, 512), skip_gain[1:2], mr_filter], axis=0)

    rows = norm_rows(jnp.arange(8, dtype=jnp.int32), gains[0], [whole])
    low, high, tail = project_in(q_index, rows, w_list, w_moves, 16)
    base, small = after((hidden, small), low)
    base, small = swap(base), swap(small)
    tail = from_behind(tail, ("xl", "y", "core"))

    def first_parts(before, main):
        parts = mix_out(
            q_index, before, main, feat_filter[0].reshape(9, 512), se_filter, skip_gain[0:1], q_list, q_moves, 16,
            [(HALF, 1024)] * 4,
        )
        return parts[0], [shift(part, "z", by) for by, part in ((1, parts[1]), (-1, parts[3]), (2, parts[2]))]

    def over_z(own, received):
        total = own.astype(jnp.float32)
        for value in received:
            total = total + value.astype(jnp.float32)
        total = total.astype(jnp.bfloat16)
        pick = lambda c: jnp.where(c == 0, total[:, :512], total[:, 512:])
        mine, others = pick(core), pick(1 - core)
        return mine, [
            lax.ppermute(mine, ("core", "xh"), [(1, 0), (2, 3)]),
            lax.ppermute(others, ("core", "xh"), [(1, 2), (2, 1)]),
            lax.ppermute(others, ("core", "xh"), [(0, 2), (3, 1)]),
        ]

    def over_x(mine, received, rows):
        kept = jnp.where(core == xh, mine, jnp.zeros_like(mine))
        current = base[rows : rows + HALF].astype(jnp.float32) + kept.astype(jnp.float32)
        for value in received:
            current = current + value.astype(jnp.float32)
        return current.astype(jnp.bfloat16)

    own_high, high_z = first_parts(low, high)
    own_low, low_z = first_parts(tail, low)
    mine_high, high_x = over_z(own_high, high_z)
    *low_z, one, two, three = together(*low_z, *high_x)
    high = over_x(mine_high, (one, two, three), HALF)
    mine_low, low_x = over_z(own_low, low_z)
    high_near = [shift(high, "z", by) for by in ways]
    one, two, three, *high_near = together(*low_x, *high_near)
    low = over_x(mine_low, (one, two, three), 0)

    places = [(p, (p // 4 % 2) * 8 + (p % 4) * 2 + p // 8) for p in range(16)]
    w_moves = [(0, p, 0, 1536, None, 0, True, block) for p, block in places]
    p_moves = [(0, p, 1536 + 256 * half, 256, None, 256 * half, False, block) for p, block in places for half in range(2)]
    x_index = jnp.stack([behind(z, by) * 2 + c for c in (core, 1 - core) for by in (0, *ways)]).astype(jnp.int32)

    def normed(near):
        return norm_rows(x_index, gains[1], near + [other_core(v) for v in near])

    high_near = [high] + high_near
    low_near = [low] + [shift(low, "z", by) for by in ways]
    rows = normed(low_near) + normed(high_near)
    p_low, p_high, tail = project_in(q_index, rows, [w1], w_moves, 144)
    tail = from_behind(tail, ("xl", "y", "xh"))

    def second_filter(before, main):
        return filtered(before, main, small[:9], small[10:], small[9:10], 144)

    def second_parts(inner):
        return project_out(q_index, inner, w1, p_moves, [(4, HALF, 512)] * 2)

    def second_z(own, theirs):
        both = (own.astype(jnp.float32) + theirs.astype(jnp.float32)).astype(jnp.bfloat16)
        return both[0], [shift(both[at], "z", by) for by, at in ((1, 1), (-1, 3), (2, 2))]

    def second_sum(own, received, rows):
        total = rows.astype(jnp.float32) + own.astype(jnp.float32)
        for value in received:
            total = total + value.astype(jnp.float32)
        return swap(total.astype(jnp.bfloat16))

    inner_high = second_filter(p_low, p_high)
    inner_low = second_filter(tail, p_low)
    inner_high, inner_low = together(inner_high, inner_low)
    own_high, theirs_high = second_parts(inner_high)
    theirs_high = other_core(theirs_high)
    theirs_high, inner_low = together(theirs_high, inner_low)
    own_high, high_z = second_z(own_high, theirs_high)
    own_low, theirs_low = second_parts(inner_low)
    theirs_low = other_core(theirs_low)
    own_low, theirs_low, *high_z = together(own_low, theirs_low, *high_z)
    high = second_sum(own_high, high_z, high)
    own_low, low_z = second_z(own_low, theirs_low)
    low = second_sum(own_low, low_z, low)
    return jnp.concatenate([low, high], axis=0)


def solution(mesh):
    fine = Mesh(np.asarray(mesh.devices).reshape(2, 4, 2, 4, 2), AXES)
    ctx, ch = ("xl", "y", "core"), ("z", "xh")
    return jax.shard_map(
        per_device,
        mesh=fine,
        in_specs=(
            P(ctx, ch),
            P(),
            P(None, ctx, None, ch),
            P(None, None, None, ch),
            P(None, ch),
            P(None, ch),
            P(None, ch),
            P(None, ch, ctx),
        ),
        out_specs=P(ctx, ch),
        check_vma=False,
    )
```

```python
import functools

import jax
import jax.numpy as jnp
import numpy as np
from jax import lax
from jax.experimental.layout import Layout, with_layout_constraint
from jax.experimental import pallas as pl
from jax.experimental.pallas import tpu as pltpu
from jax.sharding import Mesh, PartitionSpec as P

AXES = ("xl", "y", "core", "z", "xh")
HALF = 256
CUT = 1152
LANES = 128


def shift(value, axis, by):
    size = lax.axis_size(axis)
    return lax.ppermute(value, axis, [(i, (i + by) % size) for i in range(size)])


def swap(value):
    moved = lax.ppermute(value, ("core", "xh"), [(1, 2), (2, 1)])
    same = lax.axis_index("core") == lax.axis_index("xh")
    return jnp.where(same, value, moved)


def from_behind(value, axes):
    return lax.ppermute(value, axes, [(i, i + 1) for i in range(15)])


def by_rows(value):
    return with_layout_constraint(value, Layout(major_to_minor=tuple(range(value.ndim))))


def after(value, *others):
    return lax.optimization_barrier((value, *others))[0]


def together(*values):
    return lax.optimization_barrier(values)


def fetch(moves, sources, target, index_ref, semaphores):
    copies = []
    for number, (source, lead, lane, width, slot, other, by_rows, *fixed) in enumerate(moves):
        block = fixed[0] * 256 if slot is None else pl.multiple_of(index_ref[slot] * 256, 256)
        ref = sources[source]
        if lead is not None:
            ref = ref.at[lead]
        if by_rows:
            piece = target.at[pl.ds(block, 256), other : other + width]
        else:
            piece = target.at[other : other + ref.shape[0], pl.ds(block, 256)]
        copies.append(pltpu.make_async_copy(ref.at[:, lane : lane + width], piece, semaphores.at[number]))
    return copies


def norm_pieces(loads, places, raw, gain_ref, normed, squares):
    squares[...] = jnp.zeros_like(squares)
    for j, load in enumerate(loads):
        load.wait()
        lanes = pl.ds(pl.multiple_of(places[j] * 512, 512), 512)
        gain = gain_ref[pl.ds(places[j], 1), :]

        @pl.loop(0, squares.shape[0] // 64)
        def _(step):
            rows = pl.ds(pl.multiple_of(step * 64, 64), 64)
            x = raw[j, rows, :].astype(jnp.float32)
            normed[rows, lanes] = (x * gain).astype(jnp.bfloat16)
            q = x * x
            squares[rows, :] += (q[:, :128] + q[:, 128:256]) + (q[:, 256:384] + q[:, 384:])

    squares[:, :1] = lax.rsqrt(jnp.sum(squares[...], axis=1, keepdims=True) * (1.0 / 4096) + 1e-06)


def norm_kernel(index_ref, gain_ref, *refs):
    xs, (normed, squares, raw, x_sems) = refs[:-4], refs[-4:]
    xs = [xs[0].at[j] for j in range(8)] if len(xs) == 1 else xs
    loads = [pltpu.make_async_copy(x, raw.at[j], x_sems.at[j]) for j, x in enumerate(xs)]
    for load in loads:
        load.start()
    norm_pieces(loads, [index_ref[j] for j in range(8)], raw, gain_ref, normed, squares)


def norm_rows(index, gain, pieces):
    rows = pieces[0].shape[-2]
    any_space = pl.BlockSpec(memory_space=pl.ANY)
    vmem = pl.BlockSpec(memory_space=pltpu.VMEM)
    return pl.pallas_call(
        norm_kernel,
        out_shape=[
            jax.ShapeDtypeStruct((rows, 4096), jnp.bfloat16),
            jax.ShapeDtypeStruct((rows, LANES), jnp.float32),
        ],
        in_specs=[pl.BlockSpec(memory_space=pltpu.SMEM), vmem] + [any_space] * len(pieces),
        out_specs=[vmem, vmem],
        scratch_shapes=[pltpu.VMEM((8, rows, 512), jnp.bfloat16), pltpu.SemaphoreType.DMA((8,))],
        compiler_params=pltpu.CompilerParams(vmem_limit_bytes=24 * 1024 * 1024),
        cost_estimate=pl.CostEstimate(flops=rows * 4096 * 4, bytes_accessed=rows * 4096 * 4, transcendentals=0),
    )(index, gain, *pieces)


def in_kernel(moves, groups, halo, index_ref, *refs):
    ins, refs = refs[: 2 * groups], refs[2 * groups :]
    count = 1 + max(m[0] for m in moves)
    ws, refs = refs[:count], refs[count:]
    out_refs, (tail_ref, weights, w_sems) = refs[:2], refs[2:]
    copies = fetch(moves, ws, weights, index_ref, w_sems)
    for copy in copies:
        copy.start()
    for copy in copies:
        copy.wait()

    @pl.loop(0, 6)
    def _(step):
        lanes = pl.ds(pl.multiple_of(step * 256, 256), 256)
        for group in range(groups):
            normed, squares = ins[2 * group], ins[2 * group + 1]
            product = jnp.dot(normed[...], weights[:, lanes], preferred_element_type=jnp.float32)
            product = (product * squares[:, :1]).astype(jnp.bfloat16)
            for part in range(2 // groups):
                out_refs[group + part][:, lanes] = product[part * HALF : (part + 1) * HALF]

    last = out_refs[-1]
    tail_ref[:halo, :] = last[HALF - halo :, 512:]
    tail_ref[halo:, :512] = last[HALF - 16 :, :512]
    tail_ref[halo:, 512:] = jnp.zeros((16, 512), jnp.bfloat16)


def project_in(index, rows, weights, moves, halo):
    any_space = pl.BlockSpec(memory_space=pl.ANY)
    vmem = pl.BlockSpec(memory_space=pltpu.VMEM)
    return pl.pallas_call(
        functools.partial(in_kernel, moves, len(rows) // 2, halo),
        out_shape=[jax.ShapeDtypeStruct((HALF, 1536), jnp.bfloat16)] * 2
        + [jax.ShapeDtypeStruct((halo + 16, 1024), jnp.bfloat16)],
        in_specs=[pl.BlockSpec(memory_space=pltpu.SMEM)] + [vmem] * len(rows) + [any_space] * len(weights),
        out_specs=[vmem] * 3,
        scratch_shapes=[pltpu.VMEM((4096, 1536), jnp.bfloat16), pltpu.SemaphoreType.DMA((len(moves),))],
        compiler_params=pltpu.CompilerParams(vmem_limit_bytes=48 * 1024 * 1024),
        cost_estimate=pl.CostEstimate(flops=4 * HALF * 4096 * 1536, bytes_accessed=18 * 2**20, transcendentals=0),
    )(index, *rows, *weights)


def filter_rows(halo, taps, before_ref, main_ref, feat_ref, filter_ref, skip_ref, inner, shaped, gated, copies8):
    total = halo + HALF

    if before_ref.shape[1] == 1024:
        shaped[:16, :512] = before_ref[halo:, :512].astype(jnp.float32)
        shaped[:halo, 512:] = before_ref[:halo, :].astype(jnp.float32)
    else:
        shaped[:16, :512] = before_ref[HALF - 16 :, :512].astype(jnp.float32)
        shaped[:halo, 512:] = before_ref[HALF - halo :, 512:].astype(jnp.float32)
    shaped[16 : 16 + HALF, :512] = main_ref[:, :512].astype(jnp.float32)
    shaped[halo:total, 512:] = main_ref[:, 512:].astype(jnp.float32)

    def feature(start, size, s, lanes):
        value = None
        for j in range(3):
            tap = feat_ref[3 * j + s : 3 * j + s + 1, lanes]
            low = s * 512 + lanes.start
            term = tap * shaped[start - j : start - j + size, low : low + LANES]
            value = term if value is None else value + term
        return value

    for lane in range(0, 512, LANES):
        lanes = slice(lane, lane + LANES)
        for start in range(8, total, 64):
            size = min(64, total - start)
            gated[start : start + size, lanes] = feature(start, size, 1, lanes) * feature(start, size, 2, lanes)
        gated[:8, lanes] = jnp.zeros((8, LANES), jnp.float32)

    if taps == 7:
        for lane in range(0, 512, LANES):
            lanes = slice(lane, lane + LANES)
            for start in range(0, HALF, 64):
                own = gated[halo + start : halo + start + 64, lanes]
                value = (skip_ref[:1, lanes] + filter_ref[:1, lanes]) * own
                for j in range(1, taps):
                    value = value + filter_ref[j : j + 1, lanes] * gated[halo + start - j : halo + start - j + 64, lanes]
                inner[start : start + 64, lanes] = (feature(16 + start, 64, 0, lanes) * value).astype(jnp.bfloat16)
    else:
        for lane in range(0, 512, LANES):
            lanes = slice(lane, lane + LANES)
            for r in range(8):
                for start in range(0, HALF + 128, 128):
                    copies8[r, start : start + 128, :] = gated[16 + start - r : 16 + start - r + 128, lanes]

            @pl.loop(0, HALF // 128)
            def _(step):
                base = pl.multiple_of(step * 128, 128)
                value = jnp.zeros((128, LANES), jnp.float32)
                for r in range(8):
                    for a in range(0, 16, 4):
                        window = copies8[r, pl.ds(pl.multiple_of(base + 128 - 8 * (a + 3), 8), 128 + 24), :]
                        for b in range(4):
                            tap = filter_ref[8 * (a + b) + r : 8 * (a + b) + r + 1, lanes]
                            low = 8 * (3 - b)
                            value = value + tap * window[low : low + 128]
                copies8[8, pl.ds(base, 128), :] = value

            for start in range(0, HALF, 64):
                own = gated[halo + start : halo + start + 64, lanes]
                value = copies8[8, start : start + 64, :] + skip_ref[:1, lanes] * own
                inner[start : start + 64, lanes] = (feature(16 + start, 64, 0, lanes) * value).astype(jnp.bfloat16)


def product_rows(outs, index_ref, inner, weights, out_refs):
    z = index_ref[0]
    core = index_ref[1]
    for by in range(4):
        block = lax.rem(z + by, 4)
        if outs == 4:
            columns = pl.ds(pl.multiple_of(block * 1024, 1024), 1024)
            out_refs[by][...] = jnp.dot(
                inner[...], weights[:, columns], preferred_element_type=jnp.float32
            ).astype(jnp.bfloat16)
        else:
            for side in range(2):
                place = block * 2 + (core if side == 0 else 1 - core)
                columns = pl.ds(pl.multiple_of(place * 512, 512), 512)
                out_refs[side][by] = jnp.dot(
                    inner[...], weights[:, columns], preferred_element_type=jnp.float32
                ).astype(jnp.bfloat16)


def filter_scratch(halo, taps):
    return [
        pltpu.VMEM((halo + HALF + 16, 1536), jnp.float32),
        pltpu.VMEM((halo + HALF, 512), jnp.float32),
        pltpu.VMEM((9, 8, LANES) if taps == 7 else (9, HALF + 128, LANES), jnp.float32),
    ]


def mix_kernel(moves, halo, taps, outs, index_ref, before_ref, main_ref, feat_ref, filter_ref, skip_ref, *refs):
    count = 1 + max(m[0] for m in moves)
    ws, refs = refs[:count], refs[count:]
    out_refs, refs = refs[:outs], refs[outs:]
    shaped, gated, copies8, inner, weights, w_sems = refs
    copies = fetch(moves, ws, weights, index_ref, w_sems)
    for copy in copies:
        copy.start()
    filter_rows(halo, taps, before_ref, main_ref, feat_ref, filter_ref, skip_ref, inner, shaped, gated, copies8)
    for copy in copies:
        copy.wait()
    product_rows(outs, index_ref, inner, weights, out_refs)


def mix_out(index, before, main, feat, taps, skip, weights, moves, halo, out_shapes):
    any_space = pl.BlockSpec(memory_space=pl.ANY)
    vmem = pl.BlockSpec(memory_space=pltpu.VMEM)
    length = taps.shape[0]
    return pl.pallas_call(
        functools.partial(mix_kernel, moves, halo, length, len(out_shapes)),
        out_shape=[jax.ShapeDtypeStruct(s, jnp.bfloat16) for s in out_shapes],
        in_specs=[pl.BlockSpec(memory_space=pltpu.SMEM)] + [vmem] * 5 + [any_space] * len(weights),
        out_specs=[vmem] * len(out_shapes),
        scratch_shapes=filter_scratch(halo, length)
        + [
            pltpu.VMEM((HALF, 512), jnp.bfloat16),
            pltpu.VMEM((512, 4096), jnp.bfloat16),
            pltpu.SemaphoreType.DMA((len(moves),)),
        ],
        compiler_params=pltpu.CompilerParams(vmem_limit_bytes=48 * 1024 * 1024),
        cost_estimate=pl.CostEstimate(flops=2 * HALF * 512 * 4096, bytes_accessed=6 * 2**20, transcendentals=0),
    )(index, before, main, feat, taps, skip, *weights)


def filter_kernel(halo, taps, before_ref, main_ref, feat_ref, filter_ref, skip_ref, inner, shaped, gated, copies8):
    filter_rows(halo, taps, before_ref, main_ref, feat_ref, filter_ref, skip_ref, inner, shaped, gated, copies8)


def filtered(before, main, feat, taps, skip, halo):
    vmem = pl.BlockSpec(memory_space=pltpu.VMEM)
    length = taps.shape[0]
    return pl.pallas_call(
        functools.partial(filter_kernel, halo, length),
        out_shape=jax.ShapeDtypeStruct((HALF, 512), jnp.bfloat16),
        in_specs=[vmem] * 5,
        out_specs=vmem,
        scratch_shapes=filter_scratch(halo, length),
        compiler_params=pltpu.CompilerParams(vmem_limit_bytes=24 * 1024 * 1024),
        cost_estimate=pl.CostEstimate(flops=2 * HALF * 512 * 4096 * 3, bytes_accessed=3 * 2**20, transcendentals=0),
    )(before, main, feat, taps, skip)


def product_kernel(moves, outs, index_ref, inner, weight_ref, *refs):
    out_refs, (weights, w_sems) = refs[:outs], refs[outs:]
    copies = fetch(moves, [weight_ref], weights, index_ref, w_sems)
    for copy in copies:
        copy.start()
    for copy in copies:
        copy.wait()
    product_rows(outs, index_ref, inner, weights, out_refs)


def project_out(index, inner, weight, moves, out_shapes):
    vmem = pl.BlockSpec(memory_space=pltpu.VMEM)
    return pl.pallas_call(
        functools.partial(product_kernel, moves, len(out_shapes)),
        out_shape=[jax.ShapeDtypeStruct(s, jnp.bfloat16) for s in out_shapes],
        in_specs=[pl.BlockSpec(memory_space=pltpu.SMEM), vmem, pl.BlockSpec(memory_space=pl.ANY)],
        out_specs=[vmem] * len(out_shapes),
        scratch_shapes=[pltpu.VMEM((512, 4096), jnp.bfloat16), pltpu.SemaphoreType.DMA((len(moves),))],
        compiler_params=pltpu.CompilerParams(vmem_limit_bytes=48 * 1024 * 1024),
        cost_estimate=pl.CostEstimate(flops=2 * HALF * 512 * 4096, bytes_accessed=6 * 2**20, transcendentals=0),
    )(index, inner, weight)


def per_device(hidden, norm_gain, in_weight, feat_filter, se_filter, mr_filter, skip_gain, out_weight):
    xl, y, core, z, xh = (lax.axis_index(a) for a in AXES)
    behind = lambda place, by: (place - by) % 4
    gains = norm_gain.reshape(2, 8, 512)
    ways = (1, -1, 2)
    other_core = lambda value: shift(value, "core", 1)
    gather = lambda value, axes: by_rows(lax.all_gather(by_rows(value), axes, axis=0, tiled=False))

    side_by_side = lambda w, o: jnp.concatenate([w.reshape(256, 1536), o[:256], o[256:]], axis=1)

    whole = lax.all_gather(hidden, ("z", "xh"), axis=0, tiled=False)

    m = side_by_side(in_weight[0], out_weight[0])
    m_xl = shift(m, "xl", 1)
    m_xl, w1, o1, *m_y = together(
        m_xl, swap(in_weight[1]), swap(after(out_weight[1], m_xl)), *[shift(m, "y", by) for by in ways]
    )
    rest = shift(jnp.stack([v[:, CUT:] for v in m_y]), "xl", 1)
    most = [shift(m_xl[:, :CUT], "y", by) for by in ways]
    rows = norm_rows(jnp.arange(8, dtype=jnp.int32), gains[0], [whole])
    rest, *more = together(rest, *most, *rows, *[other_core(after(v, most[0])) for v in (m, m_xl, *m_y)])
    most, rows, far = more[:3], more[3:5], more[5:]
    w_list = [m, m_xl, *m_y, *far, rest, *most] + [other_core(v) for v in (rest, *most)]
    w_moves, q_moves, slots = [], [], [z, core]

    def take(number, lead, at_xl, at_y, at_core, low, high):
        w_moves.append((number, lead, 0, min(high, 1536) - low, len(slots), low, True))
        if high == 2048:
            for half in range(2):
                q_moves.append((number, lead, 1536 + 256 * half - low, 256, len(slots), 256 * half, False))
        slots.append(at_xl * 8 + at_y * 2 + at_core)

    for number, c in ((0, core), (5, 1 - core)):
        take(number, None, xl, y, c, 0, 2048)
        take(number + 1, None, 1 - xl, y, c, 0, 2048)
        for e, by in enumerate(ways):
            take(number + 2 + e, None, xl, behind(y, by), c, 0, 2048)
    for number, c in ((10, core), (14, 1 - core)):
        for e, by in enumerate(ways):
            take(number, e, 1 - xl, behind(y, by), c, CUT, 2048)
            take(number + 1 + e, None, 1 - xl, behind(y, by), c, 0, CUT)
    q_index = jnp.stack(slots).astype(jnp.int32)
    q_list = w_list[:15]

    w1 = gather(after(w1.reshape(256, 1536), rest, *most), ("xh", "xl", "y"))
    o1 = gather(o1, ("xh", "xl", "y"))
    small = jnp.concatenate([feat_filter[1].reshape(9, 512), skip_gain[1:2], mr_filter], axis=0)

    low, high, tail = project_in(q_index, rows, w_list, w_moves, 16)
    base, small = after((hidden, small), low)
    base, small = swap(base), swap(small)
    tail = from_behind(tail, ("xl", "y", "core"))

    def first_parts(before, main):
        parts = mix_out(
            q_index, before, main, feat_filter[0].reshape(9, 512), se_filter, skip_gain[0:1], q_list, q_moves, 16,
            [(HALF, 1024)] * 4,
        )
        return parts[0], [shift(part, "z", by) for by, part in ((1, parts[1]), (-1, parts[3]), (2, parts[2]))]

    def over_z(own, received):
        total = own.astype(jnp.float32)
        for value in received:
            total = total + value.astype(jnp.float32)
        total = total.astype(jnp.bfloat16)
        pick = lambda c: jnp.where(c == 0, total[:, :512], total[:, 512:])
        mine, others = pick(core), pick(1 - core)
        return mine, [
            lax.ppermute(mine, ("core", "xh"), [(1, 0), (2, 3)]),
            lax.ppermute(others, ("core", "xh"), [(1, 2), (2, 1)]),
            lax.ppermute(others, ("core", "xh"), [(0, 2), (3, 1)]),
        ]

    def over_x(mine, received, rows):
        kept = jnp.where(core == xh, mine, jnp.zeros_like(mine))
        current = base[rows : rows + HALF].astype(jnp.float32) + kept.astype(jnp.float32)
        for value in received:
            current = current + value.astype(jnp.float32)
        return current.astype(jnp.bfloat16)

    own_high, high_z = first_parts(low, high)
    own_low, low_z = first_parts(tail, low)
    mine_high, high_x = over_z(own_high, high_z)
    *low_z, one, two, three = together(*low_z, *high_x)
    high = over_x(mine_high, (one, two, three), HALF)
    mine_low, low_x = over_z(own_low, low_z)
    high = after(high, low_x[2])
    high_near = [shift(high, "z", by) for by in ways]
    one, two, three, *high_near = together(*low_x, *high_near)
    low = over_x(mine_low, (one, two, three), 0)

    places = [(p, (p // 4 % 2) * 8 + (p % 4) * 2 + p // 8) for p in range(16)]
    w_moves = [(0, p, 0, 1536, None, 0, True, block) for p, block in places]
    p_moves = [(0, p, 0, 256, None, 0, False, block) for p, block in places]
    x_index = jnp.stack([behind(z, by) * 2 + c for c in (core, 1 - core) for by in (0, *ways)]).astype(jnp.int32)

    def normed(near):
        return norm_rows(x_index, gains[1], near + [other_core(v) for v in near])

    high_near = [high] + high_near
    low_near = [low] + [shift(low, "z", by) for by in ways]
    rows = normed(low_near) + normed(high_near)
    p_low, p_high, tail = project_in(q_index, rows, [w1], w_moves, 144)
    tail = from_behind(tail, ("xl", "y", "xh"))

    def second_filter(before, main):
        return filtered(before, main, small[:9], small[10:], small[9:10], 144)

    def second_parts(inner):
        return project_out(q_index, inner, o1, p_moves, [(4, HALF, 512)] * 2)

    def second_z(own, theirs):
        both = (own.astype(jnp.float32) + theirs.astype(jnp.float32)).astype(jnp.bfloat16)
        return both[0], [shift(both[at], "z", by) for by, at in ((1, 1), (-1, 3), (2, 2))]

    def second_sum(own, received, rows):
        total = rows.astype(jnp.float32) + own.astype(jnp.float32)
        for value in received:
            total = total + value.astype(jnp.float32)
        return swap(total.astype(jnp.bfloat16))

    inner_high = second_filter(p_low, p_high)
    inner_low = second_filter(tail, p_low)
    inner_high, inner_low = together(inner_high, inner_low)
    own_high, theirs_high = second_parts(inner_high)
    theirs_high = other_core(theirs_high)
    own_high, high_z = second_z(own_high, theirs_high)
    own_low, theirs_low = second_parts(inner_low)
    theirs_low = other_core(theirs_low)
    high = second_sum(own_high, high_z, high)
    own_low, low_z = second_z(own_low, theirs_low)
    low = second_sum(own_low, low_z, low)
    return jnp.concatenate([low, high], axis=0)


def solution(mesh):
    fine = Mesh(np.asarray(mesh.devices).reshape(2, 4, 2, 4, 2), AXES)
    ctx, ch = ("xl", "y", "core"), ("z", "xh")
    return jax.shard_map(
        per_device,
        mesh=fine,
        in_specs=(
            P(ctx, ch),
            P(),
            P(None, ctx, None, ch),
            P(None, None, None, ch),
            P(None, ch),
            P(None, ch),
            P(None, ch),
            P(None, ch, ctx),
        ),
        out_specs=P(ctx, ch),
        check_vma=False,
    )
```

```python
import functools

import jax
import jax.numpy as jnp
import numpy as np
from jax import lax
from jax.experimental.layout import Layout, with_layout_constraint
from jax.experimental import pallas as pl
from jax.experimental.pallas import tpu as pltpu
from jax.sharding import Mesh, PartitionSpec as P

AXES = ("xl", "y", "core", "z", "xh")
HALF = 256
CUT = 1280
LANES = 128


def shift(value, axis, by):
    size = lax.axis_size(axis)
    return lax.ppermute(value, axis, [(i, (i + by) % size) for i in range(size)])


def swap(value):
    moved = lax.ppermute(value, ("core", "xh"), [(1, 2), (2, 1)])
    same = lax.axis_index("core") == lax.axis_index("xh")
    return jnp.where(same, value, moved)


def from_behind(value, axes):
    return lax.ppermute(value, axes, [(i, i + 1) for i in range(15)])


def by_rows(value):
    return with_layout_constraint(value, Layout(major_to_minor=tuple(range(value.ndim))))


def after(value, *others):
    return lax.optimization_barrier((value, *others))[0]


def together(*values):
    return lax.optimization_barrier(values)


def fetch(moves, sources, target, index_ref, semaphores):
    copies = []
    for number, (source, lead, lane, width, slot, other, by_rows, *fixed) in enumerate(moves):
        block = fixed[0] * 256 if slot is None else pl.multiple_of(index_ref[slot] * 256, 256)
        ref = sources[source]
        if lead is not None:
            ref = ref.at[lead]
        if by_rows:
            piece = target.at[pl.ds(block, 256), other : other + width]
        else:
            piece = target.at[other : other + ref.shape[0], pl.ds(block, 256)]
        copies.append(pltpu.make_async_copy(ref.at[:, lane : lane + width], piece, semaphores.at[number]))
    return copies


def norm_pieces(loads, places, raw, gain_ref, normed, squares):
    squares[...] = jnp.zeros_like(squares)
    for load, (j, start, count), place in zip(loads, pieces_of(len(loads)), places):
        load.wait()
        lanes = pl.ds(pl.multiple_of(place * 512, 512), 512)
        gain = gain_ref[pl.ds(place, 1), :]

        @pl.loop(0, count // 64)
        def _(step):
            rows = pl.ds(pl.multiple_of(start + step * 64, 64), 64)
            x = raw[j, rows, :].astype(jnp.float32)
            normed[rows, lanes] = (x * gain).astype(jnp.bfloat16)
            q = x * x
            squares[rows, :] += (q[:, :128] + q[:, 128:256]) + (q[:, 256:384] + q[:, 384:])

    squares[:, :1] = lax.rsqrt(jnp.sum(squares[...], axis=1, keepdims=True) * (1.0 / 4096) + 1e-06)


def pieces_of(count):
    rows = 8 * 2 * HALF // count
    return [(j % 8, j // 8 * rows, rows) for j in range(count)]


def in_kernel(moves, sources, halo, index_ref, place_ref, gain_ref, *refs):
    xs, refs = refs[:sources], refs[sources:]
    count = 1 + max(m[0] for m in moves)
    ws, refs = refs[:count], refs[count:]
    out_refs, (tail_ref, raw, normed, weights, squares, x_sems, w_sems) = refs[:2], refs[2:]
    xs = [xs[0].at[j] for j in range(8)] if sources == 1 else xs
    loads = [
        pltpu.make_async_copy(x, raw.at[j, start : start + rows], x_sems.at[number])
        for number, (x, (j, start, rows)) in enumerate(zip(xs, pieces_of(len(xs))))
    ]
    copies = fetch(moves, ws, weights, index_ref, w_sems)
    for copy in loads + copies:
        copy.start()
    norm_pieces(loads, [place_ref[j] for j in range(len(xs))], raw, gain_ref, normed, squares)
    for copy in copies:
        copy.wait()

    @pl.loop(0, 6)
    def _(step):
        lanes = pl.ds(pl.multiple_of(step * 256, 256), 256)
        product = jnp.dot(normed[...], weights[:, lanes], preferred_element_type=jnp.float32)
        product = (product * squares[:, :1]).astype(jnp.bfloat16)
        for part, out_ref in enumerate(out_refs):
            out_ref[:, lanes] = product[part * HALF : (part + 1) * HALF]

    last = out_refs[-1]
    tail_ref[:halo, :] = last[HALF - halo :, 512:]
    tail_ref[halo:, :512] = last[HALF - 16 :, :512]
    tail_ref[halo:, 512:] = jnp.zeros((16, 512), jnp.bfloat16)


def project_in(index, places, gain, pieces, weights, moves, halo):
    any_space = pl.BlockSpec(memory_space=pl.ANY)
    vmem = pl.BlockSpec(memory_space=pltpu.VMEM)
    smem = pl.BlockSpec(memory_space=pltpu.SMEM)
    return pl.pallas_call(
        functools.partial(in_kernel, moves, len(pieces), halo),
        out_shape=[jax.ShapeDtypeStruct((HALF, 1536), jnp.bfloat16)] * 2
        + [jax.ShapeDtypeStruct((halo + 16, 1024), jnp.bfloat16)],
        in_specs=[smem, smem, vmem] + [any_space] * (len(pieces) + len(weights)),
        out_specs=[vmem] * 3,
        scratch_shapes=[
            pltpu.VMEM((8, 2 * HALF, 512), jnp.bfloat16),
            pltpu.VMEM((2 * HALF, 4096), jnp.bfloat16),
            pltpu.VMEM((4096, 1536), jnp.bfloat16),
            pltpu.VMEM((2 * HALF, LANES), jnp.float32),
            pltpu.SemaphoreType.DMA((16,)),
            pltpu.SemaphoreType.DMA((len(moves),)),
        ],
        compiler_params=pltpu.CompilerParams(vmem_limit_bytes=50 * 1024 * 1024),
        cost_estimate=pl.CostEstimate(flops=4 * HALF * 4096 * 1536, bytes_accessed=18 * 2**20, transcendentals=0),
    )(index, places, gain, *pieces, *weights)


def filter_rows(halo, taps, before_ref, main_ref, feat_ref, filter_ref, skip_ref, inner, shaped, gated, copies8):
    total = halo + HALF

    if before_ref.shape[1] == 1024:
        shaped[:16, :512] = before_ref[halo:, :512].astype(jnp.float32)
        shaped[:halo, 512:] = before_ref[:halo, :].astype(jnp.float32)
    else:
        shaped[:16, :512] = before_ref[HALF - 16 :, :512].astype(jnp.float32)
        shaped[:halo, 512:] = before_ref[HALF - halo :, 512:].astype(jnp.float32)
    shaped[16 : 16 + HALF, :512] = main_ref[:, :512].astype(jnp.float32)
    shaped[halo:total, 512:] = main_ref[:, 512:].astype(jnp.float32)

    def feature(start, size, s, lanes):
        value = None
        for j in range(3):
            tap = feat_ref[3 * j + s : 3 * j + s + 1, lanes]
            low = s * 512 + lanes.start
            term = tap * shaped[start - j : start - j + size, low : low + LANES]
            value = term if value is None else value + term
        return value

    for lane in range(0, 512, LANES):
        lanes = slice(lane, lane + LANES)
        for start in range(8, total, 64):
            size = min(64, total - start)
            gated[start : start + size, lanes] = feature(start, size, 1, lanes) * feature(start, size, 2, lanes)
        gated[:8, lanes] = jnp.zeros((8, LANES), jnp.float32)

    if taps == 7:
        for lane in range(0, 512, LANES):
            lanes = slice(lane, lane + LANES)
            for start in range(0, HALF, 64):
                own = gated[halo + start : halo + start + 64, lanes]
                value = (skip_ref[:1, lanes] + filter_ref[:1, lanes]) * own
                for j in range(1, taps):
                    value = value + filter_ref[j : j + 1, lanes] * gated[halo + start - j : halo + start - j + 64, lanes]
                inner[start : start + 64, lanes] = (feature(16 + start, 64, 0, lanes) * value).astype(jnp.bfloat16)
    else:
        for lane in range(0, 512, LANES):
            lanes = slice(lane, lane + LANES)
            for r in range(8):
                for start in range(0, HALF + 128, 128):
                    copies8[r, start : start + 128, :] = gated[16 + start - r : 16 + start - r + 128, lanes]

            @pl.loop(0, HALF // 128)
            def _(step):
                base = pl.multiple_of(step * 128, 128)
                value = jnp.zeros((128, LANES), jnp.float32)
                for r in range(8):
                    for a in range(0, 16, 4):
                        window = copies8[r, pl.ds(pl.multiple_of(base + 128 - 8 * (a + 3), 8), 128 + 24), :]
                        for b in range(4):
                            tap = filter_ref[8 * (a + b) + r : 8 * (a + b) + r + 1, lanes]
                            low = 8 * (3 - b)
                            value = value + tap * window[low : low + 128]
                copies8[8, pl.ds(base, 128), :] = value

            for start in range(0, HALF, 64):
                own = gated[halo + start : halo + start + 64, lanes]
                value = copies8[8, start : start + 64, :] + skip_ref[:1, lanes] * own
                inner[start : start + 64, lanes] = (feature(16 + start, 64, 0, lanes) * value).astype(jnp.bfloat16)


def product_rows(outs, index_ref, inner, weights, out_refs):
    z = index_ref[0]
    core = index_ref[1]
    for by in range(4):
        block = lax.rem(z + by, 4)
        if outs == 4:
            columns = pl.ds(pl.multiple_of(block * 1024, 1024), 1024)
            out_refs[by][...] = jnp.dot(
                inner[...], weights[:, columns], preferred_element_type=jnp.float32
            ).astype(jnp.bfloat16)
        else:
            for side in range(2):
                place = block * 2 + (core if side == 0 else 1 - core)
                columns = pl.ds(pl.multiple_of(place * 512, 512), 512)
                out_refs[side][by] = jnp.dot(
                    inner[...], weights[:, columns], preferred_element_type=jnp.float32
                ).astype(jnp.bfloat16)


def filter_scratch(halo, taps):
    return [
        pltpu.VMEM((halo + HALF + 16, 1536), jnp.float32),
        pltpu.VMEM((halo + HALF, 512), jnp.float32),
        pltpu.VMEM((9, 8, LANES) if taps == 7 else (9, HALF + 128, LANES), jnp.float32),
    ]


def mix_kernel(moves, halo, taps, outs, index_ref, before_ref, main_ref, feat_ref, filter_ref, skip_ref, *refs):
    count = 1 + max(m[0] for m in moves)
    ws, refs = refs[:count], refs[count:]
    out_refs, refs = refs[:outs], refs[outs:]
    shaped, gated, copies8, inner, weights, w_sems = refs
    copies = fetch(moves, ws, weights, index_ref, w_sems)
    for copy in copies:
        copy.start()
    filter_rows(halo, taps, before_ref, main_ref, feat_ref, filter_ref, skip_ref, inner, shaped, gated, copies8)
    for copy in copies:
        copy.wait()
    product_rows(outs, index_ref, inner, weights, out_refs)


def mix_out(index, before, main, feat, taps, skip, weights, moves, halo, out_shapes):
    any_space = pl.BlockSpec(memory_space=pl.ANY)
    vmem = pl.BlockSpec(memory_space=pltpu.VMEM)
    length = taps.shape[0]
    return pl.pallas_call(
        functools.partial(mix_kernel, moves, halo, length, len(out_shapes)),
        out_shape=[jax.ShapeDtypeStruct(s, jnp.bfloat16) for s in out_shapes],
        in_specs=[pl.BlockSpec(memory_space=pltpu.SMEM)] + [vmem] * 5 + [any_space] * len(weights),
        out_specs=[vmem] * len(out_shapes),
        scratch_shapes=filter_scratch(halo, length)
        + [
            pltpu.VMEM((HALF, 512), jnp.bfloat16),
            pltpu.VMEM((512, 4096), jnp.bfloat16),
            pltpu.SemaphoreType.DMA((len(moves),)),
        ],
        compiler_params=pltpu.CompilerParams(vmem_limit_bytes=48 * 1024 * 1024),
        cost_estimate=pl.CostEstimate(flops=2 * HALF * 512 * 4096, bytes_accessed=6 * 2**20, transcendentals=0),
    )(index, before, main, feat, taps, skip, *weights)


def filter_kernel(halo, taps, before_ref, main_ref, feat_ref, filter_ref, skip_ref, inner, shaped, gated, copies8):
    filter_rows(halo, taps, before_ref, main_ref, feat_ref, filter_ref, skip_ref, inner, shaped, gated, copies8)


def filtered(before, main, feat, taps, skip, halo):
    vmem = pl.BlockSpec(memory_space=pltpu.VMEM)
    length = taps.shape[0]
    return pl.pallas_call(
        functools.partial(filter_kernel, halo, length),
        out_shape=jax.ShapeDtypeStruct((HALF, 512), jnp.bfloat16),
        in_specs=[vmem] * 5,
        out_specs=vmem,
        scratch_shapes=filter_scratch(halo, length),
        compiler_params=pltpu.CompilerParams(vmem_limit_bytes=24 * 1024 * 1024),
        cost_estimate=pl.CostEstimate(flops=2 * HALF * 512 * 4096 * 3, bytes_accessed=3 * 2**20, transcendentals=0),
    )(before, main, feat, taps, skip)


def product_kernel(moves, outs, index_ref, inner, weight_ref, *refs):
    out_refs, (weights, w_sems) = refs[:outs], refs[outs:]
    copies = fetch(moves, [weight_ref], weights, index_ref, w_sems)
    for copy in copies:
        copy.start()
    for copy in copies:
        copy.wait()
    product_rows(outs, index_ref, inner, weights, out_refs)


def project_out(index, inner, weight, moves, out_shapes):
    vmem = pl.BlockSpec(memory_space=pltpu.VMEM)
    return pl.pallas_call(
        functools.partial(product_kernel, moves, len(out_shapes)),
        out_shape=[jax.ShapeDtypeStruct(s, jnp.bfloat16) for s in out_shapes],
        in_specs=[pl.BlockSpec(memory_space=pltpu.SMEM), vmem, pl.BlockSpec(memory_space=pl.ANY)],
        out_specs=[vmem] * len(out_shapes),
        scratch_shapes=[pltpu.VMEM((512, 4096), jnp.bfloat16), pltpu.SemaphoreType.DMA((len(moves),))],
        compiler_params=pltpu.CompilerParams(vmem_limit_bytes=48 * 1024 * 1024),
        cost_estimate=pl.CostEstimate(flops=2 * HALF * 512 * 4096, bytes_accessed=6 * 2**20, transcendentals=0),
    )(index, inner, weight)


def per_device(hidden, norm_gain, in_weight, feat_filter, se_filter, mr_filter, skip_gain, out_weight):
    xl, y, core, z, xh = (lax.axis_index(a) for a in AXES)
    behind = lambda place, by: (place - by) % 4
    gains = norm_gain.reshape(2, 8, 512)
    ways = (1, -1, 2)
    other_core = lambda value: shift(value, "core", 1)
    gather = lambda value, axes: by_rows(lax.all_gather(by_rows(value), axes, axis=0, tiled=False))

    side_by_side = lambda w, o: jnp.concatenate([w.reshape(256, 1536), o[:256], o[256:]], axis=1)

    whole = lax.all_gather(hidden, ("z", "xh"), axis=0, tiled=False)

    m = side_by_side(in_weight[0], out_weight[0])
    m_xl = shift(m, "xl", 1)
    m_xl, w1, o1, *m_y = together(
        m_xl, swap(in_weight[1]), swap(after(out_weight[1], m_xl)), *[shift(m, "y", by) for by in ways]
    )
    rest = shift(jnp.stack([v[:, CUT:] for v in m_y]), "xl", 1)
    most = [shift(m_xl[:, :CUT], "y", by) for by in ways]
    rest, *more = together(rest, *most, *[other_core(after(v, most[0])) for v in (m, m_xl, *m_y)])
    most, far = more[:3], more[3:]
    w_list = [m, m_xl, *m_y, *far, rest, *most] + [other_core(v) for v in (rest, *most)]
    w_moves, q_moves, slots = [], [], [z, core]

    def take(number, lead, at_xl, at_y, at_core, low, high):
        w_moves.append((number, lead, 0, min(high, 1536) - low, len(slots), low, True))
        if high == 2048:
            for half in range(2):
                q_moves.append((number, lead, 1536 + 256 * half - low, 256, len(slots), 256 * half, False))
        slots.append(at_xl * 8 + at_y * 2 + at_core)

    for number, c in ((0, core), (5, 1 - core)):
        take(number, None, xl, y, c, 0, 2048)
        take(number + 1, None, 1 - xl, y, c, 0, 2048)
        for e, by in enumerate(ways):
            take(number + 2 + e, None, xl, behind(y, by), c, 0, 2048)
    for number, c in ((10, core), (14, 1 - core)):
        for e, by in enumerate(ways):
            take(number, e, 1 - xl, behind(y, by), c, CUT, 2048)
            take(number + 1 + e, None, 1 - xl, behind(y, by), c, 0, CUT)
    q_index = jnp.stack(slots).astype(jnp.int32)
    q_list = w_list[:15]

    w1 = gather(after(w1.reshape(256, 1536), rest, *most), ("xh", "xl", "y"))
    o1 = gather(o1, ("xh", "xl", "y"))
    small = jnp.concatenate([feat_filter[1].reshape(9, 512), skip_gain[1:2], mr_filter], axis=0)

    places = jnp.arange(8, dtype=jnp.int32)
    low, high, tail = project_in(q_index, places, gains[0], [whole], w_list, w_moves, 16)
    base, small = after((hidden, small), low)
    base, small = swap(base), swap(small)
    tail = from_behind(tail, ("xl", "y", "core"))

    def first_parts(before, main):
        parts = mix_out(
            q_index, before, main, feat_filter[0].reshape(9, 512), se_filter, skip_gain[0:1], q_list, q_moves, 16,
            [(HALF, 1024)] * 4,
        )
        return parts[0], [shift(part, "z", by) for by, part in ((1, parts[1]), (-1, parts[3]), (2, parts[2]))]

    def over_z(own, received):
        total = own.astype(jnp.float32)
        for value in received:
            total = total + value.astype(jnp.float32)
        total = total.astype(jnp.bfloat16)
        pick = lambda c: jnp.where(c == 0, total[:, :512], total[:, 512:])
        mine, others = pick(core), pick(1 - core)
        return mine, [
            lax.ppermute(mine, ("core", "xh"), [(1, 0), (2, 3)]),
            lax.ppermute(others, ("core", "xh"), [(1, 2), (2, 1)]),
            lax.ppermute(others, ("core", "xh"), [(0, 2), (3, 1)]),
        ]

    def over_x(mine, received, rows):
        kept = jnp.where(core == xh, mine, jnp.zeros_like(mine))
        current = base[rows : rows + HALF].astype(jnp.float32) + kept.astype(jnp.float32)
        for value in received:
            current = current + value.astype(jnp.float32)
        return current.astype(jnp.bfloat16)

    own_high, high_z = first_parts(low, high)
    own_low, low_z = first_parts(tail, low)
    mine_high, high_x = over_z(own_high, high_z)
    *low_z, one, two, three = together(*low_z, *high_x)
    high = over_x(mine_high, (one, two, three), HALF)
    mine_low, low_x = over_z(own_low, low_z)
    high = after(high, low_x[2])
    high_near = [shift(high, "z", by) for by in ways]
    one, two, three, *high_near = together(*low_x, *high_near)
    low = over_x(mine_low, (one, two, three), 0)

    places = [(p, (p // 4 % 2) * 8 + (p % 4) * 2 + p // 8) for p in range(16)]
    w_moves = [(0, p, 0, 1536, None, 0, True, block) for p, block in places]
    p_moves = [(0, p, 0, 256, None, 0, False, block) for p, block in places]
    x_index = jnp.stack([behind(z, by) * 2 + c for c in (core, 1 - core) for by in (0, *ways)] * 2).astype(jnp.int32)
    low_near = [low] + [shift(low, "z", by) for by in ways]
    high_near = [high] + high_near
    high_far = [other_core(v) for v in high_near]
    low_far = [other_core(v) for v in low_near]
    p_low, p_high, tail = project_in(
        q_index, x_index, gains[1], low_near + low_far + high_near + high_far, [w1], w_moves, 144
    )
    tail = from_behind(tail, ("xl", "y", "xh"))

    def second_filter(before, main):
        return filtered(before, main, small[:9], small[10:], small[9:10], 144)

    def second_parts(inner):
        return project_out(q_index, inner, o1, p_moves, [(4, HALF, 512)] * 2)

    def second_z(own, theirs):
        both = (own.astype(jnp.float32) + theirs.astype(jnp.float32)).astype(jnp.bfloat16)
        return both[0], [shift(both[at], "z", by) for by, at in ((1, 1), (-1, 3), (2, 2))]

    def second_sum(own, received, rows):
        total = rows.astype(jnp.float32) + own.astype(jnp.float32)
        for value in received:
            total = total + value.astype(jnp.float32)
        return swap(total.astype(jnp.bfloat16))

    inner_high = second_filter(p_low, p_high)
    inner_low = second_filter(tail, p_low)
    inner_high, inner_low = together(inner_high, inner_low)
    own_high, theirs_high = second_parts(inner_high)
    theirs_high = other_core(theirs_high)
    own_high, high_z = second_z(own_high, theirs_high)
    own_low, theirs_low = second_parts(inner_low)
    theirs_low = other_core(theirs_low)
    high = second_sum(own_high, high_z, high)
    own_low, low_z = second_z(own_low, theirs_low)
    low = second_sum(own_low, low_z, low)
    return jnp.concatenate([low, high], axis=0)


def solution(mesh):
    fine = Mesh(np.asarray(mesh.devices).reshape(2, 4, 2, 4, 2), AXES)
    ctx, ch = ("xl", "y", "core"), ("z", "xh")
    return jax.shard_map(
        per_device,
        mesh=fine,
        in_specs=(
            P(ctx, ch),
            P(),
            P(None, ctx, None, ch),
            P(None, None, None, ch),
            P(None, ch),
            P(None, ch),
            P(None, ch),
            P(None, ch, ctx),
        ),
        out_specs=P(ctx, ch),
        check_vma=False,
    )
```

```python
import functools

import jax
import jax.numpy as jnp
import numpy as np
from jax import lax
from jax.experimental.layout import Layout, with_layout_constraint
from jax.experimental import pallas as pl
from jax.experimental.pallas import tpu as pltpu
from jax.sharding import Mesh, PartitionSpec as P

AXES = ("xl", "y", "core", "z", "xh")
HALF = 256
CUT = 1280
LANES = 128


def shift(value, axis, by):
    size = lax.axis_size(axis)
    return lax.ppermute(value, axis, [(i, (i + by) % size) for i in range(size)])


def swap(value):
    moved = lax.ppermute(value, ("core", "xh"), [(1, 2), (2, 1)])
    same = lax.axis_index("core") == lax.axis_index("xh")
    return jnp.where(same, value, moved)


def from_behind(value, axes):
    return lax.ppermute(value, axes, [(i, i + 1) for i in range(15)])


def by_rows(value):
    return with_layout_constraint(value, Layout(major_to_minor=tuple(range(value.ndim))))


def after(value, *others):
    return lax.optimization_barrier((value, *others))[0]


def together(*values):
    return lax.optimization_barrier(values)


def fetch(moves, sources, target, index_ref, semaphores):
    copies = []
    for number, (source, lead, lane, width, slot, other, by_rows, *fixed) in enumerate(moves):
        block = fixed[0] * 256 if slot is None else pl.multiple_of(index_ref[slot] * 256, 256)
        start = fixed[1] if len(fixed) > 1 else 0
        ref = sources[source]
        if lead is not None:
            ref = ref.at[lead]
        if by_rows:
            piece = target.at[pl.ds(pl.multiple_of(block + start, 128), ref.shape[0]), other : other + width]
        else:
            piece = target.at[other : other + ref.shape[0], pl.ds(block, 256)]
        copies.append(pltpu.make_async_copy(ref.at[:, lane : lane + width], piece, semaphores.at[number]))
    return copies


def norm_pieces(loads, places, raw, gain_ref, normed, squares):
    squares[...] = jnp.zeros_like(squares)
    for load, (j, start, count), place in zip(loads, pieces_of(len(loads)), places):
        load.wait()
        lanes = pl.ds(pl.multiple_of(place * 512, 512), 512)
        gain = gain_ref[pl.ds(place, 1), :]

        @pl.loop(0, count // 64)
        def _(step):
            rows = pl.ds(pl.multiple_of(start + step * 64, 64), 64)
            x = raw[j, rows, :].astype(jnp.float32)
            normed[rows, lanes] = (x * gain).astype(jnp.bfloat16)
            q = x * x
            squares[rows, :] += (q[:, :128] + q[:, 128:256]) + (q[:, 256:384] + q[:, 384:])

    squares[:, :1] = lax.rsqrt(jnp.sum(squares[...], axis=1, keepdims=True) * (1.0 / 4096) + 1e-06)


def pieces_of(count):
    rows = 8 * 2 * HALF // count
    return [(j % 8, j // 8 * rows, rows) for j in range(count)]


def in_kernel(moves, sources, halo, index_ref, place_ref, gain_ref, *refs):
    xs, refs = refs[:sources], refs[sources:]
    count = 1 + max(m[0] for m in moves)
    ws, refs = refs[:count], refs[count:]
    out_refs, (tail_ref, raw, normed, weights, squares, x_sems, w_sems) = refs[:2], refs[2:]
    xs = [xs[0].at[j // 2, j % 2] for j in range(8)] if sources == 1 else xs
    loads = [
        pltpu.make_async_copy(x, raw.at[j, start : start + rows], x_sems.at[number])
        for number, (x, (j, start, rows)) in enumerate(zip(xs, pieces_of(len(xs))))
    ]
    copies = fetch(moves, ws, weights, index_ref, w_sems)
    for copy in loads + copies:
        copy.start()
    norm_pieces(loads, [place_ref[j] for j in range(len(xs))], raw, gain_ref, normed, squares)
    for copy in copies:
        copy.wait()

    @pl.loop(0, 6)
    def _(step):
        lanes = pl.ds(pl.multiple_of(step * 256, 256), 256)
        product = jnp.dot(normed[...], weights[:, lanes], preferred_element_type=jnp.float32)
        product = (product * squares[:, :1]).astype(jnp.bfloat16)
        for part, out_ref in enumerate(out_refs):
            out_ref[:, lanes] = product[part * HALF : (part + 1) * HALF]

    last = out_refs[-1]
    tail_ref[:halo, :] = last[HALF - halo :, 512:]
    tail_ref[halo:, :512] = last[HALF - 16 :, :512]
    tail_ref[halo:, 512:] = jnp.zeros((16, 512), jnp.bfloat16)


def project_in(index, places, gain, pieces, weights, moves, halo):
    any_space = pl.BlockSpec(memory_space=pl.ANY)
    vmem = pl.BlockSpec(memory_space=pltpu.VMEM)
    smem = pl.BlockSpec(memory_space=pltpu.SMEM)
    return pl.pallas_call(
        functools.partial(in_kernel, moves, len(pieces), halo),
        out_shape=[jax.ShapeDtypeStruct((HALF, 1536), jnp.bfloat16)] * 2
        + [jax.ShapeDtypeStruct((halo + 16, 1024), jnp.bfloat16)],
        in_specs=[smem, smem, vmem] + [any_space] * (len(pieces) + len(weights)),
        out_specs=[vmem] * 3,
        scratch_shapes=[
            pltpu.VMEM((8, 2 * HALF, 512), jnp.bfloat16),
            pltpu.VMEM((2 * HALF, 4096), jnp.bfloat16),
            pltpu.VMEM((4096, 1536), jnp.bfloat16),
            pltpu.VMEM((2 * HALF, LANES), jnp.float32),
            pltpu.SemaphoreType.DMA((16,)),
            pltpu.SemaphoreType.DMA((len(moves),)),
        ],
        compiler_params=pltpu.CompilerParams(vmem_limit_bytes=50 * 1024 * 1024),
        cost_estimate=pl.CostEstimate(flops=4 * HALF * 4096 * 1536, bytes_accessed=18 * 2**20, transcendentals=0),
    )(index, places, gain, *pieces, *weights)


def filter_rows(halo, taps, before_ref, main_ref, feat_ref, filter_ref, skip_ref, inner, shaped, gated, copies8):
    total = halo + HALF

    if before_ref.shape[1] == 1024:
        shaped[:16, :512] = before_ref[halo:, :512].astype(jnp.float32)
        shaped[:halo, 512:] = before_ref[:halo, :].astype(jnp.float32)
    else:
        shaped[:16, :512] = before_ref[HALF - 16 :, :512].astype(jnp.float32)
        shaped[:halo, 512:] = before_ref[HALF - halo :, 512:].astype(jnp.float32)
    shaped[16 : 16 + HALF, :512] = main_ref[:, :512].astype(jnp.float32)
    shaped[halo:total, 512:] = main_ref[:, 512:].astype(jnp.float32)

    def feature(start, size, s, lanes):
        value = None
        for j in range(3):
            tap = feat_ref[3 * j + s : 3 * j + s + 1, lanes]
            low = s * 512 + lanes.start
            term = tap * shaped[start - j : start - j + size, low : low + LANES]
            value = term if value is None else value + term
        return value

    for lane in range(0, 512, LANES):
        lanes = slice(lane, lane + LANES)
        for start in range(8, total, 64):
            size = min(64, total - start)
            gated[start : start + size, lanes] = feature(start, size, 1, lanes) * feature(start, size, 2, lanes)
        gated[:8, lanes] = jnp.zeros((8, LANES), jnp.float32)

    if taps == 7:
        for lane in range(0, 512, LANES):
            lanes = slice(lane, lane + LANES)
            for start in range(0, HALF, 64):
                own = gated[halo + start : halo + start + 64, lanes]
                value = (skip_ref[:1, lanes] + filter_ref[:1, lanes]) * own
                for j in range(1, taps):
                    value = value + filter_ref[j : j + 1, lanes] * gated[halo + start - j : halo + start - j + 64, lanes]
                inner[start : start + 64, lanes] = (feature(16 + start, 64, 0, lanes) * value).astype(jnp.bfloat16)
    else:
        for lane in range(0, 512, LANES):
            lanes = slice(lane, lane + LANES)
            for r in range(8):
                for start in range(0, HALF + 128, 128):
                    copies8[r, start : start + 128, :] = gated[16 + start - r : 16 + start - r + 128, lanes]

            @pl.loop(0, HALF // 128)
            def _(step):
                base = pl.multiple_of(step * 128, 128)
                value = jnp.zeros((128, LANES), jnp.float32)
                for r in range(8):
                    for a in range(0, 16, 4):
                        window = copies8[r, pl.ds(pl.multiple_of(base + 128 - 8 * (a + 3), 8), 128 + 24), :]
                        for b in range(4):
                            tap = filter_ref[8 * (a + b) + r : 8 * (a + b) + r + 1, lanes]
                            low = 8 * (3 - b)
                            value = value + tap * window[low : low + 128]
                copies8[8, pl.ds(base, 128), :] = value

            for start in range(0, HALF, 64):
                own = gated[halo + start : halo + start + 64, lanes]
                value = copies8[8, start : start + 64, :] + skip_ref[:1, lanes] * own
                inner[start : start + 64, lanes] = (feature(16 + start, 64, 0, lanes) * value).astype(jnp.bfloat16)


def product_rows(outs, index_ref, inner, weights, out_refs):
    z = index_ref[0]
    core = index_ref[1]
    for by in range(4):
        block = lax.rem(z + by, 4)
        if outs == 4:
            columns = pl.ds(pl.multiple_of(block * 1024, 1024), 1024)
            out_refs[by][...] = jnp.dot(
                inner[...], weights[:, columns], preferred_element_type=jnp.float32
            ).astype(jnp.bfloat16)
        else:
            for side in range(2):
                place = block * 2 + (core if side == 0 else 1 - core)
                columns = pl.ds(pl.multiple_of(place * 512, 512), 512)
                out_refs[side][by] = jnp.dot(
                    inner[...], weights[:, columns], preferred_element_type=jnp.float32
                ).astype(jnp.bfloat16)


def filter_scratch(halo, taps):
    return [
        pltpu.VMEM((halo + HALF + 16, 1536), jnp.float32),
        pltpu.VMEM((halo + HALF, 512), jnp.float32),
        pltpu.VMEM((9, 8, LANES) if taps == 7 else (9, HALF + 128, LANES), jnp.float32),
    ]


def mix_kernel(moves, halo, taps, outs, index_ref, before_ref, main_ref, feat_ref, filter_ref, skip_ref, *refs):
    count = 1 + max(m[0] for m in moves)
    ws, refs = refs[:count], refs[count:]
    out_refs, refs = refs[:outs], refs[outs:]
    shaped, gated, copies8, inner, weights, w_sems = refs
    copies = fetch(moves, ws, weights, index_ref, w_sems)
    for copy in copies:
        copy.start()
    filter_rows(halo, taps, before_ref, main_ref, feat_ref, filter_ref, skip_ref, inner, shaped, gated, copies8)
    for copy in copies:
        copy.wait()
    product_rows(outs, index_ref, inner, weights, out_refs)


def mix_out(index, before, main, feat, taps, skip, weights, moves, halo, out_shapes):
    any_space = pl.BlockSpec(memory_space=pl.ANY)
    vmem = pl.BlockSpec(memory_space=pltpu.VMEM)
    length = taps.shape[0]
    return pl.pallas_call(
        functools.partial(mix_kernel, moves, halo, length, len(out_shapes)),
        out_shape=[jax.ShapeDtypeStruct(s, jnp.bfloat16) for s in out_shapes],
        in_specs=[pl.BlockSpec(memory_space=pltpu.SMEM)] + [vmem] * 5 + [any_space] * len(weights),
        out_specs=[vmem] * len(out_shapes),
        scratch_shapes=filter_scratch(halo, length)
        + [
            pltpu.VMEM((HALF, 512), jnp.bfloat16),
            pltpu.VMEM((512, 4096), jnp.bfloat16),
            pltpu.SemaphoreType.DMA((len(moves),)),
        ],
        compiler_params=pltpu.CompilerParams(vmem_limit_bytes=48 * 1024 * 1024),
        cost_estimate=pl.CostEstimate(flops=2 * HALF * 512 * 4096, bytes_accessed=6 * 2**20, transcendentals=0),
    )(index, before, main, feat, taps, skip, *weights)


def filter_kernel(halo, taps, before_ref, main_ref, feat_ref, filter_ref, skip_ref, inner, shaped, gated, copies8):
    filter_rows(halo, taps, before_ref, main_ref, feat_ref, filter_ref, skip_ref, inner, shaped, gated, copies8)


def filtered(before, main, feat, taps, skip, halo):
    vmem = pl.BlockSpec(memory_space=pltpu.VMEM)
    length = taps.shape[0]
    return pl.pallas_call(
        functools.partial(filter_kernel, halo, length),
        out_shape=jax.ShapeDtypeStruct((HALF, 512), jnp.bfloat16),
        in_specs=[vmem] * 5,
        out_specs=vmem,
        scratch_shapes=filter_scratch(halo, length),
        compiler_params=pltpu.CompilerParams(vmem_limit_bytes=24 * 1024 * 1024),
        cost_estimate=pl.CostEstimate(flops=2 * HALF * 512 * 4096 * 3, bytes_accessed=3 * 2**20, transcendentals=0),
    )(before, main, feat, taps, skip)


def product_kernel(moves, outs, index_ref, inner, weight_ref, *refs):
    out_refs, (weights, w_sems) = refs[:outs], refs[outs:]
    copies = fetch(moves, [weight_ref], weights, index_ref, w_sems)
    for copy in copies:
        copy.start()
    for copy in copies:
        copy.wait()
    product_rows(outs, index_ref, inner, weights, out_refs)


def project_out(index, inner, weight, moves, out_shapes):
    vmem = pl.BlockSpec(memory_space=pltpu.VMEM)
    return pl.pallas_call(
        functools.partial(product_kernel, moves, len(out_shapes)),
        out_shape=[jax.ShapeDtypeStruct(s, jnp.bfloat16) for s in out_shapes],
        in_specs=[pl.BlockSpec(memory_space=pltpu.SMEM), vmem, pl.BlockSpec(memory_space=pl.ANY)],
        out_specs=[vmem] * len(out_shapes),
        scratch_shapes=[pltpu.VMEM((512, 4096), jnp.bfloat16), pltpu.SemaphoreType.DMA((len(moves),))],
        compiler_params=pltpu.CompilerParams(vmem_limit_bytes=48 * 1024 * 1024),
        cost_estimate=pl.CostEstimate(flops=2 * HALF * 512 * 4096, bytes_accessed=6 * 2**20, transcendentals=0),
    )(index, inner, weight)


def per_device(hidden, norm_gain, in_weight, feat_filter, se_filter, mr_filter, skip_gain, out_weight):
    xl, y, core, z, xh = (lax.axis_index(a) for a in AXES)
    behind = lambda place, by: (place - by) % 4
    gains = norm_gain.reshape(2, 8, 512)
    ways = (1, -1, 2)
    other_core = lambda value: shift(value, "core", 1)
    gather = lambda value, axes: by_rows(lax.all_gather(by_rows(value), axes, axis=0, tiled=False))

    side_by_side = lambda w, o: jnp.concatenate([w.reshape(256, 1536), o[:256], o[256:]], axis=1)

    m = side_by_side(in_weight[0], out_weight[0])
    hidden_x, m_xl, m_up, m_down, w1 = together(
        shift(hidden, "xh", 1), shift(m, "xl", 1), shift(m, "y", 1), shift(m, "y", -1), swap(in_weight[1])
    )
    whole = by_rows(lax.all_gather(by_rows(jnp.stack([hidden, hidden_x])), "z", axis=0, tiled=False))
    most = m_xl[:, :CUT]
    far_top, far_low, most_up, most_down, rest = together(
        shift(m_up[:128], "y", 1),
        shift(m_down[128:], "y", -1),
        shift(most, "y", 1),
        shift(most, "y", -1),
        shift(jnp.stack([m_up[:, CUT:], m_down[:, CUT:]]), "xl", 1),
    )
    early = [m, m_xl, m_up, m_down, far_top, far_low, most_up, most_down, rest]
    most_top, most_low, rest_far, *early_other = together(
        shift(most_up[:128], "y", 1),
        shift(most_down[128:], "y", -1),
        shift(jnp.stack([far_top[:, CUT:], far_low[:, CUT:]]), "xl", 1),
        *[other_core(v) for v in early],
    )
    late = [most_top, most_low, rest_far]
    w_list = early + early_other + late + [other_core(v) for v in late]
    w_moves, q_moves, slots = [], [], [z, core]

    def take(number, lead, at_xl, at_y, at_core, low, high, start):
        w_moves.append((number, lead, 0, min(high, 1536) - low, len(slots), low, True, None, start))
        if high == 2048:
            for half in range(2):
                q_moves.append((number, lead, 1536 + 256 * half - low, 256, len(slots), 256 * half + start, False))
        slots.append(at_xl * 8 + at_y * 2 + at_core)

    up, down, far = behind(y, 1), behind(y, -1), behind(y, 2)
    for number, last, c in ((0, 18, core), (9, 21, 1 - core)):
        take(number, None, xl, y, c, 0, 2048, 0)
        take(number + 1, None, 1 - xl, y, c, 0, 2048, 0)
        take(number + 2, None, xl, up, c, 0, 2048, 0)
        take(number + 3, None, xl, down, c, 0, 2048, 0)
        take(number + 4, None, xl, far, c, 0, 2048, 0)
        take(number + 5, None, xl, far, c, 0, 2048, 128)
        take(number + 6, None, 1 - xl, up, c, 0, CUT, 0)
        take(number + 7, None, 1 - xl, down, c, 0, CUT, 0)
        take(number + 8, 0, 1 - xl, up, c, CUT, 2048, 0)
        take(number + 8, 1, 1 - xl, down, c, CUT, 2048, 0)
        take(last, None, 1 - xl, far, c, 0, CUT, 0)
        take(last + 1, None, 1 - xl, far, c, 0, CUT, 128)
        take(last + 2, 0, 1 - xl, far, c, CUT, 2048, 0)
        take(last + 2, 1, 1 - xl, far, c, CUT, 2048, 128)
    q_index = jnp.stack(slots).astype(jnp.int32)
    q_list = w_list

    w1 = gather(after(w1.reshape(256, 1536), rest), ("xh", "xl", "y"))
    o1 = gather(swap(after(out_weight[1], rest_far)), ("xh", "xl", "y"))
    small = jnp.concatenate([feat_filter[1].reshape(9, 512), skip_gain[1:2], mr_filter], axis=0)

    places = jnp.stack([2 * p + c for p in range(4) for c in (xh, 1 - xh)]).astype(jnp.int32)
    low, high, tail = project_in(q_index, places, gains[0], [whole], w_list, w_moves, 16)
    base, small = after((hidden, small), low)
    base, small = swap(base), swap(small)
    tail = from_behind(tail, ("xl", "y", "core"))

    def first_parts(before, main):
        parts = mix_out(
            q_index, before, main, feat_filter[0].reshape(9, 512), se_filter, skip_gain[0:1], q_list, q_moves, 16,
            [(HALF, 1024)] * 4,
        )
        return parts[0], [shift(part, "z", by) for by, part in ((1, parts[1]), (-1, parts[3]), (2, parts[2]))]

    def over_z(own, received):
        total = own.astype(jnp.float32)
        for value in received:
            total = total + value.astype(jnp.float32)
        total = total.astype(jnp.bfloat16)
        pick = lambda c: jnp.where(c == 0, total[:, :512], total[:, 512:])
        mine, others = pick(core), pick(1 - core)
        return mine, [
            lax.ppermute(mine, ("core", "xh"), [(1, 0), (2, 3)]),
            lax.ppermute(others, ("core", "xh"), [(1, 2), (2, 1)]),
            lax.ppermute(others, ("core", "xh"), [(0, 2), (3, 1)]),
        ]

    def over_x(mine, received, rows):
        kept = jnp.where(core == xh, mine, jnp.zeros_like(mine))
        current = base[rows : rows + HALF].astype(jnp.float32) + kept.astype(jnp.float32)
        for value in received:
            current = current + value.astype(jnp.float32)
        return current.astype(jnp.bfloat16)

    own_high, high_z = first_parts(low, high)
    own_low, low_z = first_parts(tail, low)
    mine_high, high_x = over_z(own_high, high_z)
    *low_z, one, two, three = together(*low_z, *high_x)
    high = over_x(mine_high, (one, two, three), HALF)
    mine_low, low_x = over_z(own_low, low_z)
    high = after(high, low_x[2])
    high_near = [shift(high, "z", by) for by in ways]
    one, two, three, *high_near = together(*low_x, *high_near)
    low = over_x(mine_low, (one, two, three), 0)

    places = [(p, (p // 4 % 2) * 8 + (p % 4) * 2 + p // 8) for p in range(16)]
    w_moves = [(0, p, 0, 1536, None, 0, True, block) for p, block in places]
    p_moves = [(0, p, 0, 256, None, 0, False, block) for p, block in places]
    x_index = jnp.stack([behind(z, by) * 2 + c for c in (core, 1 - core) for by in (0, *ways)] * 2).astype(jnp.int32)
    low_near = [low] + [shift(low, "z", by) for by in ways]
    high_near = [high] + high_near
    high_far = [other_core(v) for v in high_near]
    low_far = [other_core(v) for v in low_near]
    p_low, p_high, tail = project_in(
        q_index, x_index, gains[1], low_near + low_far + high_near + high_far, [w1], w_moves, 144
    )
    tail = from_behind(tail, ("xl", "y", "xh"))

    def second_filter(before, main):
        return filtered(before, main, small[:9], small[10:], small[9:10], 144)

    def second_parts(inner):
        return project_out(q_index, inner, o1, p_moves, [(4, HALF, 512)] * 2)

    def second_z(own, theirs):
        both = (own.astype(jnp.float32) + theirs.astype(jnp.float32)).astype(jnp.bfloat16)
        return both[0], [shift(both[at], "z", by) for by, at in ((1, 1), (-1, 3), (2, 2))]

    def second_sum(own, received, rows):
        total = rows.astype(jnp.float32) + own.astype(jnp.float32)
        for value in received:
            total = total + value.astype(jnp.float32)
        return swap(total.astype(jnp.bfloat16))

    inner_high = second_filter(p_low, p_high)
    inner_low = second_filter(tail, p_low)
    inner_high, inner_low = together(inner_high, inner_low)
    own_high, theirs_high = second_parts(inner_high)
    theirs_high = other_core(theirs_high)
    own_high, high_z = second_z(own_high, theirs_high)
    own_low, theirs_low = second_parts(inner_low)
    theirs_low = other_core(theirs_low)
    high = second_sum(own_high, high_z, high)
    own_low, low_z = second_z(own_low, theirs_low)
    low = second_sum(own_low, low_z, low)
    return jnp.concatenate([low, high], axis=0)


def solution(mesh):
    fine = Mesh(np.asarray(mesh.devices).reshape(2, 4, 2, 4, 2), AXES)
    ctx, ch = ("xl", "y", "core"), ("z", "xh")
    return jax.shard_map(
        per_device,
        mesh=fine,
        in_specs=(
            P(ctx, ch),
            P(),
            P(None, ctx, None, ch),
            P(None, None, None, ch),
            P(None, ch),
            P(None, ch),
            P(None, ch),
            P(None, ch, ctx),
        ),
        out_specs=P(ctx, ch),
        check_vma=False,
    )
```

```python
import functools

import jax
import jax.numpy as jnp
import numpy as np
from jax import lax
from jax.experimental.layout import Layout, with_layout_constraint
from jax.experimental import pallas as pl
from jax.experimental.pallas import tpu as pltpu
from jax.sharding import Mesh, PartitionSpec as P

AXES = ("xl", "y", "core", "z", "xh")
HALF = 256
CUT = 1280
LANES = 128


def shift(value, axis, by):
    size = lax.axis_size(axis)
    return lax.ppermute(value, axis, [(i, (i + by) % size) for i in range(size)])


def swap(value):
    moved = lax.ppermute(value, ("core", "xh"), [(1, 2), (2, 1)])
    same = lax.axis_index("core") == lax.axis_index("xh")
    return jnp.where(same, value, moved)


def from_behind(value, axes):
    return lax.ppermute(value, axes, [(i, i + 1) for i in range(15)])


def by_rows(value):
    return with_layout_constraint(value, Layout(major_to_minor=tuple(range(value.ndim))))


def after(value, *others):
    return lax.optimization_barrier((value, *others))[0]


def together(*values):
    return lax.optimization_barrier(values)


def fetch(moves, sources, target, index_ref, semaphores):
    copies = []
    for number, (source, lead, lane, width, slot, other, by_rows, *fixed) in enumerate(moves):
        block = fixed[0] * 256 if slot is None else pl.multiple_of(index_ref[slot] * 256, 256)
        start = fixed[1] if len(fixed) > 1 else 0
        ref = sources[source]
        if lead is not None:
            ref = ref.at[lead]
        if by_rows:
            piece = target.at[pl.ds(pl.multiple_of(block + start, 128), ref.shape[0]), other : other + width]
        else:
            piece = target.at[other : other + ref.shape[0], pl.ds(block, 256)]
        copies.append(pltpu.make_async_copy(ref.at[:, lane : lane + width], piece, semaphores.at[number]))
    return copies


def norm_pieces(loads, places, raw, gain_ref, normed, squares):
    squares[...] = jnp.zeros_like(squares)
    for load, (j, start, count), place in zip(loads, pieces_of(len(loads)), places):
        load.wait()
        lanes = pl.ds(pl.multiple_of(place * 512, 512), 512)
        gain = gain_ref[pl.ds(place, 1), :]

        @pl.loop(0, count // 64)
        def _(step):
            rows = pl.ds(pl.multiple_of(start + step * 64, 64), 64)
            x = raw[j, rows, :].astype(jnp.float32)
            normed[rows, lanes] = (x * gain).astype(jnp.bfloat16)
            q = x * x
            squares[rows, :] += (q[:, :128] + q[:, 128:256]) + (q[:, 256:384] + q[:, 384:])

    squares[:, :1] = lax.rsqrt(jnp.sum(squares[...], axis=1, keepdims=True) * (1.0 / 4096) + 1e-06)


def pieces_of(count):
    rows = 8 * 2 * HALF // count
    return [(j % 8, j // 8 * rows, rows) for j in range(count)]


def in_kernel(moves, sources, halo, index_ref, place_ref, gain_ref, *refs):
    xs, refs = refs[:sources], refs[sources:]
    count = 1 + max(m[0] for m in moves)
    ws, refs = refs[:count], refs[count:]
    out_refs, (tail_ref, raw, normed, weights, squares, x_sems, w_sems) = refs[:2], refs[2:]
    xs = [xs[0].at[j // 2, j % 2] for j in range(8)] if sources == 1 else xs
    loads = [
        pltpu.make_async_copy(x, raw.at[j, start : start + rows], x_sems.at[number])
        for number, (x, (j, start, rows)) in enumerate(zip(xs, pieces_of(len(xs))))
    ]
    copies = fetch(moves, ws, weights, index_ref, w_sems)
    for copy in loads + copies:
        copy.start()
    norm_pieces(loads, [place_ref[j] for j in range(len(xs))], raw, gain_ref, normed, squares)
    for copy in copies:
        copy.wait()

    @pl.loop(0, 6)
    def _(step):
        lanes = pl.ds(pl.multiple_of(step * 256, 256), 256)
        product = jnp.dot(normed[...], weights[:, lanes], preferred_element_type=jnp.float32)
        product = (product * squares[:, :1]).astype(jnp.bfloat16)
        for part, out_ref in enumerate(out_refs):
            out_ref[:, lanes] = product[part * HALF : (part + 1) * HALF]

    last = out_refs[-1]
    tail_ref[:halo, :] = last[HALF - halo :, 512:]
    tail_ref[halo:, :512] = last[HALF - 16 :, :512]
    tail_ref[halo:, 512:] = jnp.zeros((16, 512), jnp.bfloat16)


def project_in(index, places, gain, pieces, weights, moves, halo):
    any_space = pl.BlockSpec(memory_space=pl.ANY)
    vmem = pl.BlockSpec(memory_space=pltpu.VMEM)
    smem = pl.BlockSpec(memory_space=pltpu.SMEM)
    return pl.pallas_call(
        functools.partial(in_kernel, moves, len(pieces), halo),
        out_shape=[jax.ShapeDtypeStruct((HALF, 1536), jnp.bfloat16)] * 2
        + [jax.ShapeDtypeStruct((halo + 16, 1024), jnp.bfloat16)],
        in_specs=[smem, smem, vmem] + [any_space] * (len(pieces) + len(weights)),
        out_specs=[vmem] * 3,
        scratch_shapes=[
            pltpu.VMEM((8, 2 * HALF, 512), jnp.bfloat16),
            pltpu.VMEM((2 * HALF, 4096), jnp.bfloat16),
            pltpu.VMEM((4096, 1536), jnp.bfloat16),
            pltpu.VMEM((2 * HALF, LANES), jnp.float32),
            pltpu.SemaphoreType.DMA((16,)),
            pltpu.SemaphoreType.DMA((len(moves),)),
        ],
        compiler_params=pltpu.CompilerParams(vmem_limit_bytes=50 * 1024 * 1024),
        cost_estimate=pl.CostEstimate(flops=4 * HALF * 4096 * 1536, bytes_accessed=18 * 2**20, transcendentals=0),
    )(index, places, gain, *pieces, *weights)


def filter_rows(halo, taps, before_ref, main_ref, feat_ref, filter_ref, skip_ref, inner, shaped, gated, copies8):
    total = halo + HALF

    if before_ref.shape[1] == 1024:
        shaped[:16, :512] = before_ref[halo:, :512].astype(jnp.float32)
        shaped[:halo, 512:] = before_ref[:halo, :].astype(jnp.float32)
    else:
        shaped[:16, :512] = before_ref[HALF - 16 :, :512].astype(jnp.float32)
        shaped[:halo, 512:] = before_ref[HALF - halo :, 512:].astype(jnp.float32)
    shaped[16 : 16 + HALF, :512] = main_ref[:, :512].astype(jnp.float32)
    shaped[halo:total, 512:] = main_ref[:, 512:].astype(jnp.float32)

    def feature(start, size, s, lanes):
        value = None
        for j in range(3):
            tap = feat_ref[3 * j + s : 3 * j + s + 1, lanes]
            low = s * 512 + lanes.start
            term = tap * shaped[start - j : start - j + size, low : low + LANES]
            value = term if value is None else value + term
        return value

    for lane in range(0, 512, LANES):
        lanes = slice(lane, lane + LANES)
        for start in range(8, total, 64):
            size = min(64, total - start)
            gated[start : start + size, lanes] = feature(start, size, 1, lanes) * feature(start, size, 2, lanes)
        gated[:8, lanes] = jnp.zeros((8, LANES), jnp.float32)

    if taps == 7:
        for lane in range(0, 512, LANES):
            lanes = slice(lane, lane + LANES)
            for start in range(0, HALF, 64):
                own = gated[halo + start : halo + start + 64, lanes]
                value = (skip_ref[:1, lanes] + filter_ref[:1, lanes]) * own
                for j in range(1, taps):
                    value = value + filter_ref[j : j + 1, lanes] * gated[halo + start - j : halo + start - j + 64, lanes]
                inner[start : start + 64, lanes] = (feature(16 + start, 64, 0, lanes) * value).astype(jnp.bfloat16)
    else:
        for lane in range(0, 512, LANES):
            lanes = slice(lane, lane + LANES)
            for r in range(8):
                for start in range(0, HALF + 128, 128):
                    copies8[r, start : start + 128, :] = gated[16 + start - r : 16 + start - r + 128, lanes]

            @pl.loop(0, HALF // 128)
            def _(step):
                base = pl.multiple_of(step * 128, 128)
                value = jnp.zeros((128, LANES), jnp.float32)
                for r in range(8):
                    for a in range(0, 16, 4):
                        window = copies8[r, pl.ds(pl.multiple_of(base + 128 - 8 * (a + 3), 8), 128 + 24), :]
                        for b in range(4):
                            tap = filter_ref[8 * (a + b) + r : 8 * (a + b) + r + 1, lanes]
                            low = 8 * (3 - b)
                            value = value + tap * window[low : low + 128]
                copies8[8, pl.ds(base, 128), :] = value

            for start in range(0, HALF, 64):
                own = gated[halo + start : halo + start + 64, lanes]
                value = copies8[8, start : start + 64, :] + skip_ref[:1, lanes] * own
                inner[start : start + 64, lanes] = (feature(16 + start, 64, 0, lanes) * value).astype(jnp.bfloat16)


def product_rows(outs, index_ref, inner, weights, out_refs):
    z = index_ref[0]
    core = index_ref[1]
    for by in range(4):
        block = lax.rem(z + by, 4)
        if outs == 4:
            columns = pl.ds(pl.multiple_of(block * 1024, 1024), 1024)
            out_refs[by][...] = jnp.dot(
                inner[...], weights[:, columns], preferred_element_type=jnp.float32
            ).astype(jnp.bfloat16)
        else:
            for side in range(2):
                place = block * 2 + (core if side == 0 else 1 - core)
                columns = pl.ds(pl.multiple_of(place * 512, 512), 512)
                out_refs[side][by] = jnp.dot(
                    inner[...], weights[:, columns], preferred_element_type=jnp.float32
                ).astype(jnp.bfloat16)


def filter_scratch(halo, taps):
    return [
        pltpu.VMEM((halo + HALF + 16, 1536), jnp.float32),
        pltpu.VMEM((halo + HALF, 512), jnp.float32),
        pltpu.VMEM((9, 8, LANES) if taps == 7 else (9, HALF + 128, LANES), jnp.float32),
    ]


def mix_kernel(moves, halo, taps, outs, index_ref, before_ref, main_ref, feat_ref, filter_ref, skip_ref, *refs):
    count = 1 + max(m[0] for m in moves)
    ws, refs = refs[:count], refs[count:]
    out_refs, refs = refs[:outs], refs[outs:]
    shaped, gated, copies8, inner, weights, w_sems = refs
    copies = fetch(moves, ws, weights, index_ref, w_sems)
    for copy in copies:
        copy.start()
    filter_rows(halo, taps, before_ref, main_ref, feat_ref, filter_ref, skip_ref, inner, shaped, gated, copies8)
    for copy in copies:
        copy.wait()
    product_rows(outs, index_ref, inner, weights, out_refs)


def mix_out(index, before, main, feat, taps, skip, weights, moves, halo, out_shapes):
    any_space = pl.BlockSpec(memory_space=pl.ANY)
    vmem = pl.BlockSpec(memory_space=pltpu.VMEM)
    length = taps.shape[0]
    return pl.pallas_call(
        functools.partial(mix_kernel, moves, halo, length, len(out_shapes)),
        out_shape=[jax.ShapeDtypeStruct(s, jnp.bfloat16) for s in out_shapes],
        in_specs=[pl.BlockSpec(memory_space=pltpu.SMEM)] + [vmem] * 5 + [any_space] * len(weights),
        out_specs=[vmem] * len(out_shapes),
        scratch_shapes=filter_scratch(halo, length)
        + [
            pltpu.VMEM((HALF, 512), jnp.bfloat16),
            pltpu.VMEM((512, 4096), jnp.bfloat16),
            pltpu.SemaphoreType.DMA((len(moves),)),
        ],
        compiler_params=pltpu.CompilerParams(vmem_limit_bytes=48 * 1024 * 1024),
        cost_estimate=pl.CostEstimate(flops=2 * HALF * 512 * 4096, bytes_accessed=6 * 2**20, transcendentals=0),
    )(index, before, main, feat, taps, skip, *weights)


def filter_kernel(halo, taps, before_ref, main_ref, feat_ref, filter_ref, skip_ref, inner, shaped, gated, copies8):
    filter_rows(halo, taps, before_ref, main_ref, feat_ref, filter_ref, skip_ref, inner, shaped, gated, copies8)


def filtered(before, main, feat, taps, skip, halo):
    vmem = pl.BlockSpec(memory_space=pltpu.VMEM)
    length = taps.shape[0]
    return pl.pallas_call(
        functools.partial(filter_kernel, halo, length),
        out_shape=jax.ShapeDtypeStruct((HALF, 512), jnp.bfloat16),
        in_specs=[vmem] * 5,
        out_specs=vmem,
        scratch_shapes=filter_scratch(halo, length),
        compiler_params=pltpu.CompilerParams(vmem_limit_bytes=24 * 1024 * 1024),
        cost_estimate=pl.CostEstimate(flops=2 * HALF * 512 * 4096 * 3, bytes_accessed=3 * 2**20, transcendentals=0),
    )(before, main, feat, taps, skip)


def product_kernel(moves, outs, index_ref, inner, weight_ref, *refs):
    out_refs, (weights, w_sems) = refs[:outs], refs[outs:]
    copies = fetch(moves, [weight_ref], weights, index_ref, w_sems)
    for copy in copies:
        copy.start()
    for copy in copies:
        copy.wait()
    product_rows(outs, index_ref, inner, weights, out_refs)


def project_out(index, inner, weight, moves, out_shapes):
    vmem = pl.BlockSpec(memory_space=pltpu.VMEM)
    return pl.pallas_call(
        functools.partial(product_kernel, moves, len(out_shapes)),
        out_shape=[jax.ShapeDtypeStruct(s, jnp.bfloat16) for s in out_shapes],
        in_specs=[pl.BlockSpec(memory_space=pltpu.SMEM), vmem, pl.BlockSpec(memory_space=pl.ANY)],
        out_specs=[vmem] * len(out_shapes),
        scratch_shapes=[pltpu.VMEM((512, 4096), jnp.bfloat16), pltpu.SemaphoreType.DMA((len(moves),))],
        compiler_params=pltpu.CompilerParams(vmem_limit_bytes=48 * 1024 * 1024),
        cost_estimate=pl.CostEstimate(flops=2 * HALF * 512 * 4096, bytes_accessed=6 * 2**20, transcendentals=0),
    )(index, inner, weight)


def per_device(hidden, norm_gain, in_weight, feat_filter, se_filter, mr_filter, skip_gain, out_weight):
    xl, y, core, z, xh = (lax.axis_index(a) for a in AXES)
    behind = lambda place, by: (place - by) % 4
    gains = norm_gain.reshape(2, 8, 512)
    ways = (1, -1, 2)
    other_core = lambda value: shift(value, "core", 1)
    gather = lambda value, axes: by_rows(lax.all_gather(by_rows(value), axes, axis=0, tiled=False))

    side_by_side = lambda w, o: jnp.concatenate([w.reshape(256, 1536), o[:256], o[256:]], axis=1)

    m = side_by_side(in_weight[0], out_weight[0])
    m_up, m_down, m_xl, hidden_x = together(
        shift(m, "y", 1), shift(m, "y", -1), shift(m, "xl", 1), shift(hidden, "xh", 1)
    )
    whole = by_rows(lax.all_gather(by_rows(jnp.stack([hidden, hidden_x])), "z", axis=0, tiled=False))
    most = m_xl[:, :CUT]
    far_top = shift(m_up[:128], "y", 1)
    far_top, far_low, most_up, most_down, rest = together(
        far_top,
        shift(m_down[128:], "y", -1),
        shift(most, "y", 1),
        shift(most, "y", -1),
        shift(jnp.stack([m_up[:, CUT:], m_down[:, CUT:]]), "xl", 1),
    )
    early = [m, m_xl, m_up, m_down, far_top, far_low, most_up, most_down, rest]
    most_top, most_low, rest_far, w1, *early_other = together(
        shift(most_up[:128], "y", 1),
        shift(most_down[128:], "y", -1),
        shift(jnp.stack([far_top[:, CUT:], far_low[:, CUT:]]), "xl", 1),
        swap(after(in_weight[1], rest)),
        *[other_core(v) for v in early],
    )
    late = [most_top, most_low, rest_far]
    w_list = early + early_other + late + [other_core(v) for v in late]
    w_moves, q_moves, slots = [], [], [z, core]

    def take(number, lead, at_xl, at_y, at_core, low, high, start):
        w_moves.append((number, lead, 0, min(high, 1536) - low, len(slots), low, True, None, start))
        if high == 2048:
            for half in range(2):
                q_moves.append((number, lead, 1536 + 256 * half - low, 256, len(slots), 256 * half + start, False))
        slots.append(at_xl * 8 + at_y * 2 + at_core)

    up, down, far = behind(y, 1), behind(y, -1), behind(y, 2)
    for number, last, c in ((0, 18, core), (9, 21, 1 - core)):
        take(number, None, xl, y, c, 0, 2048, 0)
        take(number + 1, None, 1 - xl, y, c, 0, 2048, 0)
        take(number + 2, None, xl, up, c, 0, 2048, 0)
        take(number + 3, None, xl, down, c, 0, 2048, 0)
        take(number + 4, None, xl, far, c, 0, 2048, 0)
        take(number + 5, None, xl, far, c, 0, 2048, 128)
        take(number + 6, None, 1 - xl, up, c, 0, CUT, 0)
        take(number + 7, None, 1 - xl, down, c, 0, CUT, 0)
        take(number + 8, 0, 1 - xl, up, c, CUT, 2048, 0)
        take(number + 8, 1, 1 - xl, down, c, CUT, 2048, 0)
        take(last, None, 1 - xl, far, c, 0, CUT, 0)
        take(last + 1, None, 1 - xl, far, c, 0, CUT, 128)
        take(last + 2, 0, 1 - xl, far, c, CUT, 2048, 0)
        take(last + 2, 1, 1 - xl, far, c, CUT, 2048, 128)
    q_index = jnp.stack(slots).astype(jnp.int32)
    q_list = w_list

    w1 = gather(w1.reshape(256, 1536), ("xh", "xl", "y"))
    o1 = gather(swap(after(out_weight[1], rest_far)), ("xh", "xl", "y"))
    small = jnp.concatenate([feat_filter[1].reshape(9, 512), skip_gain[1:2], mr_filter], axis=0)

    places = jnp.stack([2 * p + c for p in range(4) for c in (xh, 1 - xh)]).astype(jnp.int32)
    low, high, tail = project_in(q_index, places, gains[0], [whole], w_list, w_moves, 16)
    base, small = after((hidden, small), low)
    base, small = swap(base), swap(small)
    tail = from_behind(tail, ("xl", "y", "core"))

    def first_parts(before, main):
        parts = mix_out(
            q_index, before, main, feat_filter[0].reshape(9, 512), se_filter, skip_gain[0:1], q_list, q_moves, 16,
            [(HALF, 1024)] * 4,
        )
        return parts[0], [shift(part, "z", by) for by, part in ((1, parts[1]), (-1, parts[3]), (2, parts[2]))]

    def over_z(own, received):
        total = own.astype(jnp.float32)
        for value in received:
            total = total + value.astype(jnp.float32)
        total = total.astype(jnp.bfloat16)
        pick = lambda c: jnp.where(c == 0, total[:, :512], total[:, 512:])
        mine, others = pick(core), pick(1 - core)
        return mine, [
            lax.ppermute(mine, ("core", "xh"), [(1, 0), (2, 3)]),
            lax.ppermute(others, ("core", "xh"), [(1, 2), (2, 1)]),
            lax.ppermute(others, ("core", "xh"), [(0, 2), (3, 1)]),
        ]

    def over_x(mine, received, rows):
        kept = jnp.where(core == xh, mine, jnp.zeros_like(mine))
        current = base[rows : rows + HALF].astype(jnp.float32) + kept.astype(jnp.float32)
        for value in received:
            current = current + value.astype(jnp.float32)
        return current.astype(jnp.bfloat16)

    own_high, high_z = first_parts(low, high)
    own_low, low_z = first_parts(tail, low)
    mine_high, high_x = over_z(own_high, high_z)
    *low_z, one, two, three = together(*low_z, *high_x)
    high = over_x(mine_high, (one, two, three), HALF)
    mine_low, low_x = over_z(own_low, low_z)
    high = after(high, low_x[2])
    high_near = [shift(high, "z", by) for by in ways]
    one, two, three, *high_near = together(*low_x, *high_near)
    low = over_x(mine_low, (one, two, three), 0)

    places = [(p, (p // 4 % 2) * 8 + (p % 4) * 2 + p // 8) for p in range(16)]
    w_moves = [(0, p, 0, 1536, None, 0, True, block) for p, block in places]
    p_moves = [(0, p, 0, 256, None, 0, False, block) for p, block in places]
    x_index = jnp.stack([behind(z, by) * 2 + c for c in (core, 1 - core) for by in (0, *ways)] * 2).astype(jnp.int32)
    low_near = [low] + [shift(low, "z", by) for by in ways]
    high_near = [high] + high_near
    high_far = [other_core(v) for v in high_near]
    low_far = [other_core(v) for v in low_near]
    p_low, p_high, tail = project_in(
        q_index, x_index, gains[1], low_near + low_far + high_near + high_far, [w1], w_moves, 144
    )
    tail = from_behind(tail, ("xl", "y", "xh"))

    def second_filter(before, main):
        return filtered(before, main, small[:9], small[10:], small[9:10], 144)

    def second_parts(inner):
        return project_out(q_index, inner, o1, p_moves, [(4, HALF, 512)] * 2)

    def second_z(own, theirs):
        both = (own.astype(jnp.float32) + theirs.astype(jnp.float32)).astype(jnp.bfloat16)
        return both[0], [shift(both[at], "z", by) for by, at in ((1, 1), (-1, 3), (2, 2))]

    def second_sum(own, received, rows):
        total = rows.astype(jnp.float32) + own.astype(jnp.float32)
        for value in received:
            total = total + value.astype(jnp.float32)
        return swap(total.astype(jnp.bfloat16))

    inner_high = second_filter(p_low, p_high)
    inner_low = second_filter(tail, p_low)
    inner_high, inner_low = together(inner_high, inner_low)
    own_high, theirs_high = second_parts(inner_high)
    theirs_high = other_core(theirs_high)
    own_high, high_z = second_z(own_high, theirs_high)
    own_low, theirs_low = second_parts(inner_low)
    theirs_low = other_core(theirs_low)
    high = second_sum(own_high, high_z, high)
    own_low, low_z = second_z(own_low, theirs_low)
    low = second_sum(own_low, low_z, low)
    return jnp.concatenate([low, high], axis=0)


def solution(mesh):
    fine = Mesh(np.asarray(mesh.devices).reshape(2, 4, 2, 4, 2), AXES)
    ctx, ch = ("xl", "y", "core"), ("z", "xh")
    return jax.shard_map(
        per_device,
        mesh=fine,
        in_specs=(
            P(ctx, ch),
            P(),
            P(None, ctx, None, ch),
            P(None, None, None, ch),
            P(None, ch),
            P(None, ch),
            P(None, ch),
            P(None, ch, ctx),
        ),
        out_specs=P(ctx, ch),
        check_vma=False,
    )
```

```python
import functools

import jax
import jax.numpy as jnp
import numpy as np
from jax import lax
from jax.experimental.layout import Layout, with_layout_constraint
from jax.experimental import pallas as pl
from jax.experimental.pallas import tpu as pltpu
from jax.sharding import Mesh, PartitionSpec as P

AXES = ("xl", "y", "core", "z", "xh")
HALF = 256
CUT = 1280
LANES = 128


def shift(value, axis, by):
    size = lax.axis_size(axis)
    return lax.ppermute(value, axis, [(i, (i + by) % size) for i in range(size)])


def swap(value):
    moved = lax.ppermute(value, ("core", "xh"), [(1, 2), (2, 1)])
    same = lax.axis_index("core") == lax.axis_index("xh")
    return jnp.where(same, value, moved)


def from_behind(value, axes):
    return lax.ppermute(value, axes, [(i, i + 1) for i in range(15)])


def by_rows(value):
    return with_layout_constraint(value, Layout(major_to_minor=tuple(range(value.ndim))))


def after(value, *others):
    return lax.optimization_barrier((value, *others))[0]


def together(*values):
    return lax.optimization_barrier(values)


def fetch(moves, sources, target, index_ref, semaphores):
    copies = []
    for number, (source, lead, lane, width, slot, other, by_rows, *fixed) in enumerate(moves):
        block = fixed[0] * 256 if slot is None else pl.multiple_of(index_ref[slot] * 256, 256)
        ref = sources[source]
        if lead is not None:
            ref = ref.at[lead]
        if by_rows:
            piece = target.at[pl.ds(block, 256), other : other + width]
        else:
            piece = target.at[other : other + ref.shape[0], pl.ds(block, 256)]
        copies.append(pltpu.make_async_copy(ref.at[:, lane : lane + width], piece, semaphores.at[number]))
    return copies


def norm_pieces(loads, places, raw, gain_ref, normed, squares):
    squares[...] = jnp.zeros_like(squares)
    for load, (j, start, count), place in zip(loads, pieces_of(len(loads)), places):
        load.wait()
        lanes = pl.ds(pl.multiple_of(place * 512, 512), 512)
        gain = gain_ref[pl.ds(place, 1), :]

        @pl.loop(0, count // 64)
        def _(step):
            rows = pl.ds(pl.multiple_of(start + step * 64, 64), 64)
            x = raw[j, rows, :].astype(jnp.float32)
            normed[rows, lanes] = (x * gain).astype(jnp.bfloat16)
            q = x * x
            squares[rows, :] += (q[:, :128] + q[:, 128:256]) + (q[:, 256:384] + q[:, 384:])

    squares[:, :1] = lax.rsqrt(jnp.sum(squares[...], axis=1, keepdims=True) * (1.0 / 4096) + 1e-06)


def pieces_of(count):
    rows = 8 * 2 * HALF // count
    return [(j % 8, j // 8 * rows, rows) for j in range(count)]


def in_kernel(moves, sources, halo, index_ref, place_ref, gain_ref, *refs):
    xs, refs = refs[:sources], refs[sources:]
    count = 1 + max(m[0] for m in moves)
    ws, refs = refs[:count], refs[count:]
    out_refs, (tail_ref, raw, normed, weights, squares, x_sems, w_sems) = refs[:2], refs[2:]
    xs = [xs[0].at[j] for j in range(8)] if sources == 1 else xs
    loads = [
        pltpu.make_async_copy(x, raw.at[j, start : start + rows], x_sems.at[number])
        for number, (x, (j, start, rows)) in enumerate(zip(xs, pieces_of(len(xs))))
    ]
    copies = fetch(moves, ws, weights, index_ref, w_sems)
    for copy in loads + copies:
        copy.start()
    norm_pieces(loads, [place_ref[j] for j in range(len(xs))], raw, gain_ref, normed, squares)
    for copy in copies:
        copy.wait()

    @pl.loop(0, 6)
    def _(step):
        lanes = pl.ds(pl.multiple_of(step * 256, 256), 256)
        product = jnp.dot(normed[...], weights[:, lanes], preferred_element_type=jnp.float32)
        product = (product * squares[:, :1]).astype(jnp.bfloat16)
        for part, out_ref in enumerate(out_refs):
            out_ref[:, lanes] = product[part * HALF : (part + 1) * HALF]

    last = out_refs[-1]
    tail_ref[:halo, :] = last[HALF - halo :, 512:]
    tail_ref[halo:, :512] = last[HALF - 16 :, :512]
    tail_ref[halo:, 512:] = jnp.zeros((16, 512), jnp.bfloat16)


def project_in(index, places, gain, pieces, weights, moves, halo):
    any_space = pl.BlockSpec(memory_space=pl.ANY)
    vmem = pl.BlockSpec(memory_space=pltpu.VMEM)
    smem = pl.BlockSpec(memory_space=pltpu.SMEM)
    return pl.pallas_call(
        functools.partial(in_kernel, moves, len(pieces), halo),
        out_shape=[jax.ShapeDtypeStruct((HALF, 1536), jnp.bfloat16)] * 2
        + [jax.ShapeDtypeStruct((halo + 16, 1024), jnp.bfloat16)],
        in_specs=[smem, smem, vmem] + [any_space] * (len(pieces) + len(weights)),
        out_specs=[vmem] * 3,
        scratch_shapes=[
            pltpu.VMEM((8, 2 * HALF, 512), jnp.bfloat16),
            pltpu.VMEM((2 * HALF, 4096), jnp.bfloat16),
            pltpu.VMEM((4096, 1536), jnp.bfloat16),
            pltpu.VMEM((2 * HALF, LANES), jnp.float32),
            pltpu.SemaphoreType.DMA((16,)),
            pltpu.SemaphoreType.DMA((len(moves),)),
        ],
        compiler_params=pltpu.CompilerParams(vmem_limit_bytes=(44 if halo == 16 else 50) * 1024 * 1024),
        cost_estimate=pl.CostEstimate(flops=4 * HALF * 4096 * 1536, bytes_accessed=18 * 2**20, transcendentals=0),
    )(index, places, gain, *pieces, *weights)


def filter_rows(halo, taps, before_ref, main_ref, feat_ref, filter_ref, skip_ref, inner, shaped, gated, copies8):
    total = halo + HALF

    if before_ref.shape[1] == 1024:
        shaped[:16, :512] = before_ref[halo:, :512].astype(jnp.float32)
        shaped[:halo, 512:] = before_ref[:halo, :].astype(jnp.float32)
    else:
        shaped[:16, :512] = before_ref[HALF - 16 :, :512].astype(jnp.float32)
        shaped[:halo, 512:] = before_ref[HALF - halo :, 512:].astype(jnp.float32)
    shaped[16 : 16 + HALF, :512] = main_ref[:, :512].astype(jnp.float32)
    shaped[halo:total, 512:] = main_ref[:, 512:].astype(jnp.float32)

    def feature(start, size, s, lanes):
        value = None
        for j in range(3):
            tap = feat_ref[3 * j + s : 3 * j + s + 1, lanes]
            low = s * 512 + lanes.start
            term = tap * shaped[start - j : start - j + size, low : low + LANES]
            value = term if value is None else value + term
        return value

    for lane in range(0, 512, LANES):
        lanes = slice(lane, lane + LANES)
        for start in range(8, total, 64):
            size = min(64, total - start)
            gated[start : start + size, lanes] = feature(start, size, 1, lanes) * feature(start, size, 2, lanes)
        gated[:8, lanes] = jnp.zeros((8, LANES), jnp.float32)

    if taps == 7:
        for lane in range(0, 512, LANES):
            lanes = slice(lane, lane + LANES)
            for start in range(0, HALF, 64):
                own = gated[halo + start : halo + start + 64, lanes]
                value = (skip_ref[:1, lanes] + filter_ref[:1, lanes]) * own
                for j in range(1, taps):
                    value = value + filter_ref[j : j + 1, lanes] * gated[halo + start - j : halo + start - j + 64, lanes]
                inner[start : start + 64, lanes] = (feature(16 + start, 64, 0, lanes) * value).astype(jnp.bfloat16)
    else:
        for lane in range(0, 512, LANES):
            lanes = slice(lane, lane + LANES)
            for r in range(8):
                for start in range(0, HALF + 128, 128):
                    copies8[r, start : start + 128, :] = gated[16 + start - r : 16 + start - r + 128, lanes]

            @pl.loop(0, HALF // 128)
            def _(step):
                base = pl.multiple_of(step * 128, 128)
                value = jnp.zeros((128, LANES), jnp.float32)
                for r in range(8):
                    for a in range(0, 16, 4):
                        window = copies8[r, pl.ds(pl.multiple_of(base + 128 - 8 * (a + 3), 8), 128 + 24), :]
                        for b in range(4):
                            tap = filter_ref[8 * (a + b) + r : 8 * (a + b) + r + 1, lanes]
                            low = 8 * (3 - b)
                            value = value + tap * window[low : low + 128]
                copies8[8, pl.ds(base, 128), :] = value

            for start in range(0, HALF, 64):
                own = gated[halo + start : halo + start + 64, lanes]
                value = copies8[8, start : start + 64, :] + skip_ref[:1, lanes] * own
                inner[start : start + 64, lanes] = (feature(16 + start, 64, 0, lanes) * value).astype(jnp.bfloat16)


def product_rows(outs, index_ref, inner, weights, out_refs):
    z = index_ref[0]
    core = index_ref[1]
    for by in range(4):
        block = lax.rem(z + by, 4)
        if outs == 4:
            columns = pl.ds(pl.multiple_of(block * 1024, 1024), 1024)
            out_refs[by][...] = jnp.dot(
                inner[...], weights[:, columns], preferred_element_type=jnp.float32
            ).astype(jnp.bfloat16)
        else:
            for side in range(2):
                place = block * 2 + (core if side == 0 else 1 - core)
                columns = pl.ds(pl.multiple_of(place * 512, 512), 512)
                out_refs[side][by] = jnp.dot(
                    inner[...], weights[:, columns], preferred_element_type=jnp.float32
                ).astype(jnp.bfloat16)


def filter_scratch(halo, taps):
    return [
        pltpu.VMEM((halo + HALF + 16, 1536), jnp.float32),
        pltpu.VMEM((halo + HALF, 512), jnp.float32),
        pltpu.VMEM((9, 8, LANES) if taps == 7 else (9, HALF + 128, LANES), jnp.float32),
    ]


def mix_kernel(moves, halo, taps, outs, index_ref, before_ref, main_ref, feat_ref, filter_ref, skip_ref, *refs):
    count = 1 + max(m[0] for m in moves)
    ws, refs = refs[:count], refs[count:]
    out_refs, refs = refs[:outs], refs[outs:]
    shaped, gated, copies8, inner, weights, w_sems = refs
    copies = fetch(moves, ws, weights, index_ref, w_sems)
    for copy in copies:
        copy.start()
    filter_rows(halo, taps, before_ref, main_ref, feat_ref, filter_ref, skip_ref, inner, shaped, gated, copies8)
    for copy in copies:
        copy.wait()
    product_rows(outs, index_ref, inner, weights, out_refs)


def mix_out(index, before, main, feat, taps, skip, weights, moves, halo, out_shapes):
    any_space = pl.BlockSpec(memory_space=pl.ANY)
    vmem = pl.BlockSpec(memory_space=pltpu.VMEM)
    length = taps.shape[0]
    return pl.pallas_call(
        functools.partial(mix_kernel, moves, halo, length, len(out_shapes)),
        out_shape=[jax.ShapeDtypeStruct(s, jnp.bfloat16) for s in out_shapes],
        in_specs=[pl.BlockSpec(memory_space=pltpu.SMEM)] + [vmem] * 5 + [any_space] * len(weights),
        out_specs=[vmem] * len(out_shapes),
        scratch_shapes=filter_scratch(halo, length)
        + [
            pltpu.VMEM((HALF, 512), jnp.bfloat16),
            pltpu.VMEM((512, 4096), jnp.bfloat16),
            pltpu.SemaphoreType.DMA((len(moves),)),
        ],
        compiler_params=pltpu.CompilerParams(vmem_limit_bytes=48 * 1024 * 1024),
        cost_estimate=pl.CostEstimate(flops=2 * HALF * 512 * 4096, bytes_accessed=6 * 2**20, transcendentals=0),
    )(index, before, main, feat, taps, skip, *weights)


def filter_kernel(halo, taps, before_ref, main_ref, feat_ref, filter_ref, skip_ref, inner, shaped, gated, copies8):
    filter_rows(halo, taps, before_ref, main_ref, feat_ref, filter_ref, skip_ref, inner, shaped, gated, copies8)


def filtered(before, main, feat, taps, skip, halo):
    vmem = pl.BlockSpec(memory_space=pltpu.VMEM)
    length = taps.shape[0]
    return pl.pallas_call(
        functools.partial(filter_kernel, halo, length),
        out_shape=jax.ShapeDtypeStruct((HALF, 512), jnp.bfloat16),
        in_specs=[vmem] * 5,
        out_specs=vmem,
        scratch_shapes=filter_scratch(halo, length),
        compiler_params=pltpu.CompilerParams(vmem_limit_bytes=24 * 1024 * 1024),
        cost_estimate=pl.CostEstimate(flops=2 * HALF * 512 * 4096 * 3, bytes_accessed=3 * 2**20, transcendentals=0),
    )(before, main, feat, taps, skip)


def product_kernel(moves, outs, index_ref, inner, weight_ref, *refs):
    out_refs, (weights, w_sems) = refs[:outs], refs[outs:]
    copies = fetch(moves, [weight_ref], weights, index_ref, w_sems)
    for copy in copies:
        copy.start()
    for copy in copies:
        copy.wait()
    product_rows(outs, index_ref, inner, weights, out_refs)


def project_out(index, inner, weight, moves, out_shapes):
    vmem = pl.BlockSpec(memory_space=pltpu.VMEM)
    return pl.pallas_call(
        functools.partial(product_kernel, moves, len(out_shapes)),
        out_shape=[jax.ShapeDtypeStruct(s, jnp.bfloat16) for s in out_shapes],
        in_specs=[pl.BlockSpec(memory_space=pltpu.SMEM), vmem, pl.BlockSpec(memory_space=pl.ANY)],
        out_specs=[vmem] * len(out_shapes),
        scratch_shapes=[pltpu.VMEM((512, 4096), jnp.bfloat16), pltpu.SemaphoreType.DMA((len(moves),))],
        compiler_params=pltpu.CompilerParams(vmem_limit_bytes=48 * 1024 * 1024),
        cost_estimate=pl.CostEstimate(flops=2 * HALF * 512 * 4096, bytes_accessed=6 * 2**20, transcendentals=0),
    )(index, inner, weight)


def per_device(hidden, norm_gain, in_weight, feat_filter, se_filter, mr_filter, skip_gain, out_weight):
    xl, y, core, z, xh = (lax.axis_index(a) for a in AXES)
    behind = lambda place, by: (place - by) % 4
    gains = norm_gain.reshape(2, 8, 512)
    ways = (1, -1, 2)
    other_core = lambda value: shift(value, "core", 1)
    gather = lambda value, axes: by_rows(lax.all_gather(by_rows(value), axes, axis=0, tiled=False))

    side_by_side = lambda w, o: jnp.concatenate([w.reshape(256, 1536), o[:256], o[256:]], axis=1)

    whole = lax.all_gather(hidden, ("z", "xh"), axis=0, tiled=False)

    m = side_by_side(in_weight[0], out_weight[0])
    m_xl = shift(m, "xl", 1)
    m_xl, w1, o1, *m_y = together(
        m_xl, swap(in_weight[1]), swap(after(out_weight[1], m_xl)), *[shift(m, "y", by) for by in ways]
    )
    rest = shift(jnp.stack([v[:, CUT:] for v in m_y]), "xl", 1)
    most = [shift(m_xl[:, :CUT], "y", by) for by in ways]
    rest, *more = together(rest, *most, *[other_core(after(v, most[0])) for v in (m, m_xl, *m_y)])
    most, far = more[:3], more[3:]
    w_list = [m, m_xl, *m_y, *far, rest, *most] + [other_core(v) for v in (rest, *most)]
    w_moves, q_moves, slots = [], [], [z, core]

    def take(number, lead, at_xl, at_y, at_core, low, high):
        w_moves.append((number, lead, 0, min(high, 1536) - low, len(slots), low, True))
        if high == 2048:
            for half in range(2):
                q_moves.append((number, lead, 1536 + 256 * half - low, 256, len(slots), 256 * half, False))
        slots.append(at_xl * 8 + at_y * 2 + at_core)

    for number, c in ((0, core), (5, 1 - core)):
        take(number, None, xl, y, c, 0, 2048)
        take(number + 1, None, 1 - xl, y, c, 0, 2048)
        for e, by in enumerate(ways):
            take(number + 2 + e, None, xl, behind(y, by), c, 0, 2048)
    for number, c in ((10, core), (14, 1 - core)):
        for e, by in enumerate(ways):
            take(number, e, 1 - xl, behind(y, by), c, CUT, 2048)
            take(number + 1 + e, None, 1 - xl, behind(y, by), c, 0, CUT)
    q_index = jnp.stack(slots).astype(jnp.int32)
    q_list = w_list[:15]

    w1 = gather(after(w1.reshape(256, 1536), rest, *most), ("xh", "xl", "y"))
    o1 = gather(o1, ("xh", "xl", "y"))
    small = jnp.concatenate([feat_filter[1].reshape(9, 512), skip_gain[1:2], mr_filter], axis=0)

    places = jnp.arange(8, dtype=jnp.int32)
    low, high, tail = project_in(q_index, places, gains[0], [whole], w_list, w_moves, 16)
    base = other_core(lax.dynamic_index_in_dim(whole, 2 * z + 1 - core, 0, keepdims=False))
    base = jnp.where(core == xh, hidden, base)
    small = swap(after(small, low))
    tail = from_behind(tail, ("xl", "y", "core"))

    def first_parts(before, main):
        parts = mix_out(
            q_index, before, main, feat_filter[0].reshape(9, 512), se_filter, skip_gain[0:1], q_list, q_moves, 16,
            [(HALF, 1024)] * 4,
        )
        return parts[0], [shift(part, "z", by) for by, part in ((1, parts[1]), (-1, parts[3]), (2, parts[2]))]

    def over_z(own, received):
        total = own.astype(jnp.float32)
        for value in received:
            total = total + value.astype(jnp.float32)
        total = total.astype(jnp.bfloat16)
        pick = lambda c: jnp.where(c == 0, total[:, :512], total[:, 512:])
        mine, others = pick(core), pick(1 - core)
        return mine, [
            lax.ppermute(mine, ("core", "xh"), [(1, 0), (2, 3)]),
            lax.ppermute(others, ("core", "xh"), [(1, 2), (2, 1)]),
            lax.ppermute(others, ("core", "xh"), [(0, 2), (3, 1)]),
        ]

    def over_x(mine, received, rows):
        kept = jnp.where(core == xh, mine, jnp.zeros_like(mine))
        current = base[rows : rows + HALF].astype(jnp.float32) + kept.astype(jnp.float32)
        for value in received:
            current = current + value.astype(jnp.float32)
        return current.astype(jnp.bfloat16)

    own_high, high_z = first_parts(low, high)
    own_low, low_z = first_parts(tail, low)
    mine_high, high_x = over_z(own_high, high_z)
    *low_z, one, two, three = together(*low_z, *high_x)
    high = over_x(mine_high, (one, two, three), HALF)
    mine_low, low_x = over_z(own_low, low_z)
    high = after(high, low_x[2])
    high_near = [shift(high, "z", by) for by in ways]
    one, two, three, *high_near = together(*low_x, *high_near)
    low = over_x(mine_low, (one, two, three), 0)

    places = [(p, (p // 4 % 2) * 8 + (p % 4) * 2 + p // 8) for p in range(16)]
    w_moves = [(0, p, 0, 1536, None, 0, True, block) for p, block in places]
    p_moves = [(0, p, 0, 256, None, 0, False, block) for p, block in places]
    x_index = jnp.stack([behind(z, by) * 2 + c for c in (core, 1 - core) for by in (0, *ways)] * 2).astype(jnp.int32)
    low_near = [low] + [shift(low, "z", by) for by in ways]
    high_near = [high] + high_near
    high_far = [other_core(v) for v in high_near]
    low_far = [other_core(v) for v in low_near]
    p_low, p_high, tail = project_in(
        q_index, x_index, gains[1], low_near + low_far + high_near + high_far, [w1], w_moves, 144
    )
    tail = from_behind(tail, ("xl", "y", "xh"))

    def second_filter(before, main):
        return filtered(before, main, small[:9], small[10:], small[9:10], 144)

    def second_parts(inner):
        return project_out(q_index, inner, o1, p_moves, [(4, HALF, 512)] * 2)

    def second_z(own, theirs):
        both = (own.astype(jnp.float32) + theirs.astype(jnp.float32)).astype(jnp.bfloat16)
        return both[0], [shift(both[at], "z", by) for by, at in ((1, 1), (-1, 3), (2, 2))]

    def second_sum(own, received, rows):
        total = rows.astype(jnp.float32) + own.astype(jnp.float32)
        for value in received:
            total = total + value.astype(jnp.float32)
        return swap(total.astype(jnp.bfloat16))

    inner_high = second_filter(p_low, p_high)
    inner_low = second_filter(tail, p_low)
    inner_high, inner_low = together(inner_high, inner_low)
    own_high, theirs_high = second_parts(inner_high)
    theirs_high = other_core(theirs_high)
    own_high, high_z = second_z(own_high, theirs_high)
    own_low, theirs_low = second_parts(inner_low)
    theirs_low = other_core(theirs_low)
    high = second_sum(own_high, high_z, high)
    own_low, low_z = second_z(own_low, theirs_low)
    low = second_sum(own_low, low_z, low)
    return jnp.concatenate([low, high], axis=0)


def solution(mesh):
    fine = Mesh(np.asarray(mesh.devices).reshape(2, 4, 2, 4, 2), AXES)
    ctx, ch = ("xl", "y", "core"), ("z", "xh")
    return jax.shard_map(
        per_device,
        mesh=fine,
        in_specs=(
            P(ctx, ch),
            P(),
            P(None, ctx, None, ch),
            P(None, None, None, ch),
            P(None, ch),
            P(None, ch),
            P(None, ch),
            P(None, ch, ctx),
        ),
        out_specs=P(ctx, ch),
        check_vma=False,
    )
```

```python
import functools

import jax
import jax.numpy as jnp
import numpy as np
from jax import lax
from jax.experimental.layout import Layout, with_layout_constraint
from jax.experimental import pallas as pl
from jax.experimental.pallas import tpu as pltpu
from jax.sharding import Mesh, PartitionSpec as P

AXES = ("xl", "y", "core", "z", "xh")
HALF = 256
CUT = 1280
LANES = 128


def shift(value, axis, by):
    size = lax.axis_size(axis)
    return lax.ppermute(value, axis, [(i, (i + by) % size) for i in range(size)])


def swap(value):
    moved = lax.ppermute(value, ("core", "xh"), [(1, 2), (2, 1)])
    same = lax.axis_index("core") == lax.axis_index("xh")
    return jnp.where(same, value, moved)


def shift_swapped(value, by):
    pairs = [(a * 8 + z * 2 + b, b * 8 + (z + by) % 4 * 2 + a) for a in range(2) for z in range(4) for b in range(2)]
    return lax.ppermute(value, ("core", "z", "xh"), pairs)


def from_behind(value, axes):
    return lax.ppermute(value, axes, [(i, i + 1) for i in range(15)])


def by_rows(value):
    return with_layout_constraint(value, Layout(major_to_minor=tuple(range(value.ndim))))


def after(value, *others):
    return lax.optimization_barrier((value, *others))[0]


def together(*values):
    return lax.optimization_barrier(values)


def fetch(moves, sources, target, index_ref, semaphores):
    copies = []
    for number, (source, lead, lane, width, slot, other, by_rows, *fixed) in enumerate(moves):
        block = fixed[0] * 256 if slot is None else pl.multiple_of(index_ref[slot] * 256, 256)
        ref = sources[source]
        if lead is not None:
            ref = ref.at[lead]
        if by_rows:
            piece = target.at[pl.ds(block, 256), other : other + width]
        else:
            piece = target.at[other : other + ref.shape[0], pl.ds(block, 256)]
        copies.append(pltpu.make_async_copy(ref.at[:, lane : lane + width], piece, semaphores.at[number]))
    return copies


def norm_pieces(loads, places, raw, gain_ref, normed, squares):
    squares[...] = jnp.zeros_like(squares)
    for load, (j, start, count), place in zip(loads, pieces_of(len(loads)), places):
        load.wait()
        lanes = pl.ds(pl.multiple_of(place * 512, 512), 512)
        gain = gain_ref[pl.ds(place, 1), :]

        @pl.loop(0, count // 64)
        def _(step):
            rows = pl.ds(pl.multiple_of(start + step * 64, 64), 64)
            x = raw[j, rows, :].astype(jnp.float32)
            normed[rows, lanes] = (x * gain).astype(jnp.bfloat16)
            q = x * x
            squares[rows, :] += (q[:, :128] + q[:, 128:256]) + (q[:, 256:384] + q[:, 384:])

    squares[:, :1] = lax.rsqrt(jnp.sum(squares[...], axis=1, keepdims=True) * (1.0 / 4096) + 1e-06)


def pieces_of(count):
    rows = 8 * 2 * HALF // count
    return [(j % 8, j // 8 * rows, rows) for j in range(count)]


def in_kernel(moves, sources, halo, index_ref, place_ref, gain_ref, *refs):
    xs, refs = refs[:sources], refs[sources:]
    count = 1 + max(m[0] for m in moves)
    ws, refs = refs[:count], refs[count:]
    out_refs, (tail_ref, raw, normed, weights, squares, x_sems, w_sems) = refs[:2], refs[2:]
    xs = [xs[0].at[j] for j in range(8)] if sources == 1 else xs
    loads = [
        pltpu.make_async_copy(x, raw.at[j, start : start + rows], x_sems.at[number])
        for number, (x, (j, start, rows)) in enumerate(zip(xs, pieces_of(len(xs))))
    ]
    copies = fetch(moves, ws, weights, index_ref, w_sems)
    for copy in loads + copies:
        copy.start()
    norm_pieces(loads, [place_ref[j] for j in range(len(xs))], raw, gain_ref, normed, squares)
    for copy in copies:
        copy.wait()

    @pl.loop(0, 6)
    def _(step):
        lanes = pl.ds(pl.multiple_of(step * 256, 256), 256)
        product = jnp.dot(normed[...], weights[:, lanes], preferred_element_type=jnp.float32)
        product = (product * squares[:, :1]).astype(jnp.bfloat16)
        for part, out_ref in enumerate(out_refs):
            out_ref[:, lanes] = product[part * HALF : (part + 1) * HALF]

    last = out_refs[-1]
    tail_ref[:halo, :] = last[HALF - halo :, 512:]
    tail_ref[halo:, :512] = last[HALF - 16 :, :512]
    tail_ref[halo:, 512:] = jnp.zeros((16, 512), jnp.bfloat16)


def project_in(index, places, gain, pieces, weights, moves, halo):
    any_space = pl.BlockSpec(memory_space=pl.ANY)
    vmem = pl.BlockSpec(memory_space=pltpu.VMEM)
    smem = pl.BlockSpec(memory_space=pltpu.SMEM)
    return pl.pallas_call(
        functools.partial(in_kernel, moves, len(pieces), halo),
        out_shape=[jax.ShapeDtypeStruct((HALF, 1536), jnp.bfloat16)] * 2
        + [jax.ShapeDtypeStruct((halo + 16, 1024), jnp.bfloat16)],
        in_specs=[smem, smem, vmem] + [any_space] * (len(pieces) + len(weights)),
        out_specs=[vmem] * 3,
        scratch_shapes=[
            pltpu.VMEM((8, 2 * HALF, 512), jnp.bfloat16),
            pltpu.VMEM((2 * HALF, 4096), jnp.bfloat16),
            pltpu.VMEM((4096, 1536), jnp.bfloat16),
            pltpu.VMEM((2 * HALF, LANES), jnp.float32),
            pltpu.SemaphoreType.DMA((16,)),
            pltpu.SemaphoreType.DMA((len(moves),)),
        ],
        compiler_params=pltpu.CompilerParams(vmem_limit_bytes=(44 if halo == 16 else 50) * 1024 * 1024),
        cost_estimate=pl.CostEstimate(flops=4 * HALF * 4096 * 1536, bytes_accessed=18 * 2**20, transcendentals=0),
    )(index, places, gain, *pieces, *weights)


def filter_rows(halo, taps, before_ref, main_ref, feat_ref, filter_ref, skip_ref, inner, shaped, gated, copies8):
    total = halo + HALF

    if before_ref.shape[1] == 1024:
        shaped[:16, :512] = before_ref[halo:, :512].astype(jnp.float32)
        shaped[:halo, 512:] = before_ref[:halo, :].astype(jnp.float32)
    else:
        shaped[:16, :512] = before_ref[HALF - 16 :, :512].astype(jnp.float32)
        shaped[:halo, 512:] = before_ref[HALF - halo :, 512:].astype(jnp.float32)
    shaped[16 : 16 + HALF, :512] = main_ref[:, :512].astype(jnp.float32)
    shaped[halo:total, 512:] = main_ref[:, 512:].astype(jnp.float32)

    def feature(start, size, s, lanes):
        value = None
        for j in range(3):
            tap = feat_ref[3 * j + s : 3 * j + s + 1, lanes]
            low = s * 512 + lanes.start
            term = tap * shaped[start - j : start - j + size, low : low + LANES]
            value = term if value is None else value + term
        return value

    for lane in range(0, 512, LANES):
        lanes = slice(lane, lane + LANES)
        for start in range(8, total, 64):
            size = min(64, total - start)
            gated[start : start + size, lanes] = feature(start, size, 1, lanes) * feature(start, size, 2, lanes)
        gated[:8, lanes] = jnp.zeros((8, LANES), jnp.float32)

    if taps == 7:
        for lane in range(0, 512, LANES):
            lanes = slice(lane, lane + LANES)
            for start in range(0, HALF, 64):
                own = gated[halo + start : halo + start + 64, lanes]
                value = (skip_ref[:1, lanes] + filter_ref[:1, lanes]) * own
                for j in range(1, taps):
                    value = value + filter_ref[j : j + 1, lanes] * gated[halo + start - j : halo + start - j + 64, lanes]
                inner[start : start + 64, lanes] = (feature(16 + start, 64, 0, lanes) * value).astype(jnp.bfloat16)
    else:
        for lane in range(0, 512, LANES):
            lanes = slice(lane, lane + LANES)
            for r in range(8):
                for start in range(0, HALF + 128, 128):
                    copies8[r, start : start + 128, :] = gated[16 + start - r : 16 + start - r + 128, lanes]

            @pl.loop(0, HALF // 128)
            def _(step):
                base = pl.multiple_of(step * 128, 128)
                value = jnp.zeros((128, LANES), jnp.float32)
                for r in range(8):
                    for a in range(0, 16, 4):
                        window = copies8[r, pl.ds(pl.multiple_of(base + 128 - 8 * (a + 3), 8), 128 + 24), :]
                        for b in range(4):
                            tap = filter_ref[8 * (a + b) + r : 8 * (a + b) + r + 1, lanes]
                            low = 8 * (3 - b)
                            value = value + tap * window[low : low + 128]
                copies8[8, pl.ds(base, 128), :] = value

            for start in range(0, HALF, 64):
                own = gated[halo + start : halo + start + 64, lanes]
                value = copies8[8, start : start + 64, :] + skip_ref[:1, lanes] * own
                inner[start : start + 64, lanes] = (feature(16 + start, 64, 0, lanes) * value).astype(jnp.bfloat16)


def product_rows(outs, index_ref, inner, weights, out_refs):
    z = index_ref[0]
    core = index_ref[1]
    for by in range(4):
        block = lax.rem(z + by, 4)
        if outs == 4:
            columns = pl.ds(pl.multiple_of(block * 1024, 1024), 1024)
            out_refs[by][...] = jnp.dot(
                inner[...], weights[:, columns], preferred_element_type=jnp.float32
            ).astype(jnp.bfloat16)
        else:
            for side in range(2):
                place = block * 2 + (core if side == 0 else 1 - core)
                columns = pl.ds(pl.multiple_of(place * 512, 512), 512)
                out_refs[side][by] = jnp.dot(
                    inner[...], weights[:, columns], preferred_element_type=jnp.float32
                ).astype(jnp.bfloat16)


def filter_scratch(halo, taps):
    return [
        pltpu.VMEM((halo + HALF + 16, 1536), jnp.float32),
        pltpu.VMEM((halo + HALF, 512), jnp.float32),
        pltpu.VMEM((9, 8, LANES) if taps == 7 else (9, HALF + 128, LANES), jnp.float32),
    ]


def mix_kernel(moves, halo, taps, outs, index_ref, before_ref, main_ref, feat_ref, filter_ref, skip_ref, *refs):
    count = 1 + max(m[0] for m in moves)
    ws, refs = refs[:count], refs[count:]
    out_refs, refs = refs[:outs], refs[outs:]
    shaped, gated, copies8, inner, weights, w_sems = refs
    copies = fetch(moves, ws, weights, index_ref, w_sems)
    for copy in copies:
        copy.start()
    filter_rows(halo, taps, before_ref, main_ref, feat_ref, filter_ref, skip_ref, inner, shaped, gated, copies8)
    for copy in copies:
        copy.wait()
    product_rows(outs, index_ref, inner, weights, out_refs)


def mix_out(index, before, main, feat, taps, skip, weights, moves, halo, out_shapes):
    any_space = pl.BlockSpec(memory_space=pl.ANY)
    vmem = pl.BlockSpec(memory_space=pltpu.VMEM)
    length = taps.shape[0]
    return pl.pallas_call(
        functools.partial(mix_kernel, moves, halo, length, len(out_shapes)),
        out_shape=[jax.ShapeDtypeStruct(s, jnp.bfloat16) for s in out_shapes],
        in_specs=[pl.BlockSpec(memory_space=pltpu.SMEM)] + [vmem] * 5 + [any_space] * len(weights),
        out_specs=[vmem] * len(out_shapes),
        scratch_shapes=filter_scratch(halo, length)
        + [
            pltpu.VMEM((HALF, 512), jnp.bfloat16),
            pltpu.VMEM((512, 4096), jnp.bfloat16),
            pltpu.SemaphoreType.DMA((len(moves),)),
        ],
        compiler_params=pltpu.CompilerParams(vmem_limit_bytes=48 * 1024 * 1024),
        cost_estimate=pl.CostEstimate(flops=2 * HALF * 512 * 4096, bytes_accessed=6 * 2**20, transcendentals=0),
    )(index, before, main, feat, taps, skip, *weights)


def filter_kernel(halo, taps, before_ref, main_ref, feat_ref, filter_ref, skip_ref, inner, shaped, gated, copies8):
    filter_rows(halo, taps, before_ref, main_ref, feat_ref, filter_ref, skip_ref, inner, shaped, gated, copies8)


def filtered(before, main, feat, taps, skip, halo):
    vmem = pl.BlockSpec(memory_space=pltpu.VMEM)
    length = taps.shape[0]
    return pl.pallas_call(
        functools.partial(filter_kernel, halo, length),
        out_shape=jax.ShapeDtypeStruct((HALF, 512), jnp.bfloat16),
        in_specs=[vmem] * 5,
        out_specs=vmem,
        scratch_shapes=filter_scratch(halo, length),
        compiler_params=pltpu.CompilerParams(vmem_limit_bytes=24 * 1024 * 1024),
        cost_estimate=pl.CostEstimate(flops=2 * HALF * 512 * 4096 * 3, bytes_accessed=3 * 2**20, transcendentals=0),
    )(before, main, feat, taps, skip)


def product_kernel(moves, outs, index_ref, inner, weight_ref, *refs):
    out_refs, (weights, w_sems) = refs[:outs], refs[outs:]
    copies = fetch(moves, [weight_ref], weights, index_ref, w_sems)
    for copy in copies:
        copy.start()
    for copy in copies:
        copy.wait()
    product_rows(outs, index_ref, inner, weights, out_refs)


def project_out(index, inner, weight, moves, out_shapes):
    vmem = pl.BlockSpec(memory_space=pltpu.VMEM)
    return pl.pallas_call(
        functools.partial(product_kernel, moves, len(out_shapes)),
        out_shape=[jax.ShapeDtypeStruct(s, jnp.bfloat16) for s in out_shapes],
        in_specs=[pl.BlockSpec(memory_space=pltpu.SMEM), vmem, pl.BlockSpec(memory_space=pl.ANY)],
        out_specs=[vmem] * len(out_shapes),
        scratch_shapes=[pltpu.VMEM((512, 4096), jnp.bfloat16), pltpu.SemaphoreType.DMA((len(moves),))],
        compiler_params=pltpu.CompilerParams(vmem_limit_bytes=48 * 1024 * 1024),
        cost_estimate=pl.CostEstimate(flops=2 * HALF * 512 * 4096, bytes_accessed=6 * 2**20, transcendentals=0),
    )(index, inner, weight)


def per_device(hidden, norm_gain, in_weight, feat_filter, se_filter, mr_filter, skip_gain, out_weight):
    xl, y, core, z, xh = (lax.axis_index(a) for a in AXES)
    behind = lambda place, by: (place - by) % 4
    gains = norm_gain.reshape(2, 8, 512)
    ways = (1, -1, 2)
    other_core = lambda value: shift(value, "core", 1)
    gather = lambda value, axes: by_rows(lax.all_gather(by_rows(value), axes, axis=0, tiled=False))

    side_by_side = lambda w, o: jnp.concatenate([w.reshape(256, 1536), o[:256], o[256:]], axis=1)

    whole = lax.all_gather(hidden, ("z", "xh"), axis=0, tiled=False)

    m = side_by_side(in_weight[0], out_weight[0])
    m_xl = shift(m, "xl", 1)
    m_xl, w1, o1, *m_y = together(
        m_xl, swap(in_weight[1]), swap(after(out_weight[1], m_xl)), *[shift(m, "y", by) for by in ways]
    )
    rest = shift(jnp.stack([v[:, CUT:] for v in m_y]), "xl", 1)
    most = [shift(m_xl[:, :CUT], "y", by) for by in ways]
    rest, *more = together(rest, *most, *[other_core(after(v, most[0])) for v in (m, m_xl, *m_y)])
    most, far = more[:3], more[3:]
    w_list = [m, m_xl, *m_y, *far, rest, *most] + [other_core(v) for v in (rest, *most)]
    w_moves, q_moves, slots = [], [], [z, core]

    def take(number, lead, at_xl, at_y, at_core, low, high):
        w_moves.append((number, lead, 0, min(high, 1536) - low, len(slots), low, True))
        if high == 2048:
            for half in range(2):
                q_moves.append((number, lead, 1536 + 256 * half - low, 256, len(slots), 256 * half, False))
        slots.append(at_xl * 8 + at_y * 2 + at_core)

    for number, c in ((0, core), (5, 1 - core)):
        take(number, None, xl, y, c, 0, 2048)
        take(number + 1, None, 1 - xl, y, c, 0, 2048)
        for e, by in enumerate(ways):
            take(number + 2 + e, None, xl, behind(y, by), c, 0, 2048)
    for number, c in ((10, core), (14, 1 - core)):
        for e, by in enumerate(ways):
            take(number, e, 1 - xl, behind(y, by), c, CUT, 2048)
            take(number + 1 + e, None, 1 - xl, behind(y, by), c, 0, CUT)
    q_index = jnp.stack(slots).astype(jnp.int32)
    q_list = w_list[:15]

    w1 = gather(after(w1.reshape(256, 1536), rest, *most), ("xh", "xl", "y"))
    o1 = gather(o1, ("xh", "xl", "y"))
    small = jnp.concatenate([feat_filter[1].reshape(9, 512), skip_gain[1:2], mr_filter], axis=0)

    places = jnp.arange(8, dtype=jnp.int32)
    low, high, tail = project_in(q_index, places, gains[0], [whole], w_list, w_moves, 16)
    base = other_core(lax.dynamic_index_in_dim(whole, 2 * z + 1 - core, 0, keepdims=False))
    base = jnp.where(core == xh, hidden, base)
    small = swap(after(small, low))
    tail = from_behind(tail, ("xl", "y", "core"))

    def first_parts(before, main):
        parts = mix_out(
            q_index, before, main, feat_filter[0].reshape(9, 512), se_filter, skip_gain[0:1], q_list, q_moves, 16,
            [(HALF, 1024)] * 4,
        )
        return parts[0], [shift(part, "z", by) for by, part in ((1, parts[1]), (-1, parts[3]), (2, parts[2]))]

    def over_z(own, received):
        total = own.astype(jnp.float32)
        for value in received:
            total = total + value.astype(jnp.float32)
        total = total.astype(jnp.bfloat16)
        pick = lambda c: jnp.where(c == 0, total[:, :512], total[:, 512:])
        mine, others = pick(core), pick(1 - core)
        return mine, [
            lax.ppermute(mine, ("core", "xh"), [(1, 0), (2, 3)]),
            lax.ppermute(others, ("core", "xh"), [(1, 2), (2, 1)]),
            lax.ppermute(others, ("core", "xh"), [(0, 2), (3, 1)]),
        ]

    def over_x(mine, received, rows):
        kept = jnp.where(core == xh, mine, jnp.zeros_like(mine))
        current = base[rows : rows + HALF].astype(jnp.float32) + kept.astype(jnp.float32)
        for value in received:
            current = current + value.astype(jnp.float32)
        return current.astype(jnp.bfloat16)

    own_high, high_z = first_parts(low, high)
    own_low, low_z = first_parts(tail, low)
    mine_high, high_x = over_z(own_high, high_z)
    *low_z, one, two, three = together(*low_z, *high_x)
    high = over_x(mine_high, (one, two, three), HALF)
    mine_low, low_x = over_z(own_low, low_z)
    high = after(high, low_x[2])
    high_near = [shift(high, "z", by) for by in ways]
    one, two, three, *high_near = together(*low_x, *high_near)
    low = over_x(mine_low, (one, two, three), 0)

    places = [(p, (p // 4 % 2) * 8 + (p % 4) * 2 + p // 8) for p in range(16)]
    w_moves = [(0, p, 0, 1536, None, 0, True, block) for p, block in places]
    p_moves = [(0, p, 0, 256, None, 0, False, block) for p, block in places]
    x_index = jnp.stack([behind(z, by) * 2 + c for c in (core, 1 - core) for by in (0, *ways)] * 2).astype(jnp.int32)
    low_near = [low] + [shift(low, "z", by) for by in ways]
    high_near = [high] + high_near
    high_far = [other_core(v) for v in high_near]
    low_far = [other_core(v) for v in low_near]
    p_low, p_high, tail = project_in(
        q_index, x_index, gains[1], low_near + low_far + high_near + high_far, [w1], w_moves, 144
    )
    tail = from_behind(tail, ("xl", "y", "xh"))

    def second_filter(before, main):
        return filtered(before, main, small[:9], small[10:], small[9:10], 144)

    def second_parts(inner):
        return project_out(q_index, inner, o1, p_moves, [(4, HALF, 512)] * 2)

    def second_z(own, theirs):
        both = (own.astype(jnp.float32) + theirs.astype(jnp.float32)).astype(jnp.bfloat16)
        return [shift_swapped(both[at], by) for by, at in ((1, 1), (-1, 3), (2, 2))] + [swap(both[0])]

    def second_sum(received, rows):
        total = rows.astype(jnp.float32)
        for value in received:
            total = total + value.astype(jnp.float32)
        return total.astype(jnp.bfloat16)

    high, low = after((high, low), p_low)
    high, low = swap(high), swap(low)
    inner_high = second_filter(p_low, p_high)
    inner_low = second_filter(tail, p_low)
    inner_high, inner_low, high, low = together(inner_high, inner_low, high, low)
    own_high, theirs_high = second_parts(inner_high)
    theirs_high = other_core(theirs_high)
    high_z = second_z(own_high, theirs_high)
    own_low, theirs_low = second_parts(inner_low)
    low_z = second_z(own_low, other_core(theirs_low))
    high = second_sum(high_z, high)
    low = second_sum(low_z, low)
    return jnp.concatenate([low, high], axis=0)


def solution(mesh):
    fine = Mesh(np.asarray(mesh.devices).reshape(2, 4, 2, 4, 2), AXES)
    ctx, ch = ("xl", "y", "core"), ("z", "xh")
    return jax.shard_map(
        per_device,
        mesh=fine,
        in_specs=(
            P(ctx, ch),
            P(),
            P(None, ctx, None, ch),
            P(None, None, None, ch),
            P(None, ch),
            P(None, ch),
            P(None, ch),
            P(None, ch, ctx),
        ),
        out_specs=P(ctx, ch),
        check_vma=False,
    )
```

```python
import functools

import jax
import jax.numpy as jnp
import numpy as np
from jax import lax
from jax.experimental.layout import Layout, with_layout_constraint
from jax.experimental import pallas as pl
from jax.experimental.pallas import tpu as pltpu
from jax.sharding import Mesh, PartitionSpec as P

AXES = ("xl", "y", "core", "z", "xh")
HALF = 256
CUT = 1280
LANES = 128


def shift(value, axis, by):
    size = lax.axis_size(axis)
    return lax.ppermute(value, axis, [(i, (i + by) % size) for i in range(size)])


def swap(value):
    moved = lax.ppermute(value, ("core", "xh"), [(1, 2), (2, 1)])
    same = lax.axis_index("core") == lax.axis_index("xh")
    return jnp.where(same, value, moved)


def shift_swapped(value, by):
    pairs = [(a * 8 + z * 2 + b, b * 8 + (z + by) % 4 * 2 + a) for a in range(2) for z in range(4) for b in range(2)]
    return lax.ppermute(value, ("core", "z", "xh"), pairs)


def from_behind(value, axes):
    return lax.ppermute(value, axes, [(i, i + 1) for i in range(15)])


def by_rows(value):
    return with_layout_constraint(value, Layout(major_to_minor=tuple(range(value.ndim))))


def after(value, *others):
    return lax.optimization_barrier((value, *others))[0]


def together(*values):
    return lax.optimization_barrier(values)


def fetch(moves, sources, target, index_ref, semaphores):
    copies = []
    for number, (source, lead, lane, width, slot, other, by_rows, *fixed) in enumerate(moves):
        block = fixed[0] * 256 if slot is None else pl.multiple_of(index_ref[slot] * 256, 256)
        ref = sources[source]
        if lead is not None:
            ref = ref.at[lead]
        if by_rows:
            piece = target.at[pl.ds(block, 256), other : other + width]
        else:
            piece = target.at[other : other + ref.shape[0], pl.ds(block, 256)]
        copies.append(pltpu.make_async_copy(ref.at[:, lane : lane + width], piece, semaphores.at[number]))
    return copies


def norm_pieces(loads, places, raw, gain_ref, normed, squares):
    squares[...] = jnp.zeros_like(squares)
    for load, (j, start, count), place in zip(loads, pieces_of(len(loads)), places):
        load.wait()
        lanes = pl.ds(pl.multiple_of(place * 512, 512), 512)
        gain = gain_ref[pl.ds(place, 1), :]

        @pl.loop(0, count // 64)
        def _(step):
            rows = pl.ds(pl.multiple_of(start + step * 64, 64), 64)
            x = raw[j, rows, :].astype(jnp.float32)
            normed[rows, lanes] = (x * gain).astype(jnp.bfloat16)
            q = x * x
            squares[rows, :] += (q[:, :128] + q[:, 128:256]) + (q[:, 256:384] + q[:, 384:])

    squares[:, :1] = lax.rsqrt(jnp.sum(squares[...], axis=1, keepdims=True) * (1.0 / 4096) + 1e-06)


def pieces_of(count):
    rows = 8 * 2 * HALF // count
    return [(j % 8, j // 8 * rows, rows) for j in range(count)]


def in_kernel(moves, sources, halo, index_ref, place_ref, gain_ref, *refs):
    xs, refs = refs[:sources], refs[sources:]
    count = 1 + max(m[0] for m in moves)
    ws, refs = refs[:count], refs[count:]
    out_refs, (tail_ref, raw, normed, weights, squares, x_sems, w_sems) = refs[:2], refs[2:]
    xs = [xs[0].at[j] for j in range(8)] if sources == 1 else xs
    loads = [
        pltpu.make_async_copy(x, raw.at[j, start : start + rows], x_sems.at[number])
        for number, (x, (j, start, rows)) in enumerate(zip(xs, pieces_of(len(xs))))
    ]
    copies = fetch(moves, ws, weights, index_ref, w_sems)
    for copy in loads + copies:
        copy.start()
    norm_pieces(loads, [place_ref[j] for j in range(len(xs))], raw, gain_ref, normed, squares)
    for copy in copies:
        copy.wait()

    @pl.loop(0, 6)
    def _(step):
        lanes = pl.ds(pl.multiple_of(step * 256, 256), 256)
        product = jnp.dot(normed[...], weights[:, lanes], preferred_element_type=jnp.float32)
        product = (product * squares[:, :1]).astype(jnp.bfloat16)
        for part, out_ref in enumerate(out_refs):
            out_ref[:, lanes] = product[part * HALF : (part + 1) * HALF]

    last = out_refs[-1]
    tail_ref[:halo, :] = last[HALF - halo :, 512:]
    tail_ref[halo:, :512] = last[HALF - 16 :, :512]
    tail_ref[halo:, 512:] = jnp.zeros((16, 512), jnp.bfloat16)


def project_in(index, places, gain, pieces, weights, moves, halo):
    any_space = pl.BlockSpec(memory_space=pl.ANY)
    vmem = pl.BlockSpec(memory_space=pltpu.VMEM)
    smem = pl.BlockSpec(memory_space=pltpu.SMEM)
    return pl.pallas_call(
        functools.partial(in_kernel, moves, len(pieces), halo),
        out_shape=[jax.ShapeDtypeStruct((HALF, 1536), jnp.bfloat16)] * 2
        + [jax.ShapeDtypeStruct((halo + 16, 1024), jnp.bfloat16)],
        in_specs=[smem, smem, vmem] + [any_space] * (len(pieces) + len(weights)),
        out_specs=[vmem] * 3,
        scratch_shapes=[
            pltpu.VMEM((8, 2 * HALF, 512), jnp.bfloat16),
            pltpu.VMEM((2 * HALF, 4096), jnp.bfloat16),
            pltpu.VMEM((4096, 1536), jnp.bfloat16),
            pltpu.VMEM((2 * HALF, LANES), jnp.float32),
            pltpu.SemaphoreType.DMA((16,)),
            pltpu.SemaphoreType.DMA((len(moves),)),
        ],
        compiler_params=pltpu.CompilerParams(vmem_limit_bytes=(44 if halo == 16 else 50) * 1024 * 1024),
        cost_estimate=pl.CostEstimate(flops=4 * HALF * 4096 * 1536, bytes_accessed=18 * 2**20, transcendentals=0),
    )(index, places, gain, *pieces, *weights)


def filter_rows(halo, taps, before_ref, main_ref, feat_ref, filter_ref, skip_ref, inner, shaped, gated, copies8):
    total = halo + HALF

    if before_ref.shape[1] == 1024:
        shaped[:16, :512] = before_ref[halo:, :512].astype(jnp.float32)
        shaped[:halo, 512:] = before_ref[:halo, :].astype(jnp.float32)
    else:
        shaped[:16, :512] = before_ref[HALF - 16 :, :512].astype(jnp.float32)
        shaped[:halo, 512:] = before_ref[HALF - halo :, 512:].astype(jnp.float32)
    shaped[16 : 16 + HALF, :512] = main_ref[:, :512].astype(jnp.float32)
    shaped[halo:total, 512:] = main_ref[:, 512:].astype(jnp.float32)

    def feature(start, size, s, lanes):
        value = None
        for j in range(3):
            tap = feat_ref[3 * j + s : 3 * j + s + 1, lanes]
            low = s * 512 + lanes.start
            term = tap * shaped[start - j : start - j + size, low : low + LANES]
            value = term if value is None else value + term
        return value

    for lane in range(0, 512, LANES):
        lanes = slice(lane, lane + LANES)
        for start in range(8, total, 64):
            size = min(64, total - start)
            gated[start : start + size, lanes] = feature(start, size, 1, lanes) * feature(start, size, 2, lanes)
        gated[:8, lanes] = jnp.zeros((8, LANES), jnp.float32)

    if taps == 7:
        for lane in range(0, 512, LANES):
            lanes = slice(lane, lane + LANES)
            for start in range(0, HALF, 64):
                own = gated[halo + start : halo + start + 64, lanes]
                value = (skip_ref[:1, lanes] + filter_ref[:1, lanes]) * own
                for j in range(1, taps):
                    value = value + filter_ref[j : j + 1, lanes] * gated[halo + start - j : halo + start - j + 64, lanes]
                inner[start : start + 64, lanes] = (feature(16 + start, 64, 0, lanes) * value).astype(jnp.bfloat16)
    else:
        for lane in range(0, 512, LANES):
            lanes = slice(lane, lane + LANES)
            for r in range(8):
                for start in range(0, HALF + 128, 128):
                    copies8[r, start : start + 128, :] = gated[16 + start - r : 16 + start - r + 128, lanes]

            @pl.loop(0, HALF // 128)
            def _(step):
                base = pl.multiple_of(step * 128, 128)
                value = jnp.zeros((128, LANES), jnp.float32)
                for r in range(8):
                    for a in range(0, 16, 4):
                        window = copies8[r, pl.ds(pl.multiple_of(base + 128 - 8 * (a + 3), 8), 128 + 24), :]
                        for b in range(4):
                            tap = filter_ref[8 * (a + b) + r : 8 * (a + b) + r + 1, lanes]
                            low = 8 * (3 - b)
                            value = value + tap * window[low : low + 128]
                copies8[8, pl.ds(base, 128), :] = value

            for start in range(0, HALF, 64):
                own = gated[halo + start : halo + start + 64, lanes]
                value = copies8[8, start : start + 64, :] + skip_ref[:1, lanes] * own
                inner[start : start + 64, lanes] = (feature(16 + start, 64, 0, lanes) * value).astype(jnp.bfloat16)


def product_rows(outs, index_ref, inner, weights, out_refs):
    z = index_ref[0]
    core = index_ref[1]
    for by in range(4):
        block = lax.rem(z + by, 4)
        if outs == 4:
            columns = pl.ds(pl.multiple_of(block * 1024, 1024), 1024)
            out_refs[by][...] = jnp.dot(
                inner[...], weights[:, columns], preferred_element_type=jnp.float32
            ).astype(jnp.bfloat16)
        else:
            for side in range(2):
                place = block * 2 + (core if side == 0 else 1 - core)
                columns = pl.ds(pl.multiple_of(place * 512, 512), 512)
                out_refs[side][by] = jnp.dot(
                    inner[...], weights[:, columns], preferred_element_type=jnp.float32
                ).astype(jnp.bfloat16)


def filter_scratch(halo, taps):
    return [
        pltpu.VMEM((halo + HALF + 16, 1536), jnp.float32),
        pltpu.VMEM((halo + HALF, 512), jnp.float32),
        pltpu.VMEM((9, 8, LANES) if taps == 7 else (9, HALF + 128, LANES), jnp.float32),
    ]


def mix_kernel(moves, halo, taps, outs, index_ref, before_ref, main_ref, feat_ref, filter_ref, skip_ref, *refs):
    count = 1 + max(m[0] for m in moves)
    ws, refs = refs[:count], refs[count:]
    out_refs, refs = refs[:outs], refs[outs:]
    shaped, gated, copies8, inner, weights, w_sems = refs
    copies = fetch(moves, ws, weights, index_ref, w_sems)
    for copy in copies:
        copy.start()
    filter_rows(halo, taps, before_ref, main_ref, feat_ref, filter_ref, skip_ref, inner, shaped, gated, copies8)
    for copy in copies:
        copy.wait()
    product_rows(outs, index_ref, inner, weights, out_refs)


def mix_out(index, before, main, feat, taps, skip, weights, moves, halo, out_shapes):
    any_space = pl.BlockSpec(memory_space=pl.ANY)
    vmem = pl.BlockSpec(memory_space=pltpu.VMEM)
    length = taps.shape[0]
    return pl.pallas_call(
        functools.partial(mix_kernel, moves, halo, length, len(out_shapes)),
        out_shape=[jax.ShapeDtypeStruct(s, jnp.bfloat16) for s in out_shapes],
        in_specs=[pl.BlockSpec(memory_space=pltpu.SMEM)] + [vmem] * 5 + [any_space] * len(weights),
        out_specs=[vmem] * len(out_shapes),
        scratch_shapes=filter_scratch(halo, length)
        + [
            pltpu.VMEM((HALF, 512), jnp.bfloat16),
            pltpu.VMEM((512, 4096), jnp.bfloat16),
            pltpu.SemaphoreType.DMA((len(moves),)),
        ],
        compiler_params=pltpu.CompilerParams(vmem_limit_bytes=48 * 1024 * 1024),
        cost_estimate=pl.CostEstimate(flops=2 * HALF * 512 * 4096, bytes_accessed=6 * 2**20, transcendentals=0),
    )(index, before, main, feat, taps, skip, *weights)


def filter_kernel(halo, taps, before_ref, main_ref, feat_ref, filter_ref, skip_ref, inner, shaped, gated, copies8):
    filter_rows(halo, taps, before_ref, main_ref, feat_ref, filter_ref, skip_ref, inner, shaped, gated, copies8)


def filtered(before, main, feat, taps, skip, halo):
    vmem = pl.BlockSpec(memory_space=pltpu.VMEM)
    length = taps.shape[0]
    return pl.pallas_call(
        functools.partial(filter_kernel, halo, length),
        out_shape=jax.ShapeDtypeStruct((HALF, 512), jnp.bfloat16),
        in_specs=[vmem] * 5,
        out_specs=vmem,
        scratch_shapes=filter_scratch(halo, length),
        compiler_params=pltpu.CompilerParams(vmem_limit_bytes=24 * 1024 * 1024),
        cost_estimate=pl.CostEstimate(flops=2 * HALF * 512 * 4096 * 3, bytes_accessed=3 * 2**20, transcendentals=0),
    )(before, main, feat, taps, skip)


def product_kernel(moves, outs, index_ref, inner, weight_ref, *refs):
    out_refs, (weights, w_sems) = refs[:outs], refs[outs:]
    copies = fetch(moves, [weight_ref], weights, index_ref, w_sems)
    for copy in copies:
        copy.start()
    for copy in copies:
        copy.wait()
    product_rows(outs, index_ref, inner, weights, out_refs)


def project_out(index, inner, weight, moves, out_shapes):
    vmem = pl.BlockSpec(memory_space=pltpu.VMEM)
    return pl.pallas_call(
        functools.partial(product_kernel, moves, len(out_shapes)),
        out_shape=[jax.ShapeDtypeStruct(s, jnp.bfloat16) for s in out_shapes],
        in_specs=[pl.BlockSpec(memory_space=pltpu.SMEM), vmem, pl.BlockSpec(memory_space=pl.ANY)],
        out_specs=[vmem] * len(out_shapes),
        scratch_shapes=[pltpu.VMEM((512, 4096), jnp.bfloat16), pltpu.SemaphoreType.DMA((len(moves),))],
        compiler_params=pltpu.CompilerParams(vmem_limit_bytes=48 * 1024 * 1024),
        cost_estimate=pl.CostEstimate(flops=2 * HALF * 512 * 4096, bytes_accessed=6 * 2**20, transcendentals=0),
    )(index, inner, weight)


def per_device(hidden, norm_gain, in_weight, feat_filter, se_filter, mr_filter, skip_gain, out_weight):
    xl, y, core, z, xh = (lax.axis_index(a) for a in AXES)
    behind = lambda place, by: (place - by) % 4
    gains = norm_gain.reshape(2, 8, 512)
    ways = (1, -1, 2)
    other_core = lambda value: shift(value, "core", 1)
    gather = lambda value, axes: by_rows(lax.all_gather(by_rows(value), axes, axis=0, tiled=False))

    side_by_side = lambda w, o: jnp.concatenate([w.reshape(256, 1536), o[:256], o[256:]], axis=1)

    whole = lax.all_gather(hidden, ("z", "xh"), axis=0, tiled=False)

    m = side_by_side(in_weight[0], out_weight[0])
    m_xl = shift(m, "xl", 1)
    m_xl, w1, o1, *m_y = together(
        m_xl, swap(in_weight[1]), swap(after(out_weight[1], m_xl)), *[shift(m, "y", by) for by in ways]
    )
    rest = shift(jnp.stack([v[:, CUT:] for v in m_y]), "xl", 1)
    most = [shift(m_xl[:, :CUT], "y", by) for by in ways]
    rest, *more = together(rest, *most, *[other_core(after(v, most[0])) for v in (m, m_xl, *m_y)])
    most, far = more[:3], more[3:]
    w_list = [m, m_xl, *m_y, *far, rest, *most] + [other_core(v) for v in (rest, *most)]
    w_moves, q_moves, slots = [], [], [z, core]

    def take(number, lead, at_xl, at_y, at_core, low, high):
        w_moves.append((number, lead, 0, min(high, 1536) - low, len(slots), low, True))
        if high == 2048:
            for half in range(2):
                q_moves.append((number, lead, 1536 + 256 * half - low, 256, len(slots), 256 * half, False))
        slots.append(at_xl * 8 + at_y * 2 + at_core)

    for number, c in ((0, core), (5, 1 - core)):
        take(number, None, xl, y, c, 0, 2048)
        take(number + 1, None, 1 - xl, y, c, 0, 2048)
        for e, by in enumerate(ways):
            take(number + 2 + e, None, xl, behind(y, by), c, 0, 2048)
    for number, c in ((10, core), (14, 1 - core)):
        for e, by in enumerate(ways):
            take(number, e, 1 - xl, behind(y, by), c, CUT, 2048)
            take(number + 1 + e, None, 1 - xl, behind(y, by), c, 0, CUT)
    q_index = jnp.stack(slots).astype(jnp.int32)
    q_list = w_list[:15]

    w1 = gather(after(w1.reshape(256, 1536), rest, *most), ("xh", "xl", "y"))
    o1 = gather(o1, ("xh", "xl", "y"))
    small = jnp.concatenate([feat_filter[1].reshape(9, 512), skip_gain[1:2], mr_filter], axis=0)

    places = jnp.arange(8, dtype=jnp.int32)
    low, high, tail = project_in(q_index, places, gains[0], [whole], w_list, w_moves, 16)
    base = other_core(lax.dynamic_index_in_dim(whole, 2 * z + 1 - core, 0, keepdims=False))
    base = jnp.where(core == xh, hidden, base)
    small = swap(after(small, low))
    tail = from_behind(tail, ("xl", "y", "core"))

    def first_parts(before, main):
        parts = mix_out(
            q_index, before, main, feat_filter[0].reshape(9, 512), se_filter, skip_gain[0:1], q_list, q_moves, 16,
            [(HALF, 1024)] * 4,
        )
        return parts[0], [shift(part, "z", by) for by, part in ((1, parts[1]), (-1, parts[3]), (2, parts[2]))]

    def over_z(own, received):
        total = own.astype(jnp.float32)
        for value in received:
            total = total + value.astype(jnp.float32)
        total = total.astype(jnp.bfloat16)
        pick = lambda c: jnp.where(c == 0, total[:, :512], total[:, 512:])
        mine, others = pick(core), pick(1 - core)
        return mine, [
            lax.ppermute(mine, ("core", "xh"), [(1, 0), (2, 3)]),
            lax.ppermute(others, ("core", "xh"), [(1, 2), (2, 1)]),
            lax.ppermute(others, ("core", "xh"), [(0, 2), (3, 1)]),
        ]

    def over_x(mine, received, rows):
        kept = jnp.where(core == xh, mine, jnp.zeros_like(mine))
        current = base[rows : rows + HALF].astype(jnp.float32) + kept.astype(jnp.float32)
        for value in received:
            current = current + value.astype(jnp.float32)
        return current.astype(jnp.bfloat16)

    own_high, high_z = first_parts(low, high)
    own_low, low_z = first_parts(tail, low)
    mine_high, high_x = over_z(own_high, high_z)
    *low_z, one, two, three = together(*low_z, *high_x)
    high = over_x(mine_high, (one, two, three), HALF)
    mine_low, low_x = over_z(own_low, low_z)
    high = after(high, low_x[2])
    high_near = [shift(high, "z", by) for by in ways]
    one, two, three, *high_near = together(*low_x, *high_near)
    low = over_x(mine_low, (one, two, three), 0)

    places = [(p, (p // 4 % 2) * 8 + (p % 4) * 2 + p // 8) for p in range(16)]
    w_moves = [(0, p, 0, 1536, None, 0, True, block) for p, block in places]
    p_moves = [(0, p, 0, 256, None, 0, False, block) for p, block in places]
    x_index = jnp.stack([behind(z, by) * 2 + c for c in (core, 1 - core) for by in (0, *ways)] * 2).astype(jnp.int32)
    low_near = [low] + [shift(low, "z", by) for by in ways]
    high_near = [high] + high_near
    high_far = [other_core(v) for v in high_near]
    low_far = [other_core(v) for v in low_near]
    p_low, p_high, tail = project_in(
        q_index, x_index, gains[1], low_near + low_far + high_near + high_far, [w1], w_moves, 144
    )
    tail = from_behind(tail, ("xl", "y", "xh"))

    def second_filter(before, main):
        return filtered(before, main, small[:9], small[10:], small[9:10], 144)

    def second_parts(inner):
        return project_out(q_index, inner, o1, p_moves, [(4, HALF, 512)] * 2)

    def second_z(own, theirs):
        both = (own.astype(jnp.float32) + theirs.astype(jnp.float32)).astype(jnp.bfloat16)
        return [shift_swapped(both[at], by) for by, at in ((1, 1), (-1, 3), (2, 2))] + [swap(both[0])]

    def second_sum(received, rows):
        total = rows.astype(jnp.float32)
        for value in received:
            total = total + value.astype(jnp.float32)
        return total.astype(jnp.bfloat16)

    high, low = after((high, low), *low_far)
    high, low = swap(high), swap(low)
    inner_high = second_filter(p_low, p_high)
    inner_low = second_filter(tail, p_low)
    inner_high, inner_low, high, low = together(inner_high, inner_low, high, low)
    own_high, theirs_high = second_parts(inner_high)
    theirs_high = other_core(theirs_high)
    high_z = second_z(own_high, theirs_high)
    own_low, theirs_low = second_parts(inner_low)
    low_z = second_z(own_low, other_core(theirs_low))
    high = second_sum(high_z, high)
    low = second_sum(low_z, low)
    return jnp.concatenate([low, high], axis=0)


def solution(mesh):
    fine = Mesh(np.asarray(mesh.devices).reshape(2, 4, 2, 4, 2), AXES)
    ctx, ch = ("xl", "y", "core"), ("z", "xh")
    return jax.shard_map(
        per_device,
        mesh=fine,
        in_specs=(
            P(ctx, ch),
            P(),
            P(None, ctx, None, ch),
            P(None, None, None, ch),
            P(None, ch),
            P(None, ch),
            P(None, ch),
            P(None, ch, ctx),
        ),
        out_specs=P(ctx, ch),
        check_vma=False,
    )
```
